256 devices in a mesh: dp: 4 (over z_hi), expert: 8 (over z_lo, y), tensor: 8 (over x, core).
Axes of the slice: x: 4, y: 4, z: 8 (z_hi: 4, z_lo: 2; z = z_hi * 2 + z_lo), core: 2. Of those that a mesh axis runs over, the one named last changes fastest.
Arguments:
- tokens: bfloat16 [2048, 6144], P(('dp', 'expert', 'tensor'))
- norm_gain: float32 [6144], replicated, may hold values from 0.1 to 1.9
- routes: int32 [2048, 2], P(('dp', 'expert', 'tensor')), may hold values from 0 to 7, all different within a row; in each aligned block of 8 rows (0 to 7, 8 to 15, ...) at most 4 rows name the same one
- route_weights: float32 [2048, 2], P(('dp', 'expert', 'tensor')), may hold values from 0.2 to 1
- w_gate: bfloat16 [8, 6144, 8192], P('expert', None, ('dp', 'tensor')), may hold values from -0.078125 to 0.078125
- w_up: bfloat16 [8, 6144, 8192], P('expert', None, ('dp', 'tensor')), may hold values from -0.078125 to 0.078125
- w_down: bfloat16 [8, 8192, 6144], P('expert', ('dp', 'tensor')), may hold values from -0.0625 to 0.0625
Outputs:
- mixed: bfloat16 [2048, 6144], P(('dp', 'expert', 'tensor'))
The draws below stay inside these ranges and needn't reach their ends.
Inputs may be any that keep to these rules, and one draw needn't show every extreme that they name: `routes`: A token's two experts differ. In each aligned block of 8 tokens (the tokens of one device) no expert is named more than 4 times, a bound that some block reaches.
All inputs are finite; a program needn't handle non-finite values.
Results may differ from the reference program's by a relative error of at most 0.013.
Values may be sent and summed in bfloat16 or wider, within the bound.
No kernel may reach another device: no remote copies, remote signals or barrier semaphores. Data moves between devices by JAX's collectives and lax.ppermute only.
A program may use at most 128 MiB of HBM per device.

```python
import math
import jax
import jax.numpy as jnp
import numpy as np
from jax import lax

D = 6144
FF = 8192
TOK_DEV = 8
EXPERTS = 8
CAP = 4
TOKENS = 2048
N_DP = 4
N_TENSOR = 8


def draw_tokens(key, part):
    key = jax.random.fold_in(key, 11)
    key_rows, key_cols, key_base = jax.random.split(key, 3)
    row_scale = jnp.exp(jax.random.uniform(key_rows, (TOKENS, 1), jnp.float32, math.log(0.3), math.log(2.5)))
    col_scale = jnp.exp(jax.random.uniform(key_cols, (1, D), jnp.float32, math.log(0.6), math.log(1.6)))
    base = jnp.clip(jax.random.normal(key_base, (TOKENS, D), jnp.float32), -4.0, 4.0)
    return (base * row_scale * col_scale).astype(jnp.bfloat16)


def shard_levels(own_key, dims, cuts, least, high):
    def one(position, shards_of):
        heights = jax.random.uniform(jax.random.fold_in(jax.random.fold_in(own_key, 6), position), (shards_of,), jnp.float32, least / len(cuts), high / len(cuts))
        return jnp.repeat(jnp.exp(heights), dims[position] // shards_of).reshape((-1,) + (1,) * (len(dims) - position - 1))

    gain = one(*cuts[0])
    for cut in cuts[1:]:
        gain = gain * one(*cut)
    return gain


def shared_out(stream_key, own, number, rows, amount, top, most, skew):
    sequence = jax.random.permutation(stream_key, amount)
    packed, common = load_shares(amount, rows * top, most, skew, True), load_shares(amount, rows * top, most, skew, False)
    places = jnp.arange(amount)

    def named(sizes, offset_by):
        used = int((sizes > 0).sum())
        fixed = max(1, used // 4)
        passed = fixed + (places - fixed + offset_by * (used - fixed)) % max(1, amount - fixed)
        return jnp.zeros((amount,), jnp.int32).at[sequence[jnp.where(places < fixed, places, passed)]].set(jnp.asarray(sizes, jnp.int32))

    sizes = jnp.where(number % 4 == 0, named(packed, number // 4), named(common, number - number // 4 - 1))
    mixed = jax.random.permutation(jax.random.fold_in(own, 3), amount)
    donor, sink = mixed[0:amount // 2 * 2:2], mixed[1:amount // 2 * 2:2]
    room = jnp.minimum(sizes[donor] - 1, most - sizes[sink]) // 2
    room = jnp.where((donor == sequence[0]) | (sink == sequence[0]) | (sizes[sink] == 0), 0, jnp.maximum(room, 0))
    passed = jax.random.randint(jax.random.fold_in(own, 4), (amount // 2,), 0, 1 << 20) % (room + 1)
    sizes = sizes.at[donor].add(-passed).at[sink].add(passed)
    members = jnp.searchsorted(jnp.cumsum(sizes), jnp.arange(rows * top), side="right").astype(jnp.int32)
    listing = members.reshape(top, rows).T
    listing = listing[jax.random.permutation(jax.random.fold_in(own, 1), rows)]
    offset_by = jax.random.randint(jax.random.fold_in(own, 2), (rows, 1), 0, top)
    return jnp.take_along_axis(listing, (jnp.arange(top)[None, :] + offset_by) % top, axis=1)


def load_shares(count, total, bound, slope, full):
    weights = [(1 << 20) // math.isqrt(grade ** slope) + 1 for grade in range(1, count + 1)]
    largest = bound if full else min(bound, max(-(-total // count), total * weights[0] // sum(weights)))
    least = 1 if total - largest >= count - 1 else 0
    holding, rest = [largest] + [least] * (count - 1), total - largest - least * (count - 1)
    while rest > 0:
        movable = [i for i in range(1, count) if holding[i] < largest] or [i for i in range(1, count) if holding[i] < bound]
        mass, left = sum([weights[i] for i in movable]), rest
        for i in movable:
            extra = min(bound - holding[i], max(1, left * weights[i] // mass), rest)
            holding[i] = holding[i] + extra
            rest = rest - extra
    return np.array(holding)


def noise(key, dims, scale, reach, cuts=(), kind=jnp.bfloat16):
    values = scale * jax.random.normal(key, dims, jnp.float32)
    if cuts:
        values = values * shard_levels(key, dims, cuts, -0.22, 0.18)
    return jnp.clip(values, -reach, reach).astype(kind)


def setup_inputs(seed: int = 0) -> dict:
    key_of = jax.random.split(jax.random.key(seed), 8)
    tokens = draw_tokens(jax.random.fold_in(key_of[7], 71), 0)
    norm_gain = jnp.clip(1.0 + 0.18 * jax.random.normal(key_of[1], (D,), jnp.float32), 0.1, 1.9)
    routes_keys = jax.random.split(jax.random.fold_in(key_of[2], 1), TOKENS // TOK_DEV)
    routes_turns = jax.random.permutation(jax.random.fold_in(key_of[2], 3), TOKENS // TOK_DEV)
    routes = jax.vmap(lambda own, number: shared_out(jax.random.fold_in(key_of[2], 2), own, number, TOK_DEV, EXPERTS, 2, CAP, 2))(routes_keys, routes_turns).reshape((TOKENS, 2))
    route_weights = jnp.clip(jnp.exp(math.log(1.0) - 1.609438 * jax.random.uniform(key_of[3], (TOKENS, 2), jnp.float32) ** shard_levels(key_of[3], (TOKENS, 2), ((0, 256),), -0.2, 0.2)), 0.2, 1.0)
    w_gate = noise(key_of[4], (EXPERTS, D, FF), D ** -0.5, 0.078125, ((0, 8), (2, 32)))
    w_up = noise(key_of[5], (EXPERTS, D, FF), D ** -0.5, 0.078125, ((0, 8), (2, 32)))
    w_down = noise(key_of[6], (EXPERTS, FF, D), FF ** -0.5, 0.0625, ((0, 8), (1, 32)))
    return dict(tokens=tokens, norm_gain=norm_gain, routes=routes, route_weights=route_weights, w_gate=w_gate, w_up=w_up, w_down=w_down)


def slot_index(block_routes, experts, cap):
    flat = block_routes.reshape(-1)
    onehot = (flat[:, None] == jnp.arange(experts, dtype=jnp.int32)[None, :]).astype(jnp.int32)
    before = jnp.cumsum(onehot, axis=0) - onehot
    rank = lax.optimization_barrier(jnp.sum(before * onehot, axis=1))
    return (flat * cap + rank).reshape(block_routes.shape).astype(jnp.int32)

def reference(tokens, norm_gain, routes, route_weights, w_gate, w_up, w_down):
    blocks = TOKENS // TOK_DEV
    slot_count = EXPERTS * CAP
    wide = tokens.astype(jnp.float32)
    scale = lax.rsqrt(lax.optimization_barrier(jnp.mean(wide * wide, axis=1, keepdims=True)) + 1e-05)
    normed = (wide * scale * norm_gain[None, :]).astype(jnp.bfloat16)
    slots = jax.vmap(lambda r: slot_index(r, EXPERTS, CAP))(routes.reshape(blocks, TOK_DEV, 2))
    hits = (slots[:, :, :, None] == jnp.arange(slot_count, dtype=jnp.int32)[None, None, None, :]).astype(jnp.float32)
    picked = lax.optimization_barrier(jnp.sum(hits, axis=2))
    buffers = jnp.einsum('bts,btd->bsd', picked, normed.reshape(blocks, TOK_DEV, D).astype(jnp.float32))
    buffers = buffers.astype(jnp.bfloat16)
    per_expert = buffers.reshape(blocks, EXPERTS, CAP, D).transpose(1, 0, 2, 3).reshape(EXPERTS, blocks * CAP, D)
    pieces = N_DP * N_TENSOR

    def expert_fn(operands):
        rows, wg, wu, wd = operands
        gate = jnp.dot(rows, wg, preferred_element_type=jnp.float32)
        upper = jnp.dot(rows, wu, preferred_element_type=jnp.float32)
        hidden = (jax.nn.silu(gate) * upper).astype(jnp.bfloat16)
        hidden_blocks = hidden.reshape(rows.shape[0], pieces, FF // pieces).transpose(1, 0, 2)
        down_blocks = wd.reshape(pieces, FF // pieces, D)

        def accumulate(total, item):
            part = jnp.dot(item[0], item[1], preferred_element_type=jnp.float32).astype(jnp.bfloat16)
            part = lax.optimization_barrier(part)
            return (total + part.astype(jnp.float32), None)
        total, _ = lax.scan(accumulate, jnp.zeros((rows.shape[0], D), jnp.float32), (hidden_blocks, down_blocks))
        return total.astype(jnp.bfloat16)
    results = lax.map(expert_fn, (per_expert, w_gate, w_up, w_down))
    results = results.reshape(EXPERTS, blocks, CAP, D).transpose(1, 0, 2, 3).reshape(blocks, slot_count, D)
    weights = route_weights.reshape(blocks, TOK_DEV, 2)
    combine = lax.optimization_barrier(jnp.sum(weights[:, :, :, None] * hits, axis=2))
    moe = jnp.einsum('bts,bsd->btd', combine, results.astype(jnp.float32), precision=lax.Precision.HIGHEST)
    return (wide + moe.reshape(TOKENS, D)).astype(jnp.bfloat16)
```

```python
import functools

import jax
import jax.numpy as jnp
from jax import lax
from jax.experimental import pallas as pl
from jax.experimental.pallas import tpu as pltpu
from jax.sharding import Mesh
from jax.sharding import PartitionSpec as P

AXES = ("dp", "zl", "y", "x", "c")
STEPS = 6


def shift(value, axis, by):
    n = lax.axis_size(axis)
    return lax.ppermute(value, axis, [(i, (i + by) % n) for i in range(n)])


def gather_small(block, axis):
    half = block.shape[1] // 2
    low = shift(block, axis, 1)
    high = shift(block, axis, -1)
    far_a = shift(low[:, :half], axis, 1)
    far_b = shift(high[:, half:], axis, -1)
    return jnp.concatenate([block, low, high, jnp.concatenate([far_a, far_b], axis=1)], axis=0)


def gather_large(block, axis):
    half = block.shape[0] // 2
    low = shift(block, axis, 1)
    high = shift(block, axis, -1)
    far_a = shift(low[:half], axis, 1)
    far_b = shift(high[half:], axis, -1)
    return block, low, high, far_a, far_b


def scatter_large(pieces, axis):
    own, low, high, far_a, far_b = pieces
    half = far_a.shape[0]
    f32 = jnp.float32
    for_low = shift(far_a, axis, -1)
    for_high = shift(far_b, axis, 1)
    low = jnp.concatenate(
        [(low[:half].astype(f32) + for_low.astype(f32)).astype(low.dtype), low[half:]], axis=0
    )
    high = jnp.concatenate(
        [high[:half], (high[half:].astype(f32) + for_high.astype(f32)).astype(low.dtype)], axis=0
    )
    from_high = shift(low, axis, -1)
    from_low = shift(high, axis, 1)
    return (own.astype(f32) + from_high.astype(f32) + from_low.astype(f32)).astype(own.dtype)


def scatter_small(block, axis):
    f32 = jnp.float32
    rows, half = block.shape[0] // 4, block.shape[1] // 2
    own, low, high, far = (block[i * rows : (i + 1) * rows] for i in range(4))
    for_low = shift(far[:, :half], axis, -1)
    for_high = shift(far[:, half:], axis, 1)
    low = jnp.concatenate(
        [(low[:, :half].astype(f32) + for_low.astype(f32)).astype(low.dtype), low[:, half:]], axis=1
    )
    high = jnp.concatenate(
        [high[:, :half], (high[:, half:].astype(f32) + for_high.astype(f32)).astype(low.dtype)],
        axis=1,
    )
    from_high = shift(low, axis, -1)
    from_low = shift(high, axis, 1)
    return (own.astype(f32) + from_high.astype(f32) + from_low.astype(f32)).astype(own.dtype)


def expert_kernel(sizes, *refs):
    n = len(sizes)
    pieces = refs[:n]
    wg0, wu0, wg1, wu1, wd0, wd1 = refs[n : n + 6]
    outs = refs[n + 6 : n + 6 + n]
    rows, acc, hidden = refs[n + 6 + n :]
    step = pl.program_id(0)
    depth = wg0.shape[0]
    f32 = jnp.float32

    @pl.when(step == 0)
    def _():
        at = 0
        for piece, size in zip(pieces, sizes):
            rows[pl.ds(at, size), :] = piece[...]
            at += size

    @pl.when(step < STEPS)
    def _():
        part = rows[:, pl.ds(pl.multiple_of(step * depth, 128), depth)]
        for i, w in enumerate((wg0, wu0, wg1, wu1)):
            product = jnp.dot(part, w[...], preferred_element_type=f32)

            @pl.when(step == 0)
            def _(i=i, product=product):
                acc[i] = product

            @pl.when(step > 0)
            def _(i=i, product=product):
                acc[i] = acc[i] + product

    @pl.when(step == STEPS - 1)
    def _():
        for i in range(2):
            gate = acc[2 * i]
            hidden[i] = (gate / (1.0 + jnp.exp(-gate)) * acc[2 * i + 1]).astype(hidden.dtype)

    @pl.when(step >= STEPS)
    def _():
        total = jnp.dot(hidden[0], wd0[...], preferred_element_type=f32) + jnp.dot(
            hidden[1], wd1[...], preferred_element_type=f32
        )
        total = total.astype(outs[0].dtype)
        at = 0
        for out, size in zip(outs, sizes):
            out[...] = total[at : at + size]
            at += size


def expert(pieces, weights):
    sizes = tuple(p.shape[0] for p in pieces)
    width = pieces[0].shape[1]
    count = sum(sizes)
    units = weights[0].shape[1]
    part = width // STEPS
    first = lambda i: (jnp.minimum(i, STEPS - 1), 0)
    second = lambda i: (0, jnp.maximum(i - STEPS, 0))
    return pl.pallas_call(
        functools.partial(expert_kernel, sizes),
        grid=(2 * STEPS,),
        out_shape=[jax.ShapeDtypeStruct((s, width), jnp.bfloat16) for s in sizes],
        in_specs=[pl.BlockSpec((s, width), lambda i: (0, 0)) for s in sizes]
        + [pl.BlockSpec((part, units), first)] * 4
        + [pl.BlockSpec((units, part), second)] * 2,
        out_specs=[pl.BlockSpec((s, part), second) for s in sizes],
        scratch_shapes=[
            pltpu.VMEM((count, width), jnp.bfloat16),
            pltpu.VMEM((4, count, units), jnp.float32),
            pltpu.VMEM((2, count, units), jnp.bfloat16),
        ],
        compiler_params=pltpu.CompilerParams(vmem_limit_bytes=32 << 20),
        cost_estimate=pl.CostEstimate(
            flops=12 * count * width * units,
            bytes_accessed=12 * width * units + 4 * count * width,
            transcendentals=2 * count * units,
        ),
        name="expert",
    )(*pieces, *weights)


def relative_slots(routes, cap):
    flat = routes.reshape(-1)
    y_count = lax.axis_size("y")
    z = flat // y_count
    y = flat % y_count
    z = (z + lax.axis_index("zl")) % 2
    y = (y - lax.axis_index("y") + y_count) % y_count
    experts = 2 * y_count
    rel = z * y_count + y
    onehot = (rel[:, None] == jnp.arange(experts, dtype=jnp.int32)[None, :]).astype(jnp.int32)
    before = jnp.cumsum(onehot, axis=0) - onehot
    rank = jnp.sum(before * onehot, axis=1)
    return (rel * cap + rank).reshape(routes.shape)


def per_device(tokens, norm_gain, routes, route_weights, w_gate, w_up, w_down):
    f32 = jnp.float32
    wg0, wu0, wd0 = w_gate[0], w_up[0], w_down[0]
    wg1, wu1, wd1 = (shift(w, "c", 1) for w in (wg0, wu0, wd0))
    weights = (wg0, wu0, wg1, wu1, wd0, wd1)

    cap = 4
    slot_count = 32
    wide = tokens.astype(f32)
    scale = lax.rsqrt(jnp.mean(wide * wide, axis=1, keepdims=True) + 1e-05)
    normed = (wide * scale * norm_gain[None, :]).astype(jnp.bfloat16)
    slots = relative_slots(routes, cap)
    hits = (slots[:, :, None] == jnp.arange(slot_count, dtype=jnp.int32)[None, None, :]).astype(f32)
    picked = jnp.transpose(jnp.sum(hits, axis=1)).astype(jnp.bfloat16)
    buffer = jnp.dot(picked, normed, preferred_element_type=f32).astype(jnp.bfloat16)
    combine = jnp.sum(route_weights[:, :, None] * hits, axis=1)

    keep = buffer[:16]
    got = shift(buffer[16:], "zl", 1)
    results = {}
    for by in (0, 1, 3, 2):
        at = slice(by * cap, (by + 1) * cap)
        block = jnp.concatenate([keep[at], got[at]], axis=0)
        if by:
            block = shift(block, "y", by)
        small, large = ("dp", "x") if by != 2 else ORDER
        gathered = gather_small(block, small)
        pieces = gather_large(gathered, large)
        pieces = expert(pieces, weights)
        summed = scatter_large(pieces, large)
        mine = scatter_small(summed, small)
        if by:
            mine = shift(mine, "y", -by)
        results[by] = mine
    kept = jnp.concatenate([results[by][:cap] for by in range(4)], axis=0)
    away = jnp.concatenate([results[by][cap:] for by in range(4)], axis=0)
    back = jnp.concatenate([kept, shift(away, "zl", 1)], axis=0)
    moe = jnp.dot(combine, back.astype(f32), precision=lax.Precision.HIGHEST)
    return (wide + moe).astype(jnp.bfloat16)


ORDER = ("dp", "x")


def solution(mesh):
    fine = Mesh(mesh.devices.reshape(4, 2, 4, 4, 2), AXES)
    rows = P(AXES, None)
    return jax.shard_map(
        per_device,
        mesh=fine,
        in_specs=(
            rows,
            P(),
            rows,
            rows,
            P(("zl", "y"), None, ("dp", "x", "c")),
            P(("zl", "y"), None, ("dp", "x", "c")),
            P(("zl", "y"), ("dp", "x", "c"), None),
        ),
        out_specs=rows,
        check_vma=False,
    )
```

```python
import functools

import jax
import jax.numpy as jnp
from jax import lax
from jax.experimental import pallas as pl
from jax.experimental.pallas import tpu as pltpu
from jax.sharding import Mesh
from jax.sharding import PartitionSpec as P

AXES = ("dp", "zl", "y", "x", "c")
STEPS = 6


def shift(value, axis, by):
    n = lax.axis_size(axis)
    return lax.ppermute(value, axis, [(i, (i + by) % n) for i in range(n)])


DIMS = {"xa": ("x", 1), "xb": ("x", 3), "za": ("dp", 1), "zb": ("dp", 3)}
CHAINS = (
    (0, 2048, ("za", "zb", "xb", "xa")),
    (2048, 2048, ("zb", "za", "xa", "xb")),
    (4096, 1024, ("xa", "xb", "zb", "za")),
    (5120, 1024, ("xb", "xa", "za", "zb")),
)
CANON = ("xa", "xb", "za", "zb")
UNIT = 32
HALF = 8 * UNIT


def canon_block(order, index):
    return sum(((index >> k) & 1) << CANON.index(d) for k, d in enumerate(order))


def trade(value, dim):
    axis, mask = DIMS[dim]
    return lax.ppermute(value, axis, [(i, i ^ mask) for i in range(4)])


def add(a, b):
    return (a.astype(jnp.float32) + b.astype(jnp.float32)).astype(a.dtype)


def expert_kernel(*refs):
    n = len(CHAINS)
    ins = refs[: 2 * n]
    wg0, wu0, wg1, wu1, wd0, wd1 = refs[2 * n : 2 * n + 6]
    outs = refs[2 * n + 6 : 4 * n + 6]
    part, acc, hidden = refs[4 * n + 6 :]
    step = pl.program_id(0)
    f32 = jnp.float32
    at = 0
    for c, (_, width, order) in enumerate(CHAINS):
        steps = width // PART

        @pl.when((step >= at) & (step < at + steps))
        def _(c=c, order=order):
            for index in range(16):
                to = canon_block(order, index) * UNIT
                row = (index % 8) * UNIT
                part[to : to + UNIT, :] = ins[2 * c + index // 8][row : row + UNIT, :]

        at += steps

    @pl.when(step == 0)
    def _():
        acc[...] = jnp.zeros_like(acc)

    @pl.when(step < STEPS)
    def _():
        for i, w in enumerate((wg0, wu0, wg1, wu1)):
            acc[i] += jnp.dot(part[...], w[...], preferred_element_type=f32)

    @pl.when(step == STEPS - 1)
    def _():
        for i in range(2):
            gate = acc[2 * i]
            hidden[i] = (gate / (1.0 + jnp.exp(-gate)) * acc[2 * i + 1]).astype(hidden.dtype)

    at = STEPS
    for c, (_, width, order) in enumerate(CHAINS):
        steps = width // PART

        @pl.when((step >= at) & (step < at + steps))
        def _(c=c, order=order):
            total = jnp.dot(hidden[0], wd0[...], preferred_element_type=f32) + jnp.dot(
                hidden[1], wd1[...], preferred_element_type=f32
            )
            total = total.astype(jnp.bfloat16)
            for index in range(16):
                row = canon_block(order, index) * UNIT
                to = (index % 8) * UNIT
                outs[2 * c + index // 8][to : to + UNIT, :] = total[row : row + UNIT]

        at += steps


PART = 1024


def expert(pieces, weights):
    width, units = weights[0].shape
    count = 2 * HALF
    first = lambda i: (jnp.minimum(i, STEPS - 1), 0)
    second = lambda i: (0, jnp.maximum(i - STEPS, 0))
    in_specs, out_specs, out_shape = [], [], []
    for start, size, _ in CHAINS:
        low, steps = start // PART, size // PART
        to = lambda i, low=low, steps=steps: (0, jnp.clip(i - low, 0, steps - 1))
        back = lambda i, low=low, steps=steps: (0, jnp.clip(i - STEPS - low, 0, steps - 1))
        in_specs += [pl.BlockSpec((HALF, PART), to)] * 2
        out_specs += [pl.BlockSpec((HALF, PART), back)] * 2
        out_shape += [jax.ShapeDtypeStruct((HALF, size), jnp.bfloat16)] * 2
    return pl.pallas_call(
        expert_kernel,
        grid=(2 * STEPS,),
        out_shape=out_shape,
        in_specs=in_specs
        + [pl.BlockSpec((PART, units), first)] * 4
        + [pl.BlockSpec((units, PART), second)] * 2,
        out_specs=out_specs,
        scratch_shapes=[
            pltpu.VMEM((count, PART), jnp.bfloat16),
            pltpu.VMEM((4, count, units), jnp.float32),
            pltpu.VMEM((2, count, units), jnp.bfloat16),
        ],
        compiler_params=pltpu.CompilerParams(vmem_limit_bytes=40 << 20),
        cost_estimate=pl.CostEstimate(
            flops=12 * count * width * units,
            bytes_accessed=12 * width * units + 4 * count * width,
            transcendentals=2 * count * units,
        ),
        name="expert",
    )(*pieces, *weights)


def relative_slots(routes, cap):
    flat = routes.reshape(-1)
    y_count = lax.axis_size("y")
    z = flat // y_count
    y = flat % y_count
    z = (z + lax.axis_index("zl")) % 2
    y = (y - lax.axis_index("y") + y_count) % y_count
    experts = 2 * y_count
    rel = z * y_count + y
    onehot = (rel[:, None] == jnp.arange(experts, dtype=jnp.int32)[None, :]).astype(jnp.int32)
    before = jnp.cumsum(onehot, axis=0) - onehot
    rank = jnp.sum(before * onehot, axis=1)
    return (rel * cap + rank).reshape(routes.shape)


def per_device(tokens, norm_gain, routes, route_weights, w_gate, w_up, w_down):
    f32 = jnp.float32
    wg0, wu0, wd0 = w_gate[0], w_up[0], w_down[0]
    wg1, wu1, wd1 = (shift(w, "c", 1) for w in (wg0, wu0, wd0))
    weights = (wg0, wu0, wg1, wu1, wd0, wd1)

    cap = 4
    slot_count = 32
    wide = tokens.astype(f32)
    scale = lax.rsqrt(jnp.mean(wide * wide, axis=1, keepdims=True) + 1e-05)
    normed = (wide * scale * norm_gain[None, :]).astype(jnp.bfloat16)
    slots = relative_slots(routes, cap)
    hits = (slots[:, :, None] == jnp.arange(slot_count, dtype=jnp.int32)[None, None, :]).astype(f32)
    picked = jnp.transpose(jnp.sum(hits, axis=1)).astype(jnp.bfloat16)
    buffer = jnp.dot(picked, normed, preferred_element_type=f32).astype(jnp.bfloat16)
    combine = jnp.sum(route_weights[:, :, None] * hits, axis=1)

    keep = buffer[:16]
    got = shift(buffer[16:], "zl", 1)
    blocks = []
    for by in range(4):
        at = slice(by * cap, (by + 1) * cap)
        block = jnp.concatenate([keep[at], got[at]], axis=0)
        blocks.append(shift(block, "y", by) if by else block)
    rows = jnp.concatenate(blocks, axis=0)

    pieces = []
    held = [rows[:, start : start + size] for start, size, _ in CHAINS]
    for step in range(4):
        came = [trade(h, order[step]) for h, (_, _, order) in zip(held, CHAINS)]
        if step < 3:
            held = [jnp.concatenate([h, r], axis=0) for h, r in zip(held, came)]
    for h, r in zip(held, came):
        pieces += [h, r]

    done = expert(pieces, weights)

    held, away = done[0::2], done[1::2]
    for step in (3, 2, 1, 0):
        came = [trade(a, order[step]) for a, (_, _, order) in zip(away, CHAINS)]
        held = [add(h, r) for h, r in zip(held, came)]
        half = held[0].shape[0] // 2
        if step:
            held, away = [h[:half] for h in held], [h[half:] for h in held]
    mine = jnp.concatenate(held, axis=1)

    results = []
    for by in range(4):
        block = mine[8 * by : 8 * by + 8]
        results.append(shift(block, "y", -by) if by else block)
    kept = jnp.concatenate([r[:cap] for r in results], axis=0)
    away = jnp.concatenate([r[cap:] for r in results], axis=0)
    back = jnp.concatenate([kept, shift(away, "zl", 1)], axis=0)
    moe = jnp.dot(combine, back.astype(f32), precision=lax.Precision.HIGHEST)
    return (wide + moe).astype(jnp.bfloat16)


def solution(mesh):
    fine = Mesh(mesh.devices.reshape(4, 2, 4, 4, 2), AXES)
    rows = P(AXES, None)
    return jax.shard_map(
        per_device,
        mesh=fine,
        in_specs=(
            rows,
            P(),
            rows,
            rows,
            P(("zl", "y"), None, ("dp", "x", "c")),
            P(("zl", "y"), None, ("dp", "x", "c")),
            P(("zl", "y"), ("dp", "x", "c"), None),
        ),
        out_specs=rows,
        check_vma=False,
    )
```

```python
import functools

import jax
import jax.numpy as jnp
from jax import lax
from jax.experimental import pallas as pl
from jax.experimental.pallas import tpu as pltpu
from jax.sharding import Mesh
from jax.sharding import PartitionSpec as P

AXES = ("dp", "zl", "y", "x", "c")
STEPS = 6


def shift(value, axis, by):
    n = lax.axis_size(axis)
    return lax.ppermute(value, axis, [(i, (i + by) % n) for i in range(n)])


DIMS = {"xa": ("x", 1), "xb": ("x", 3), "za": ("dp", 1), "zb": ("dp", 3)}
CHAINS = (
    (0, 2048, ("za", "zb", "xb", "xa")),
    (2048, 2048, ("zb", "za", "xa", "xb")),
    (4096, 1024, ("xa", "xb", "zb", "za")),
    (5120, 1024, ("xb", "xa", "za", "zb")),
)
CANON = ("xa", "xb", "za", "zb")
UNIT = 32
HALF = 8 * UNIT


def canon_block(order, index):
    return sum(((index >> k) & 1) << CANON.index(d) for k, d in enumerate(order))


def trade(value, dim):
    axis, mask = DIMS[dim]
    return lax.ppermute(value, axis, [(i, i ^ mask) for i in range(4)])


def add(a, b):
    return (a.astype(jnp.float32) + b.astype(jnp.float32)).astype(a.dtype)


def expert_kernel(*refs):
    n = len(CHAINS)
    ins = refs[: 2 * n]
    wg0, wu0, wg1, wu1, wd0, wd1 = refs[2 * n : 2 * n + 6]
    outs = refs[2 * n + 6 : 4 * n + 6]
    part, acc, hidden = refs[4 * n + 6 :]
    step = pl.program_id(0)
    f32 = jnp.float32
    at = 0
    for c, (_, width, order) in enumerate(CHAINS):
        steps = width // PART

        @pl.when((step >= at) & (step < at + steps))
        def _(c=c, order=order):
            for index in range(16):
                to = canon_block(order, index) * UNIT
                row = (index % 8) * UNIT
                part[to : to + UNIT, :] = ins[2 * c + index // 8][row : row + UNIT, :]

        at += steps

    @pl.when(step == 0)
    def _():
        acc[...] = jnp.zeros_like(acc)

    @pl.when(step < STEPS)
    def _():
        for i, w in enumerate((wg0, wu0, wg1, wu1)):
            acc[i] += jnp.dot(part[...], w[...], preferred_element_type=f32)

    @pl.when(step == STEPS - 1)
    def _():
        for i in range(2):
            gate = acc[2 * i]
            hidden[i] = (gate / (1.0 + jnp.exp(-gate)) * acc[2 * i + 1]).astype(hidden.dtype)

    at = STEPS
    for c, (_, width, order) in enumerate(CHAINS):
        steps = width // PART

        @pl.when((step >= at) & (step < at + steps))
        def _(c=c, order=order):
            total = jnp.dot(hidden[0], wd0[...], preferred_element_type=f32) + jnp.dot(
                hidden[1], wd1[...], preferred_element_type=f32
            )
            total = total.astype(jnp.bfloat16)
            for index in range(16):
                row = canon_block(order, index) * UNIT
                to = (index % 8) * UNIT
                outs[2 * c + index // 8][to : to + UNIT, :] = total[row : row + UNIT]

        at += steps


PART = 1024


def expert(pieces, weights):
    width, units = weights[0].shape
    count = 2 * HALF
    first = lambda i: (jnp.minimum(i, STEPS - 1), 0)
    second = lambda i: (0, jnp.maximum(i - STEPS, 0))
    in_specs, out_specs, out_shape = [], [], []
    for start, size, _ in CHAINS:
        low, steps = start // PART, size // PART
        to = lambda i, low=low, steps=steps: (0, jnp.clip(i - low, 0, steps - 1))
        back = lambda i, low=low, steps=steps: (0, jnp.clip(i - STEPS - low, 0, steps - 1))
        in_specs += [pl.BlockSpec((HALF, PART), to)] * 2
        out_specs += [pl.BlockSpec((HALF, PART), back)] * 2
        out_shape += [jax.ShapeDtypeStruct((HALF, size), jnp.bfloat16)] * 2
    return pl.pallas_call(
        expert_kernel,
        grid=(2 * STEPS,),
        out_shape=out_shape,
        in_specs=in_specs
        + [pl.BlockSpec((PART, units), first)] * 4
        + [pl.BlockSpec((units, PART), second)] * 2,
        out_specs=out_specs,
        scratch_shapes=[
            pltpu.VMEM((count, PART), jnp.bfloat16),
            pltpu.VMEM((4, count, units), jnp.float32),
            pltpu.VMEM((2, count, units), jnp.bfloat16),
        ],
        compiler_params=pltpu.CompilerParams(vmem_limit_bytes=40 << 20),
        cost_estimate=pl.CostEstimate(
            flops=12 * count * width * units,
            bytes_accessed=12 * width * units + 4 * count * width,
            transcendentals=2 * count * units,
        ),
        name="expert",
    )(*pieces, *weights)


def relative_slots(routes, cap):
    flat = routes.reshape(-1)
    y_count = lax.axis_size("y")
    z = flat // y_count
    y = flat % y_count
    z = (z + lax.axis_index("zl")) % 2
    y = (y - lax.axis_index("y") + y_count) % y_count
    experts = 2 * y_count
    rel = z * y_count + y
    onehot = (rel[:, None] == jnp.arange(experts, dtype=jnp.int32)[None, :]).astype(jnp.int32)
    before = jnp.cumsum(onehot, axis=0) - onehot
    rank = jnp.sum(before * onehot, axis=1)
    return (rel * cap + rank).reshape(routes.shape)


def per_device(tokens, norm_gain, routes, route_weights, w_gate, w_up, w_down):
    f32 = jnp.float32
    wg0, wu0, wd0 = w_gate[0], w_up[0], w_down[0]
    cap = 4
    slot_count = 32
    wide = tokens.astype(f32)
    scale = lax.rsqrt(jnp.mean(wide * wide, axis=1, keepdims=True) + 1e-05)
    normed = (wide * scale * norm_gain[None, :]).astype(jnp.bfloat16)
    slots = relative_slots(routes, cap)
    hits = (slots[:, :, None] == jnp.arange(slot_count, dtype=jnp.int32)[None, None, :]).astype(f32)
    picked = jnp.transpose(jnp.sum(hits, axis=1)).astype(jnp.bfloat16)
    buffer = jnp.dot(picked, normed, preferred_element_type=f32).astype(jnp.bfloat16)
    combine = jnp.sum(route_weights[:, :, None] * hits, axis=1)

    keep = buffer[:16]
    got, wg1 = lax.optimization_barrier((shift(buffer[16:], "zl", 1), shift(wg0, "c", 1)))
    blocks = []
    for by in range(4):
        at = slice(by * cap, (by + 1) * cap)
        block = jnp.concatenate([keep[at], got[at]], axis=0)
        blocks.append(shift(block, "y", by) if by else block)
    blocks, wu0, wg1 = lax.optimization_barrier((blocks, wu0, wg1))
    wu1 = shift(wu0, "c", 1)
    rows = jnp.concatenate(blocks, axis=0)

    pieces = []
    held = [rows[:, start : start + size] for start, size, _ in CHAINS]
    for step in range(4):
        came = [trade(h, order[step]) for h, (_, _, order) in zip(held, CHAINS)]
        if step == 0:
            came, wu1, wd0 = lax.optimization_barrier((came, wu1, wd0))
        elif step == 1:
            wd1 = shift(wd0, "c", 1)
            came, wd1 = lax.optimization_barrier((came, wd1))
        else:
            came = lax.optimization_barrier(came)
        if step < 3:
            held = [jnp.concatenate([h, r], axis=0) for h, r in zip(held, came)]
    for h, r in zip(held, came):
        pieces += [h, r]

    done = expert(pieces, (wg0, wu0, wg1, wu1, wd0, wd1))

    held, away = done[0::2], done[1::2]
    for step in (3, 2, 1, 0):
        came = [trade(a, order[step]) for a, (_, _, order) in zip(away, CHAINS)]
        came = lax.optimization_barrier(came)
        held = [add(h, r) for h, r in zip(held, came)]
        half = held[0].shape[0] // 2
        if step:
            held, away = [h[:half] for h in held], [h[half:] for h in held]
    mine = jnp.concatenate(held, axis=1)

    results = []
    for by in range(4):
        block = mine[8 * by : 8 * by + 8]
        results.append(shift(block, "y", -by) if by else block)
    kept = jnp.concatenate([r[:cap] for r in results], axis=0)
    away = jnp.concatenate([r[cap:] for r in results], axis=0)
    back = jnp.concatenate([kept, shift(away, "zl", 1)], axis=0)
    moe = jnp.dot(combine, back.astype(f32), precision=lax.Precision.HIGHEST)
    return (wide + moe).astype(jnp.bfloat16)


def solution(mesh):
    fine = Mesh(mesh.devices.reshape(4, 2, 4, 4, 2), AXES)
    rows = P(AXES, None)
    return jax.shard_map(
        per_device,
        mesh=fine,
        in_specs=(
            rows,
            P(),
            rows,
            rows,
            P(("zl", "y"), None, ("dp", "x", "c")),
            P(("zl", "y"), None, ("dp", "x", "c")),
            P(("zl", "y"), ("dp", "x", "c"), None),
        ),
        out_specs=rows,
        check_vma=False,
    )
```

```python
import functools

import jax
import jax.numpy as jnp
from jax import lax
from jax.experimental import pallas as pl
from jax.experimental.pallas import tpu as pltpu
from jax.sharding import Mesh
from jax.sharding import PartitionSpec as P

AXES = ("dp", "zl", "y", "x", "c")
STEPS = 6


def shift(value, axis, by):
    n = lax.axis_size(axis)
    return lax.ppermute(value, axis, [(i, (i + by) % n) for i in range(n)])


DIMS = {"xa": ("x", 1), "xb": ("x", 3), "za": ("dp", 1), "zb": ("dp", 3)}
CHAINS = (
    (0, 2048, ("za", "zb", "xb", "xa")),
    (2048, 2048, ("zb", "za", "xa", "xb")),
    (4096, 1024, ("xa", "xb", "zb", "za")),
    (5120, 1024, ("xb", "xa", "za", "zb")),
)
CANON = ("xa", "xb", "za", "zb")
UNIT = 32
HALF = 8 * UNIT


def canon_block(order, index):
    return sum(((index >> k) & 1) << CANON.index(d) for k, d in enumerate(order))


def trade(value, dim):
    axis, mask = DIMS[dim]
    return lax.ppermute(value, axis, [(i, i ^ mask) for i in range(4)])


def add(a, b):
    return (a.astype(jnp.float32) + b.astype(jnp.float32)).astype(a.dtype)


def after(value, *others):
    return lax.optimization_barrier((value, *others))[0]


def hidden_kernel(*refs):
    n = len(CHAINS)
    ins = refs[: 2 * n]
    wg0, wu0, wg1, wu1 = refs[2 * n : 2 * n + 4]
    hidden, part, acc = refs[2 * n + 4 :]
    step = pl.program_id(0)
    units = wg0.shape[1]
    f32 = jnp.float32
    at = 0
    for c, (_, width, order) in enumerate(CHAINS):
        steps = width // PART

        @pl.when((step >= at) & (step < at + steps))
        def _(c=c, order=order):
            for index in range(16):
                to = canon_block(order, index) * UNIT
                row = (index % 8) * UNIT
                part[to : to + UNIT, :] = ins[2 * c + index // 8][row : row + UNIT, :]

        at += steps

    @pl.when(step == 0)
    def _():
        acc[...] = jnp.zeros_like(acc)

    for i, w in enumerate((wg0, wu0, wg1, wu1)):
        acc[i] += jnp.dot(part[...], w[...], preferred_element_type=f32)

    @pl.when(step == STEPS - 1)
    def _():
        for i in range(2):
            gate = acc[2 * i]
            value = gate / (1.0 + jnp.exp(-gate)) * acc[2 * i + 1]
            hidden[:, i * units : (i + 1) * units] = value.astype(hidden.dtype)


def out_kernel(order, hidden, wd0, wd1, keep, away):
    units = wd0.shape[0]
    f32 = jnp.float32
    total = jnp.dot(hidden[:, :units], wd0[...], preferred_element_type=f32) + jnp.dot(
        hidden[:, units:], wd1[...], preferred_element_type=f32
    )
    total = total.astype(jnp.bfloat16)
    for index in range(16):
        row = canon_block(order, index) * UNIT
        to = (index % 8) * UNIT
        (keep, away)[index // 8][to : to + UNIT, :] = total[row : row + UNIT]


PART = 1024


def hidden_units(pieces, weights):
    width, units = weights[0].shape
    count = 2 * HALF
    in_specs = []
    for start, size, _ in CHAINS:
        low, steps = start // PART, size // PART
        to = lambda i, low=low, steps=steps: (0, jnp.clip(i - low, 0, steps - 1))
        in_specs += [pl.BlockSpec((HALF, PART), to)] * 2
    return pl.pallas_call(
        hidden_kernel,
        grid=(STEPS,),
        out_shape=jax.ShapeDtypeStruct((count, 2 * units), jnp.bfloat16),
        in_specs=in_specs + [pl.BlockSpec((PART, units), lambda i: (i, 0))] * 4,
        out_specs=pl.BlockSpec((count, 2 * units), lambda i: (0, 0)),
        scratch_shapes=[
            pltpu.VMEM((count, PART), jnp.bfloat16),
            pltpu.VMEM((4, count, units), jnp.float32),
        ],
        compiler_params=pltpu.CompilerParams(vmem_limit_bytes=32 << 20),
        cost_estimate=pl.CostEstimate(
            flops=8 * count * width * units,
            bytes_accessed=8 * width * units + 2 * count * width,
            transcendentals=2 * count * units,
        ),
        name="hidden",
    )(*pieces, *weights)


def expert_out(hidden, wd0, wd1, chain):
    start, size, order = CHAINS[chain]
    units = wd0.shape[0]
    low, count = start // PART, 2 * HALF
    shape = jax.ShapeDtypeStruct((HALF, size), jnp.bfloat16)
    return pl.pallas_call(
        functools.partial(out_kernel, order),
        grid=(size // PART,),
        out_shape=[shape] * 2,
        in_specs=[pl.BlockSpec((count, 2 * units), lambda i: (0, 0))]
        + [pl.BlockSpec((units, PART), lambda i: (0, low + i))] * 2,
        out_specs=[pl.BlockSpec((HALF, PART), lambda i: (0, i))] * 2,
        compiler_params=pltpu.CompilerParams(vmem_limit_bytes=24 << 20),
        cost_estimate=pl.CostEstimate(
            flops=4 * count * size * units,
            bytes_accessed=4 * size * units + 2 * count * size,
            transcendentals=0,
        ),
        name="out",
    )(hidden, wd0, wd1)


def relative_slots(routes, cap):
    flat = routes.reshape(-1)
    y_count = lax.axis_size("y")
    z = flat // y_count
    y = flat % y_count
    z = (z + lax.axis_index("zl")) % 2
    y = (y - lax.axis_index("y") + y_count) % y_count
    experts = 2 * y_count
    rel = z * y_count + y
    onehot = (rel[:, None] == jnp.arange(experts, dtype=jnp.int32)[None, :]).astype(jnp.int32)
    before = jnp.cumsum(onehot, axis=0) - onehot
    rank = jnp.sum(before * onehot, axis=1)
    return (rel * cap + rank).reshape(routes.shape)


def per_device(tokens, norm_gain, routes, route_weights, w_gate, w_up, w_down):
    f32 = jnp.float32
    wg0, wu0, wd0 = w_gate[0], w_up[0], w_down[0]
    cap = 4
    slot_count = 32
    wide = tokens.astype(f32)
    scale = lax.rsqrt(jnp.mean(wide * wide, axis=1, keepdims=True) + 1e-05)
    normed = (wide * scale * norm_gain[None, :]).astype(jnp.bfloat16)
    slots = relative_slots(routes, cap)
    hits = (slots[:, :, None] == jnp.arange(slot_count, dtype=jnp.int32)[None, None, :]).astype(f32)
    picked = jnp.transpose(jnp.sum(hits, axis=1)).astype(jnp.bfloat16)
    buffer = jnp.dot(picked, normed, preferred_element_type=f32).astype(jnp.bfloat16)
    combine = jnp.sum(route_weights[:, :, None] * hits, axis=1)

    keep = buffer[:16]
    wg1, wu1, wd1 = (shift(w, "c", 1) for w in (wg0, wu0, wd0))
    got, wg1 = lax.optimization_barrier((shift(buffer[16:], "zl", 1), wg1))
    blocks = []
    for by in range(4):
        at = slice(by * cap, (by + 1) * cap)
        block = jnp.concatenate([keep[at], got[at]], axis=0)
        blocks.append(shift(block, "y", by) if by else block)
    blocks, wu1, wd1 = lax.optimization_barrier((blocks, wu1, wd1))
    rows = jnp.concatenate(blocks, axis=0)

    pieces = []
    held = [rows[:, start : start + size] for start, size, _ in CHAINS]
    last = None
    for step in range(4):
        came = [trade(h, order[step]) for h, (_, _, order) in zip(held, CHAINS)]
        for j in range(4):
            got = came[j] if last is None else after(came[j], last)
            if step < 3:
                held[j] = last = jnp.concatenate([held[j], got], axis=0)
            else:
                pieces += [held[j], got]
                last = got

    hidden = hidden_units(pieces, (wg0, wu0, wg1, wu1))

    held, away = [None] * 4, [None] * 4
    for j in range(4):
        held[j], away[j] = expert_out(hidden if j == 0 else after(hidden, away[j - 1]), wd0, wd1, j)
    last = None
    for step in (3, 2, 1, 0):
        came = [trade(a, order[step]) for a, (_, _, order) in zip(away, CHAINS)]
        half = held[0].shape[0] // 2
        for j in range(4):
            got = came[j] if last is None else after(came[j], last)
            if step:
                away[j] = last = add(held[j][half:], got[half:])
                held[j] = add(held[j][:half], got[:half])
            else:
                held[j] = last = add(held[j], got)
    mine = jnp.concatenate(held, axis=1)

    results = []
    for by in range(4):
        block = mine[8 * by : 8 * by + 8]
        results.append(shift(block, "y", -by) if by else block)
    kept = jnp.concatenate([r[:cap] for r in results], axis=0)
    away = jnp.concatenate([r[cap:] for r in results], axis=0)
    back = jnp.concatenate([kept, shift(away, "zl", 1)], axis=0)
    moe = jnp.dot(combine, back.astype(f32), precision=lax.Precision.HIGHEST)
    return (wide + moe).astype(jnp.bfloat16)


def solution(mesh):
    fine = Mesh(mesh.devices.reshape(4, 2, 4, 4, 2), AXES)
    rows = P(AXES, None)
    return jax.shard_map(
        per_device,
        mesh=fine,
        in_specs=(
            rows,
            P(),
            rows,
            rows,
            P(("zl", "y"), None, ("dp", "x", "c")),
            P(("zl", "y"), None, ("dp", "x", "c")),
            P(("zl", "y"), ("dp", "x", "c"), None),
        ),
        out_specs=rows,
        check_vma=False,
    )
```

```python
import functools

import jax
import jax.numpy as jnp
from jax import lax
from jax.experimental import pallas as pl
from jax.experimental.pallas import tpu as pltpu
from jax.sharding import Mesh
from jax.sharding import PartitionSpec as P

AXES = ("dp", "zl", "y", "x", "c")
STEPS = 6


def shift(value, axis, by):
    n = lax.axis_size(axis)
    return lax.ppermute(value, axis, [(i, (i + by) % n) for i in range(n)])


DIMS = {"xa": ("x", 1), "xb": ("x", 3), "za": ("dp", 1), "zb": ("dp", 3)}
CHAINS = (
    (0, 2048, ("za", "zb", "xb", "xa")),
    (2048, 2048, ("zb", "za", "xa", "xb")),
    (4096, 1024, ("xa", "xb", "zb", "za")),
    (5120, 1024, ("xb", "xa", "za", "zb")),
)
CANON = ("xa", "xb", "za", "zb")
UNIT = 32
HALF = 8 * UNIT


def canon_block(order, index):
    return sum(((index >> k) & 1) << CANON.index(d) for k, d in enumerate(order))


def trade(value, dim):
    axis, mask = DIMS[dim]
    return lax.ppermute(value, axis, [(i, i ^ mask) for i in range(4)])


def add(a, b):
    return (a.astype(jnp.float32) + b.astype(jnp.float32)).astype(a.dtype)


def after(value, *others):
    return lax.optimization_barrier((value, *others))[0]


def hidden_kernel(*refs):
    n = len(CHAINS)
    ins = refs[: 2 * n]
    wg0, wu0, wg1, wu1 = refs[2 * n : 2 * n + 4]
    hidden, part, acc = refs[2 * n + 4 :]
    step = pl.program_id(0)
    units = wg0.shape[1]
    f32 = jnp.float32
    at = 0
    for c, (_, width, order) in enumerate(CHAINS):
        steps = width // PART

        @pl.when((step >= at) & (step < at + steps))
        def _(c=c, order=order):
            for index in range(16):
                to = canon_block(order, index) * UNIT
                row = (index % 8) * UNIT
                part[to : to + UNIT, :] = ins[2 * c + index // 8][row : row + UNIT, :]

        at += steps

    @pl.when(step == 0)
    def _():
        acc[...] = jnp.zeros_like(acc)

    for i, w in enumerate((wg0, wu0, wg1, wu1)):
        acc[i] += jnp.dot(part[...], w[...], preferred_element_type=f32)

    @pl.when(step == STEPS - 1)
    def _():
        for i in range(2):
            gate = acc[2 * i]
            value = gate / (1.0 + jnp.exp(-gate)) * acc[2 * i + 1]
            hidden[:, i * units : (i + 1) * units] = value.astype(hidden.dtype)


def out_kernel(order, hidden, wd0, wd1, keep, away):
    units = wd0.shape[0]
    f32 = jnp.float32
    total = jnp.dot(hidden[:, :units], wd0[...], preferred_element_type=f32) + jnp.dot(
        hidden[:, units:], wd1[...], preferred_element_type=f32
    )
    total = total.astype(jnp.bfloat16)
    for index in range(16):
        row = canon_block(order, index) * UNIT
        to = (index % 8) * UNIT
        (keep, away)[index // 8][to : to + UNIT, :] = total[row : row + UNIT]


PART = 1024


def hidden_units(pieces, weights):
    width, units = weights[0].shape
    count = 2 * HALF
    in_specs = []
    for start, size, _ in CHAINS:
        low, steps = start // PART, size // PART
        to = lambda i, low=low, steps=steps: (0, jnp.clip(i - low, 0, steps - 1))
        in_specs += [pl.BlockSpec((HALF, PART), to)] * 2
    return pl.pallas_call(
        hidden_kernel,
        grid=(STEPS,),
        out_shape=jax.ShapeDtypeStruct((count, 2 * units), jnp.bfloat16),
        in_specs=in_specs + [pl.BlockSpec((PART, units), lambda i: (i, 0))] * 4,
        out_specs=pl.BlockSpec((count, 2 * units), lambda i: (0, 0)),
        scratch_shapes=[
            pltpu.VMEM((count, PART), jnp.bfloat16),
            pltpu.VMEM((4, count, units), jnp.float32),
        ],
        compiler_params=pltpu.CompilerParams(vmem_limit_bytes=32 << 20),
        cost_estimate=pl.CostEstimate(
            flops=8 * count * width * units,
            bytes_accessed=8 * width * units + 2 * count * width,
            transcendentals=2 * count * units,
        ),
        name="hidden",
    )(*pieces, *weights)


def expert_out(hidden, wd0, wd1, chain):
    start, size, order = CHAINS[chain]
    units = wd0.shape[0]
    low, count = start // PART, 2 * HALF
    shape = jax.ShapeDtypeStruct((HALF, size), jnp.bfloat16)
    return pl.pallas_call(
        functools.partial(out_kernel, order),
        grid=(size // PART,),
        out_shape=[shape] * 2,
        in_specs=[pl.BlockSpec((count, 2 * units), lambda i: (0, 0))]
        + [pl.BlockSpec((units, PART), lambda i: (0, low + i))] * 2,
        out_specs=[pl.BlockSpec((HALF, PART), lambda i: (0, i))] * 2,
        compiler_params=pltpu.CompilerParams(vmem_limit_bytes=24 << 20),
        cost_estimate=pl.CostEstimate(
            flops=4 * count * size * units,
            bytes_accessed=4 * size * units + 2 * count * size,
            transcendentals=0,
        ),
        name="out",
    )(hidden, wd0, wd1)


def relative_slots(routes, cap):
    flat = routes.reshape(-1)
    y_count = lax.axis_size("y")
    z = flat // y_count
    y = flat % y_count
    z = (z + lax.axis_index("zl")) % 2
    y = (y - lax.axis_index("y") + y_count) % y_count
    experts = 2 * y_count
    rel = z * y_count + y
    onehot = (rel[:, None] == jnp.arange(experts, dtype=jnp.int32)[None, :]).astype(jnp.int32)
    before = jnp.cumsum(onehot, axis=0) - onehot
    rank = jnp.sum(before * onehot, axis=1)
    return (rel * cap + rank).reshape(routes.shape)


def per_device(tokens, norm_gain, routes, route_weights, w_gate, w_up, w_down):
    f32 = jnp.float32
    wg0, wu0, wd0 = w_gate[0], w_up[0], w_down[0]
    cap = 4
    slot_count = 32
    wide = tokens.astype(f32)
    scale = lax.rsqrt(jnp.mean(wide * wide, axis=1, keepdims=True) + 1e-05)
    normed = (wide * scale * norm_gain[None, :]).astype(jnp.bfloat16)
    slots = relative_slots(routes, cap)
    hits = (slots[:, :, None] == jnp.arange(slot_count, dtype=jnp.int32)[None, None, :]).astype(f32)
    picked = jnp.transpose(jnp.sum(hits, axis=1)).astype(jnp.bfloat16)
    buffer = jnp.dot(picked, normed, preferred_element_type=f32).astype(jnp.bfloat16)
    combine = jnp.sum(route_weights[:, :, None] * hits, axis=1)

    keep = buffer[:16]
    wg1, wu1, wd1 = (shift(w, "c", 1) for w in (wg0, wu0, wd0))
    got, wg1 = lax.optimization_barrier((shift(buffer[16:], "zl", 1), wg1))
    blocks = []
    for by in range(4):
        at = slice(by * cap, (by + 1) * cap)
        block = jnp.concatenate([keep[at], got[at]], axis=0)
        blocks.append(shift(block, "y", by) if by else block)
    blocks, wu1, wd1 = lax.optimization_barrier((blocks, wu1, wd1))
    rows = jnp.concatenate(blocks, axis=0)

    pieces = []
    held = [rows[:, start : start + size] for start, size, _ in CHAINS]
    last = None
    for step in range(4):
        came = [trade(h, order[step]) for h, (_, _, order) in zip(held, CHAINS)]
        for j in (2, 3, 0, 1):
            if last is not None:
                came[j] = after(came[j], last)
            if step < 3:
                held[j] = last = jnp.concatenate([held[j], came[j]], axis=0)
            else:
                last = came[j]
    for h, c in zip(held, came):
        pieces += [h, c]

    hidden = hidden_units(pieces, (wg0, wu0, wg1, wu1))

    held, away = [None] * 4, [None] * 4
    for j in range(4):
        held[j], away[j] = expert_out(hidden if j == 0 else after(hidden, away[j - 1]), wd0, wd1, j)
    last = None
    for step in (3, 2, 1, 0):
        came = [trade(a, order[step]) for a, (_, _, order) in zip(away, CHAINS)]
        half = held[0].shape[0] // 2
        for j in range(4):
            got = came[j] if last is None else after(came[j], last)
            if step:
                away[j] = last = add(held[j][half:], got[half:])
                held[j] = add(held[j][:half], got[:half])
            else:
                held[j] = last = add(held[j], got)
    mine = jnp.concatenate(held, axis=1)

    results = []
    for by in range(4):
        block = mine[8 * by : 8 * by + 8]
        results.append(shift(block, "y", -by) if by else block)
    kept = jnp.concatenate([r[:cap] for r in results], axis=0)
    away = jnp.concatenate([r[cap:] for r in results], axis=0)
    back = jnp.concatenate([kept, shift(away, "zl", 1)], axis=0)
    moe = jnp.dot(combine, back.astype(f32), precision=lax.Precision.HIGHEST)
    return (wide + moe).astype(jnp.bfloat16)


def solution(mesh):
    fine = Mesh(mesh.devices.reshape(4, 2, 4, 4, 2), AXES)
    rows = P(AXES, None)
    return jax.shard_map(
        per_device,
        mesh=fine,
        in_specs=(
            rows,
            P(),
            rows,
            rows,
            P(("zl", "y"), None, ("dp", "x", "c")),
            P(("zl", "y"), None, ("dp", "x", "c")),
            P(("zl", "y"), ("dp", "x", "c"), None),
        ),
        out_specs=rows,
        check_vma=False,
    )
```

```python
import functools

import jax
import jax.numpy as jnp
from jax import lax
from jax.experimental import pallas as pl
from jax.experimental.pallas import tpu as pltpu
from jax.sharding import Mesh
from jax.sharding import PartitionSpec as P

AXES = ("dp", "zl", "y", "x", "c")
STEPS = 6


DIMS = {"xa": ("x", 1), "xb": ("x", 3), "za": ("dp", 1), "zb": ("dp", 3), "c": ("c", 1)}
CHAINS = (
    (0, 2048, ("za", "zb", "xb", "xa")),
    (3072, 2048, ("zb", "za", "xa", "xb")),
    (2048, 1024, ("xa", "xb", "zb", "za")),
    (5120, 1024, ("xb", "xa", "za", "zb")),
)
CANON = ("xa", "xb", "za", "zb")
UNIT = 32
HALF = 8 * UNIT


def canon_block(order, index):
    return sum(((index >> k) & 1) << CANON.index(d) for k, d in enumerate(order))


def trade(value, dim):
    axis, mask = DIMS[dim]
    n = lax.axis_size(axis)
    return lax.ppermute(value, axis, [(i, i ^ mask) for i in range(n)])


def add(a, b):
    return (a.astype(jnp.float32) + b.astype(jnp.float32)).astype(a.dtype)


def after(value, *others):
    return lax.optimization_barrier((value, *others))[0]


def hidden_kernel(chains, first, last, *refs):
    n = len(chains)
    ins = refs[: 2 * n]
    wg0, wu0, wg1, wu1 = refs[2 * n : 2 * n + 4]
    refs = refs[2 * n + 4 :]
    before = None if first else refs[0]
    refs = refs if first else refs[1:]
    total, part = refs[0], refs[1]
    acc = refs[2] if last else total
    step = pl.program_id(0)
    units = wg0.shape[1]
    f32 = jnp.float32
    at = 0
    for k, c in enumerate(chains):
        _, width, order = CHAINS[c]
        steps = width // PART

        @pl.when((step >= at) & (step < at + steps))
        def _(k=k, order=order):
            for index in range(16):
                to = canon_block(order, index) * UNIT
                row = (index % 8) * UNIT
                part[to : to + UNIT, :] = ins[2 * k + index // 8][row : row + UNIT, :]

        at += steps

    @pl.when(step == 0)
    def _():
        acc[...] = jnp.zeros_like(acc) if first else before[...]

    for i, w in enumerate((wg0, wu0, wg1, wu1)):
        acc[i] += jnp.dot(part[...], w[...], preferred_element_type=f32)

    if last:

        @pl.when(step == at - 1)
        def _():
            for i in range(2):
                gate = acc[2 * i]
                value = gate / (1.0 + jnp.exp(-gate)) * acc[2 * i + 1]
                total[:, i * units : (i + 1) * units] = value.astype(total.dtype)


def out_kernel(order, hidden, wd0, wd1, keep, away):
    units = wd0.shape[0]
    f32 = jnp.float32
    total = jnp.dot(hidden[:, :units], wd0[...], preferred_element_type=f32) + jnp.dot(
        hidden[:, units:], wd1[...], preferred_element_type=f32
    )
    total = total.astype(jnp.bfloat16)
    for index in range(16):
        row = canon_block(order, index) * UNIT
        to = (index % 8) * UNIT
        (keep, away)[index // 8][to : to + UNIT, :] = total[row : row + UNIT]


PART = 1024


def pick(table, i):
    value = table[0]
    for k, entry in enumerate(table[1:], 1):
        value = jnp.where(i >= k, entry, value)
    return value


def hidden_units(pieces, weights, chains, before, last):
    width, units = weights[0].shape
    count = 2 * HALF
    first = before is None
    in_specs, parts = [], []
    for c in chains:
        start, size, _ = CHAINS[c]
        low, steps = len(parts), size // PART
        to = lambda i, low=low, steps=steps: (0, jnp.clip(i - low, 0, steps - 1))
        in_specs += [pl.BlockSpec((HALF, PART), to)] * 2
        parts += [start // PART + k for k in range(steps)]
    whole = lambda *shape: pl.BlockSpec(shape, lambda i: (0,) * len(shape))
    in_specs += [pl.BlockSpec((PART, units), lambda i: (pick(parts, i), 0))] * 4
    sums = (4, count, units)
    if not first:
        in_specs.append(whole(*sums))
    scratch = [pltpu.VMEM((count, PART), jnp.bfloat16)]
    if last:
        out, out_spec = jax.ShapeDtypeStruct((count, 2 * units), jnp.bfloat16), whole(count, 2 * units)
        scratch.append(pltpu.VMEM(sums, jnp.float32))
    else:
        out, out_spec = jax.ShapeDtypeStruct(sums, jnp.float32), whole(*sums)
    depth = len(parts) * PART
    return pl.pallas_call(
        functools.partial(hidden_kernel, chains, first, last),
        grid=(len(parts),),
        out_shape=out,
        in_specs=in_specs,
        out_specs=out_spec,
        scratch_shapes=scratch,
        compiler_params=pltpu.CompilerParams(vmem_limit_bytes=32 << 20),
        cost_estimate=pl.CostEstimate(
            flops=8 * count * depth * units,
            bytes_accessed=8 * depth * units + 2 * count * depth,
            transcendentals=2 * count * units if last else 0,
        ),
        name="hidden",
    )(*pieces, *weights, *(() if first else (before,)))


def expert_out(hidden, wd0, wd1, chain):
    start, size, order = CHAINS[chain]
    units = wd0.shape[0]
    low, count = start // PART, 2 * HALF
    shape = jax.ShapeDtypeStruct((HALF, size), jnp.bfloat16)
    return pl.pallas_call(
        functools.partial(out_kernel, order),
        grid=(size // PART,),
        out_shape=[shape] * 2,
        in_specs=[pl.BlockSpec((count, 2 * units), lambda i: (0, 0))]
        + [pl.BlockSpec((units, PART), lambda i: (0, low + i))] * 2,
        out_specs=[pl.BlockSpec((HALF, PART), lambda i: (0, i))] * 2,
        compiler_params=pltpu.CompilerParams(vmem_limit_bytes=24 << 20),
        cost_estimate=pl.CostEstimate(
            flops=4 * count * size * units,
            bytes_accessed=4 * size * units + 2 * count * size,
            transcendentals=0,
        ),
        name="out",
    )(hidden, wd0, wd1)


def onehot(rows, columns, hit):
    row = lax.broadcasted_iota(jnp.int32, (rows, columns), 0)
    column = lax.broadcasted_iota(jnp.int32, (rows, columns), 1)
    return hit(row, column).astype(jnp.bfloat16)


def place_kernel(routes, weights, tokens, gain, folded, combine):
    f32 = jnp.float32
    count, width = tokens.shape
    half = width // 2
    wide = tokens[...].astype(f32)
    scale = lax.rsqrt(jnp.mean(wide * wide, axis=1, keepdims=True) + 1e-05)
    normed = (wide * scale * gain[...]).astype(jnp.bfloat16)
    rows = folded.shape[0]
    row = lax.broadcasted_iota(jnp.int32, (rows, 2 * count), 0)
    column = lax.broadcasted_iota(jnp.int32, (rows, 2 * count), 1)
    slot = lax.broadcasted_iota(jnp.int32, (2 * count, rows), 1)
    token = lax.broadcasted_iota(jnp.int32, (2 * count, rows), 0)
    picked = jnp.zeros((rows, 2 * count), f32)
    mixing = jnp.zeros((2 * count, rows), f32)
    flat = [routes[t, k] for t in range(count) for k in range(2)]
    for i, expert in enumerate(flat):
        rank = jnp.int32(0)
        for other in flat[:i]:
            rank += (other == expert).astype(jnp.int32)
        at = expert * 8 + rank
        weight = weights[i // 2, i % 2]
        for side in range(2):
            where = at + 4 * side
            of = i // 2 + count * side
            picked = jnp.where((row == where) & (column == of), 1.0, picked)
            mixing = jnp.where((slot == where) & (token == of), weight, mixing)
    picked = picked.astype(jnp.bfloat16)
    combine[...] = mixing
    both = jnp.concatenate([normed[:, :half], normed[:, half:]], axis=0)
    folded[...] = jnp.dot(picked, both, preferred_element_type=f32).astype(folded.dtype)


def unfold_kernel(folded, *outs):
    half = folded.shape[1]
    for side in range(2):
        take = onehot(UNIT, 2 * UNIT, lambda r, c: c == (r // 4) * 8 + r % 4 + 4 * side)
        rows = jnp.dot(take, folded[...], preferred_element_type=jnp.float32)
        for out, (start, size, _) in zip(outs, CHAINS):
            if start // half == side:
                out[...] = rows[:, start - side * half : start - side * half + size].astype(out.dtype)


def fold_kernel(*refs):
    n = len(CHAINS)
    held, came, folded = refs[:n], refs[n : 2 * n], refs[2 * n]
    half = folded.shape[1]
    f32 = jnp.float32
    for c, (start, size, _) in enumerate(CHAINS):
        total = (held[c][...].astype(f32) + came[c][...].astype(f32)).astype(folded.dtype)
        side = start // half
        give = onehot(2 * UNIT, UNIT, lambda r, c: r == (c // 4) * 8 + c % 4 + 4 * side)
        rows = jnp.dot(give, total, preferred_element_type=f32).astype(folded.dtype)
        columns = slice(start - side * half, start - side * half + size)
        if side == 0:
            folded[:, columns] = rows
        else:
            folded[:, columns] = folded[:, columns] + rows


def mix_kernel(tokens, combine, back, out):
    half = back.shape[1]
    count = tokens.shape[0]
    f32 = jnp.float32
    moe = jnp.dot(
        combine[...],
        back[...].astype(f32),
        precision=lax.Precision.HIGHEST,
        preferred_element_type=f32,
    )
    for side in range(2):
        columns = slice(side * half, side * half + half)
        total = tokens[:, columns].astype(f32) + moe[side * count : side * count + count]
        out[:, columns] = total.astype(out.dtype)


def small(kernel, out_shape, *args, scalars=0, name):
    vmem, smem = pl.BlockSpec(memory_space=pltpu.VMEM), pl.BlockSpec(memory_space=pltpu.SMEM)
    return pl.pallas_call(
        kernel,
        out_shape=out_shape,
        in_specs=[smem] * scalars + [vmem] * (len(args) - scalars),
        out_specs=jax.tree.map(lambda _: vmem, out_shape),
        compiler_params=pltpu.CompilerParams(vmem_limit_bytes=16 << 20),
        name=name,
    )(*args)


def swap_experts(folded):
    blocks = folded.reshape(8, 8, folded.shape[1])
    blocks = lax.all_to_all(blocks, ("zl", "y"), split_axis=0, concat_axis=0, tiled=True)
    return blocks.reshape(folded.shape)


def per_device(tokens, norm_gain, routes, route_weights, w_gate, w_up, w_down):
    bf16 = jnp.bfloat16
    count, width = tokens.shape
    wg0, wu0, wd0 = w_gate[0], w_up[0], w_down[0]
    wg1, wu1, wd1 = (trade(w, "c") for w in (wg0, wu0, wd0))

    folded_shape = jax.ShapeDtypeStruct((64, width // 2), bf16)
    folded, combine = small(
        place_kernel,
        [folded_shape, jax.ShapeDtypeStruct((2 * count, 64), jnp.float32)],
        routes,
        route_weights,
        tokens,
        norm_gain.reshape(1, width),
        scalars=2,
        name="place",
    )
    folded = swap_experts(folded)
    folded, wg1, wu1, wd1 = lax.optimization_barrier((folded, wg1, wu1, wd1))
    heads = [jax.ShapeDtypeStruct((UNIT, size), bf16) for _, size, _ in CHAINS]
    held = list(small(unfold_kernel, heads, folded, name="unfold"))

    last = None
    for step in range(4):
        came = [trade(h, order[step]) for h, (_, _, order) in zip(held, CHAINS)]
        if step == 3:
            break
        for j in (2, 3, 0, 1):
            if last is not None:
                came[j] = after(came[j], last)
            held[j] = last = jnp.concatenate([held[j], came[j]], axis=0)
    for j in (2, 3, 0, 1):
        came[j] = last = after(came[j], last)
    pieces = [piece for pair in zip(held, came) for piece in pair]
    hidden = hidden_units(pieces, (wg0, wu0, wg1, wu1), (0, 1, 2, 3), None, True)

    held, away = [None] * 4, [None] * 4
    for j in range(4):
        held[j], away[j] = expert_out(hidden if j == 0 else after(hidden, away[j - 1]), wd0, wd1, j)
    last = None
    for step in (3, 2, 1, 0):
        came = [trade(a, order[step]) for a, (_, _, order) in zip(away, CHAINS)]
        if not step:
            break
        half = held[0].shape[0] // 2
        for j in range(4):
            got = came[j] if last is None else after(came[j], last)
            away[j] = last = add(held[j][half:], got[half:])
            held[j] = add(held[j][:half], got[:half])

    folded = small(fold_kernel, folded_shape, *held, *came, name="fold")
    back = swap_experts(folded)
    out = jax.ShapeDtypeStruct(tokens.shape, bf16)
    return small(mix_kernel, out, tokens, combine, back, name="mix")


def solution(mesh):
    fine = Mesh(mesh.devices.reshape(4, 2, 4, 4, 2), AXES)
    rows = P(AXES, None)
    return jax.shard_map(
        per_device,
        mesh=fine,
        in_specs=(
            rows,
            P(),
            rows,
            rows,
            P(("zl", "y"), None, ("dp", "x", "c")),
            P(("zl", "y"), None, ("dp", "x", "c")),
            P(("zl", "y"), ("dp", "x", "c"), None),
        ),
        out_specs=rows,
        check_vma=False,
    )
```

```python
import functools

import jax
import jax.numpy as jnp
from jax import lax
from jax.experimental import pallas as pl
from jax.experimental.pallas import tpu as pltpu
from jax.sharding import Mesh
from jax.sharding import PartitionSpec as P

AXES = ("dp", "zl", "y", "x", "c")
STEPS = 6


DIMS = {"xa": ("x", 1), "xb": ("x", 3), "za": ("dp", 1), "zb": ("dp", 3), "c": ("c", 1)}
CHAINS = (
    (0, 2048, ("za", "zb", "xb", "xa")),
    (3072, 2048, ("zb", "za", "xa", "xb")),
    (2048, 1024, ("xa", "xb", "zb", "za")),
    (5120, 1024, ("xb", "xa", "za", "zb")),
)
CANON = ("xa", "xb", "za", "zb")
UNIT = 32
HALF = 8 * UNIT


def canon_block(order, index):
    return sum(((index >> k) & 1) << CANON.index(d) for k, d in enumerate(order))


def trade(value, dim):
    axis, mask = DIMS[dim]
    n = lax.axis_size(axis)
    return lax.ppermute(value, axis, [(i, i ^ mask) for i in range(n)])


def add(a, b):
    return (a.astype(jnp.float32) + b.astype(jnp.float32)).astype(a.dtype)


def after(value, *others):
    return lax.optimization_barrier((value, *others))[0]


def hidden_kernel(chains, first, last, *refs):
    n = len(chains)
    ins = refs[: 2 * n]
    wg0, wu0, wg1, wu1 = refs[2 * n : 2 * n + 4]
    refs = refs[2 * n + 4 :]
    before = None if first else refs[0]
    refs = refs if first else refs[1:]
    total, part = refs[0], refs[1]
    acc = refs[2] if last else total
    step = pl.program_id(0)
    units = wg0.shape[1]
    f32 = jnp.float32
    at = 0
    for k, c in enumerate(chains):
        _, width, order = CHAINS[c]
        steps = width // PART

        @pl.when((step >= at) & (step < at + steps))
        def _(k=k, order=order):
            for index in range(16):
                to = canon_block(order, index) * UNIT
                row = (index % 8) * UNIT
                part[to : to + UNIT, :] = ins[2 * k + index // 8][row : row + UNIT, :]

        at += steps

    @pl.when(step == 0)
    def _():
        acc[...] = jnp.zeros_like(acc) if first else before[...]

    for i, w in enumerate((wg0, wu0, wg1, wu1)):
        acc[i] += jnp.dot(part[...], w[...], preferred_element_type=f32)

    if last:

        @pl.when(step == at - 1)
        def _():
            for i in range(2):
                gate = acc[2 * i]
                value = gate / (1.0 + jnp.exp(-gate)) * acc[2 * i + 1]
                total[:, i * units : (i + 1) * units] = value.astype(total.dtype)


def out_kernel(order, hidden, wd0, wd1, keep, away):
    units = wd0.shape[0]
    f32 = jnp.float32
    total = jnp.dot(hidden[:, :units], wd0[...], preferred_element_type=f32) + jnp.dot(
        hidden[:, units:], wd1[...], preferred_element_type=f32
    )
    total = total.astype(jnp.bfloat16)
    for index in range(16):
        row = canon_block(order, index) * UNIT
        to = (index % 8) * UNIT
        (keep, away)[index // 8][to : to + UNIT, :] = total[row : row + UNIT]


PART = 1024


def pick(table, i):
    value = table[0]
    for k, entry in enumerate(table[1:], 1):
        value = jnp.where(i >= k, entry, value)
    return value


def hidden_units(pieces, weights, chains, before, last):
    width, units = weights[0].shape
    count = 2 * HALF
    first = before is None
    in_specs, parts = [], []
    for c in chains:
        start, size, _ = CHAINS[c]
        low, steps = len(parts), size // PART
        to = lambda i, low=low, steps=steps: (0, jnp.clip(i - low, 0, steps - 1))
        in_specs += [pl.BlockSpec((HALF, PART), to)] * 2
        parts += [start // PART + k for k in range(steps)]
    whole = lambda *shape: pl.BlockSpec(shape, lambda i: (0,) * len(shape))
    in_specs += [pl.BlockSpec((PART, units), lambda i: (pick(parts, i), 0))] * 4
    sums = (4, count, units)
    if not first:
        in_specs.append(whole(*sums))
    scratch = [pltpu.VMEM((count, PART), jnp.bfloat16)]
    if last:
        out, out_spec = jax.ShapeDtypeStruct((count, 2 * units), jnp.bfloat16), whole(count, 2 * units)
        scratch.append(pltpu.VMEM(sums, jnp.float32))
    else:
        out, out_spec = jax.ShapeDtypeStruct(sums, jnp.float32), whole(*sums)
    depth = len(parts) * PART
    return pl.pallas_call(
        functools.partial(hidden_kernel, chains, first, last),
        grid=(len(parts),),
        out_shape=out,
        in_specs=in_specs,
        out_specs=out_spec,
        scratch_shapes=scratch,
        compiler_params=pltpu.CompilerParams(vmem_limit_bytes=32 << 20),
        cost_estimate=pl.CostEstimate(
            flops=8 * count * depth * units,
            bytes_accessed=8 * depth * units + 2 * count * depth,
            transcendentals=2 * count * units if last else 0,
        ),
        name="hidden",
    )(*pieces, *weights, *(() if first else (before,)))


def expert_out(hidden, wd0, wd1, chain):
    start, size, order = CHAINS[chain]
    units = wd0.shape[0]
    low, count = start // PART, 2 * HALF
    shape = jax.ShapeDtypeStruct((HALF, size), jnp.bfloat16)
    return pl.pallas_call(
        functools.partial(out_kernel, order),
        grid=(size // PART,),
        out_shape=[shape] * 2,
        in_specs=[pl.BlockSpec((count, 2 * units), lambda i: (0, 0))]
        + [pl.BlockSpec((units, PART), lambda i: (0, low + i))] * 2,
        out_specs=[pl.BlockSpec((HALF, PART), lambda i: (0, i))] * 2,
        compiler_params=pltpu.CompilerParams(vmem_limit_bytes=24 << 20),
        cost_estimate=pl.CostEstimate(
            flops=4 * count * size * units,
            bytes_accessed=4 * size * units + 2 * count * size,
            transcendentals=0,
        ),
        name="out",
    )(hidden, wd0, wd1)


def onehot(rows, columns, hit):
    row = lax.broadcasted_iota(jnp.int32, (rows, columns), 0)
    column = lax.broadcasted_iota(jnp.int32, (rows, columns), 1)
    return hit(row, column).astype(jnp.bfloat16)


def place_kernel(routes, weights, tokens, gain, folded, combine):
    f32 = jnp.float32
    count, width = tokens.shape
    half = width // 2
    wide = tokens[...].astype(f32)
    scale = lax.rsqrt(jnp.mean(wide * wide, axis=1, keepdims=True) + 1e-05)
    normed = (wide * scale * gain[...]).astype(jnp.bfloat16)
    rows = folded.shape[0]
    row = lax.broadcasted_iota(jnp.int32, (rows, 2 * count), 0)
    column = lax.broadcasted_iota(jnp.int32, (rows, 2 * count), 1)
    slot = lax.broadcasted_iota(jnp.int32, (2 * count, rows), 1)
    token = lax.broadcasted_iota(jnp.int32, (2 * count, rows), 0)
    picked = jnp.zeros((rows, 2 * count), f32)
    mixing = jnp.zeros((2 * count, rows), f32)
    flat = [routes[k, t] for t in range(count) for k in range(2)]
    for i, expert in enumerate(flat):
        rank = jnp.int32(0)
        for other in flat[:i]:
            rank += (other == expert).astype(jnp.int32)
        at = expert * 8 + rank
        weight = weights[i % 2, i // 2]
        for side in range(2):
            where = at + 4 * side
            of = i // 2 + count * side
            picked = jnp.where((row == where) & (column == of), 1.0, picked)
            mixing = jnp.where((slot == where) & (token == of), weight, mixing)
    picked = picked.astype(jnp.bfloat16)
    combine[...] = mixing
    both = jnp.concatenate([normed[:, :half], normed[:, half:]], axis=0)
    folded[...] = jnp.dot(picked, both, preferred_element_type=f32).astype(folded.dtype)


def unfold_kernel(folded, *outs):
    half = folded.shape[1]
    for side in range(2):
        take = onehot(UNIT, 2 * UNIT, lambda r, c: c == (r // 4) * 8 + r % 4 + 4 * side)
        rows = jnp.dot(take, folded[...], preferred_element_type=jnp.float32)
        for out, (start, size, _) in zip(outs, CHAINS):
            if start // half == side:
                out[...] = rows[:, start - side * half : start - side * half + size].astype(out.dtype)


def fold_kernel(*refs):
    n = len(CHAINS)
    held, came, folded = refs[:n], refs[n : 2 * n], refs[2 * n]
    half = folded.shape[1]
    f32 = jnp.float32
    for c, (start, size, _) in enumerate(CHAINS):
        total = (held[c][...].astype(f32) + came[c][...].astype(f32)).astype(folded.dtype)
        side = start // half
        give = onehot(2 * UNIT, UNIT, lambda r, c: r == (c // 4) * 8 + c % 4 + 4 * side)
        rows = jnp.dot(give, total, preferred_element_type=f32).astype(folded.dtype)
        columns = slice(start - side * half, start - side * half + size)
        if side == 0:
            folded[:, columns] = rows
        else:
            folded[:, columns] = folded[:, columns] + rows


def mix_kernel(tokens, combine, back, out):
    half = back.shape[1]
    count = tokens.shape[0]
    f32 = jnp.float32
    moe = jnp.dot(
        combine[...],
        back[...].astype(f32),
        precision=lax.Precision.HIGHEST,
        preferred_element_type=f32,
    )
    for side in range(2):
        columns = slice(side * half, side * half + half)
        total = tokens[:, columns].astype(f32) + moe[side * count : side * count + count]
        out[:, columns] = total.astype(out.dtype)


def small(kernel, out_shape, *args, scalars=0, name):
    vmem, smem = pl.BlockSpec(memory_space=pltpu.VMEM), pl.BlockSpec(memory_space=pltpu.SMEM)
    return pl.pallas_call(
        kernel,
        out_shape=out_shape,
        in_specs=[smem] * scalars + [vmem] * (len(args) - scalars),
        out_specs=jax.tree.map(lambda _: vmem, out_shape),
        compiler_params=pltpu.CompilerParams(vmem_limit_bytes=16 << 20),
        name=name,
    )(*args)


def swap_experts(folded):
    blocks = folded.reshape(8, 8, folded.shape[1])
    blocks = lax.all_to_all(blocks, ("zl", "y"), split_axis=0, concat_axis=0, tiled=True)
    return blocks.reshape(folded.shape)


def per_device(tokens, norm_gain, routes, route_weights, w_gate, w_up, w_down):
    bf16 = jnp.bfloat16
    count, width = tokens.shape
    wg0, wu0, wd0 = w_gate[0], w_up[0], w_down[0]
    wg1, wu1, wd1 = (trade(w, "c") for w in (wg0, wu0, wd0))

    folded_shape = jax.ShapeDtypeStruct((64, width // 2), bf16)
    folded, combine = small(
        place_kernel,
        [folded_shape, jax.ShapeDtypeStruct((2 * count, 64), jnp.float32)],
        routes.T,
        route_weights.T,
        tokens,
        norm_gain.reshape(1, width),
        scalars=2,
        name="place",
    )
    folded = swap_experts(folded)
    folded, wg1, wu1, wd1 = lax.optimization_barrier((folded, wg1, wu1, wd1))
    heads = [jax.ShapeDtypeStruct((UNIT, size), bf16) for _, size, _ in CHAINS]
    held = list(small(unfold_kernel, heads, folded, name="unfold"))

    last = None
    for step in range(4):
        came = [trade(h, order[step]) for h, (_, _, order) in zip(held, CHAINS)]
        if step == 3:
            break
        for j in (0, 1, 2, 3) if step == 1 else (2, 3, 0, 1):
            if last is not None:
                came[j] = after(came[j], last)
            held[j] = last = jnp.concatenate([held[j], came[j]], axis=0)
    for j in (2, 3, 0, 1):
        came[j] = last = after(came[j], last)
    pieces = [piece for pair in zip(held, came) for piece in pair]
    hidden = hidden_units(pieces, (wg0, wu0, wg1, wu1), (0, 1, 2, 3), None, True)

    held, away = [None] * 4, [None] * 4
    last = None
    for j in (2, 3, 0, 1):
        held[j], away[j] = expert_out(hidden if last is None else after(hidden, last), wd0, wd1, j)
        last = away[j]
    last = None
    for step in (3, 2, 1, 0):
        came = [trade(a, order[step]) for a, (_, _, order) in zip(away, CHAINS)]
        if not step:
            break
        half = held[0].shape[0] // 2
        for j in (2, 3, 0, 1):
            got = came[j] if last is None else after(came[j], last)
            away[j] = last = add(held[j][half:], got[half:])
            held[j] = add(held[j][:half], got[:half])

    folded = small(fold_kernel, folded_shape, *held, *came, name="fold")
    back = swap_experts(folded)
    out = jax.ShapeDtypeStruct(tokens.shape, bf16)
    return small(mix_kernel, out, tokens, combine, back, name="mix")


def solution(mesh):
    fine = Mesh(mesh.devices.reshape(4, 2, 4, 4, 2), AXES)
    rows = P(AXES, None)
    return jax.shard_map(
        per_device,
        mesh=fine,
        in_specs=(
            rows,
            P(),
            rows,
            rows,
            P(("zl", "y"), None, ("dp", "x", "c")),
            P(("zl", "y"), None, ("dp", "x", "c")),
            P(("zl", "y"), ("dp", "x", "c"), None),
        ),
        out_specs=rows,
        check_vma=False,
    )
```

```python
import functools

import jax
import jax.numpy as jnp
from jax import lax
from jax.experimental import pallas as pl
from jax.experimental.pallas import tpu as pltpu
from jax.sharding import Mesh
from jax.sharding import PartitionSpec as P

AXES = ("dp", "zl", "y", "x", "c")
STEPS = 6


DIMS = {"xa": ("x", 1), "xb": ("x", 3), "za": ("dp", 1), "zb": ("dp", 3), "c": ("c", 1)}
CHAINS = (
    (0, 2048, ("za", "zb", "xb", "xa")),
    (3072, 2048, ("zb", "za", "xa", "xb")),
    (2048, 1024, ("xa", "xb", "zb", "za")),
    (5120, 1024, ("xb", "xa", "za", "zb")),
)
OUT_CHAINS = tuple(
    (start, size, order)
    for (start, size), (_, _, order) in zip(
        ((0, 2304), (3072, 2304), (2304, 768), (5376, 768)), CHAINS
    )
)
CANON = ("xa", "xb", "za", "zb")
UNIT = 32
HALF = 8 * UNIT


def canon_block(order, index):
    return sum(((index >> k) & 1) << CANON.index(d) for k, d in enumerate(order))


def trade(value, dim):
    axis, mask = DIMS[dim]
    n = lax.axis_size(axis)
    return lax.ppermute(value, axis, [(i, i ^ mask) for i in range(n)])


def add(a, b):
    return (a.astype(jnp.float32) + b.astype(jnp.float32)).astype(a.dtype)


def after(value, *others):
    return lax.optimization_barrier((value, *others))[0]


def hidden_kernel(chains, first, last, *refs):
    n = len(chains)
    ins = refs[: 2 * n]
    wg0, wu0, wg1, wu1 = refs[2 * n : 2 * n + 4]
    refs = refs[2 * n + 4 :]
    before = None if first else refs[0]
    refs = refs if first else refs[1:]
    total, part = refs[0], refs[1]
    acc = refs[2] if last else total
    step = pl.program_id(0)
    units = wg0.shape[1]
    f32 = jnp.float32
    at = 0
    for k, c in enumerate(chains):
        _, width, order = CHAINS[c]
        steps = width // PART

        @pl.when((step >= at) & (step < at + steps))
        def _(k=k, order=order):
            for index in range(16):
                to = canon_block(order, index) * UNIT
                row = (index % 8) * UNIT
                part[to : to + UNIT, :] = ins[2 * k + index // 8][row : row + UNIT, :]

        at += steps

    @pl.when(step == 0)
    def _():
        acc[...] = jnp.zeros_like(acc) if first else before[...]

    for i, w in enumerate((wg0, wu0, wg1, wu1)):
        acc[i] += jnp.dot(part[...], w[...], preferred_element_type=f32)

    if last:

        @pl.when(step == at - 1)
        def _():
            for i in range(2):
                gate = acc[2 * i]
                value = gate / (1.0 + jnp.exp(-gate)) * acc[2 * i + 1]
                total[:, i * units : (i + 1) * units] = value.astype(total.dtype)


def out_kernel(order, hidden, wd0, wd1, keep, away):
    units = wd0.shape[0]
    f32 = jnp.float32
    total = jnp.dot(hidden[:, :units], wd0[...], preferred_element_type=f32) + jnp.dot(
        hidden[:, units:], wd1[...], preferred_element_type=f32
    )
    total = total.astype(jnp.bfloat16)
    for index in range(16):
        row = canon_block(order, index) * UNIT
        to = (index % 8) * UNIT
        (keep, away)[index // 8][to : to + UNIT, :] = total[row : row + UNIT]


PART = 1024
OUT_PART = 768


def pick(table, i):
    value = table[0]
    for k, entry in enumerate(table[1:], 1):
        value = jnp.where(i >= k, entry, value)
    return value


def hidden_units(pieces, weights, chains, before, last):
    width, units = weights[0].shape
    count = 2 * HALF
    first = before is None
    in_specs, parts = [], []
    for c in chains:
        start, size, _ = CHAINS[c]
        low, steps = len(parts), size // PART
        to = lambda i, low=low, steps=steps: (0, jnp.clip(i - low, 0, steps - 1))
        in_specs += [pl.BlockSpec((HALF, PART), to)] * 2
        parts += [start // PART + k for k in range(steps)]
    whole = lambda *shape: pl.BlockSpec(shape, lambda i: (0,) * len(shape))
    in_specs += [pl.BlockSpec((PART, units), lambda i: (pick(parts, i), 0))] * 4
    sums = (4, count, units)
    if not first:
        in_specs.append(whole(*sums))
    scratch = [pltpu.VMEM((count, PART), jnp.bfloat16)]
    if last:
        out, out_spec = jax.ShapeDtypeStruct((count, 2 * units), jnp.bfloat16), whole(count, 2 * units)
        scratch.append(pltpu.VMEM(sums, jnp.float32))
    else:
        out, out_spec = jax.ShapeDtypeStruct(sums, jnp.float32), whole(*sums)
    depth = len(parts) * PART
    return pl.pallas_call(
        functools.partial(hidden_kernel, chains, first, last),
        grid=(len(parts),),
        out_shape=out,
        in_specs=in_specs,
        out_specs=out_spec,
        scratch_shapes=scratch,
        compiler_params=pltpu.CompilerParams(vmem_limit_bytes=32 << 20),
        cost_estimate=pl.CostEstimate(
            flops=8 * count * depth * units if last else 0,
            bytes_accessed=8 * depth * units + 2 * count * depth if last else 0,
            transcendentals=2 * count * units if last else 0,
        ),
        name="hidden",
    )(*pieces, *weights, *(() if first else (before,)))


def expert_out(hidden, wd0, wd1, chain):
    start, size, order = OUT_CHAINS[chain]
    units = wd0.shape[0]
    low, count = start // OUT_PART, 2 * HALF
    shape = jax.ShapeDtypeStruct((HALF, size), jnp.bfloat16)
    return pl.pallas_call(
        functools.partial(out_kernel, order),
        grid=(size // OUT_PART,),
        out_shape=[shape] * 2,
        in_specs=[pl.BlockSpec((count, 2 * units), lambda i: (0, 0))]
        + [pl.BlockSpec((units, OUT_PART), lambda i: (0, low + i))] * 2,
        out_specs=[pl.BlockSpec((HALF, OUT_PART), lambda i: (0, i))] * 2,
        compiler_params=pltpu.CompilerParams(vmem_limit_bytes=24 << 20),
        cost_estimate=pl.CostEstimate(
            flops=4 * count * size * units,
            bytes_accessed=4 * size * units + 2 * count * size,
            transcendentals=0,
        ),
        name="out",
    )(hidden, wd0, wd1)


def onehot(rows, columns, hit):
    row = lax.broadcasted_iota(jnp.int32, (rows, columns), 0)
    column = lax.broadcasted_iota(jnp.int32, (rows, columns), 1)
    return hit(row, column).astype(jnp.bfloat16)


def place_kernel(routes, weights, tokens, gain, folded, combine):
    f32 = jnp.float32
    count, width = tokens.shape
    half = width // 2
    wide = tokens[...].astype(f32)
    scale = lax.rsqrt(jnp.mean(wide * wide, axis=1, keepdims=True) + 1e-05)
    normed = (wide * scale * gain[...]).astype(jnp.bfloat16)
    rows = folded.shape[0]
    row = lax.broadcasted_iota(jnp.int32, (rows, 2 * count), 0)
    column = lax.broadcasted_iota(jnp.int32, (rows, 2 * count), 1)
    slot = lax.broadcasted_iota(jnp.int32, (2 * count, rows), 1)
    token = lax.broadcasted_iota(jnp.int32, (2 * count, rows), 0)
    picked = jnp.zeros((rows, 2 * count), f32)
    mixing = jnp.zeros((2 * count, rows), f32)
    flat = [routes[k, t] for t in range(count) for k in range(2)]
    for i, expert in enumerate(flat):
        rank = jnp.int32(0)
        for other in flat[:i]:
            rank += (other == expert).astype(jnp.int32)
        at = expert * 8 + rank
        weight = weights[i % 2, i // 2]
        for side in range(2):
            where = at + 4 * side
            of = i // 2 + count * side
            picked = jnp.where((row == where) & (column == of), 1.0, picked)
            mixing = jnp.where((slot == where) & (token == of), weight, mixing)
    picked = picked.astype(jnp.bfloat16)
    combine[...] = mixing
    both = jnp.concatenate([normed[:, :half], normed[:, half:]], axis=0)
    folded[...] = jnp.dot(picked, both, preferred_element_type=f32).astype(folded.dtype)


def unfold_kernel(folded, *outs):
    half = folded.shape[1]
    for side in range(2):
        take = onehot(UNIT, 2 * UNIT, lambda r, c: c == (r // 4) * 8 + r % 4 + 4 * side)
        rows = jnp.dot(take, folded[...], preferred_element_type=jnp.float32)
        for out, (start, size, _) in zip(outs, CHAINS):
            if start // half == side:
                out[...] = rows[:, start - side * half : start - side * half + size].astype(out.dtype)


def fold_kernel(*refs):
    n = len(CHAINS)
    held, came, folded = refs[:n], refs[n : 2 * n], refs[2 * n]
    half = folded.shape[1]
    f32 = jnp.float32
    for c, (start, size, _) in enumerate(OUT_CHAINS):
        total = (held[c][...].astype(f32) + came[c][...].astype(f32)).astype(folded.dtype)
        side = start // half
        give = onehot(2 * UNIT, UNIT, lambda r, c: r == (c // 4) * 8 + c % 4 + 4 * side)
        rows = jnp.dot(give, total, preferred_element_type=f32).astype(folded.dtype)
        columns = slice(start - side * half, start - side * half + size)
        if side == 0:
            folded[:, columns] = rows
        else:
            folded[:, columns] = folded[:, columns] + rows


def mix_kernel(tokens, combine, back, out):
    half = back.shape[1]
    count = tokens.shape[0]
    f32 = jnp.float32
    moe = jnp.dot(
        combine[...],
        back[...].astype(f32),
        precision=lax.Precision.HIGHEST,
        preferred_element_type=f32,
    )
    for side in range(2):
        columns = slice(side * half, side * half + half)
        total = tokens[:, columns].astype(f32) + moe[side * count : side * count + count]
        out[:, columns] = total.astype(out.dtype)


def small(kernel, out_shape, *args, scalars=0, name):
    vmem, smem = pl.BlockSpec(memory_space=pltpu.VMEM), pl.BlockSpec(memory_space=pltpu.SMEM)
    return pl.pallas_call(
        kernel,
        out_shape=out_shape,
        in_specs=[smem] * scalars + [vmem] * (len(args) - scalars),
        out_specs=jax.tree.map(lambda _: vmem, out_shape),
        compiler_params=pltpu.CompilerParams(vmem_limit_bytes=16 << 20),
        name=name,
    )(*args)


def swap_experts(folded):
    blocks = folded.reshape(8, 8, folded.shape[1])
    blocks = lax.all_to_all(blocks, ("zl", "y"), split_axis=0, concat_axis=0, tiled=True)
    return blocks.reshape(folded.shape)


def per_device(tokens, norm_gain, routes, route_weights, w_gate, w_up, w_down):
    bf16 = jnp.bfloat16
    count, width = tokens.shape
    wg0, wu0, wd0 = w_gate[0], w_up[0], w_down[0]
    wg1, wu1, wd1 = (trade(w, "c") for w in (wg0, wu0, wd0))

    folded_shape = jax.ShapeDtypeStruct((64, width // 2), bf16)
    folded, combine = small(
        place_kernel,
        [folded_shape, jax.ShapeDtypeStruct((2 * count, 64), jnp.float32)],
        routes.T,
        route_weights.T,
        tokens,
        norm_gain.reshape(1, width),
        scalars=2,
        name="place",
    )
    folded = swap_experts(folded)
    folded, wg1, wu1, wd1 = lax.optimization_barrier((folded, wg1, wu1, wd1))
    heads = [jax.ShapeDtypeStruct((UNIT, size), bf16) for _, size, _ in CHAINS]
    held = list(small(unfold_kernel, heads, folded, name="unfold"))

    last = None
    for step in range(4):
        came = [trade(h, order[step]) for h, (_, _, order) in zip(held, CHAINS)]
        if step == 3:
            break
        for j in (2, 3, 0, 1):
            if last is not None:
                came[j] = after(came[j], last)
            held[j] = last = jnp.concatenate([held[j], came[j]], axis=0)
    weights = (wg0, wu0, wg1, wu1)
    came[0] = after(came[0], last)
    came[1] = after(came[1], came[0])
    sums = hidden_units((held[0], came[0], held[1], came[1]), weights, (0, 1), None, False)
    came[2] = after(came[2], sums)
    came[3] = after(came[3], came[2])
    hidden = hidden_units((held[2], came[2], held[3], came[3]), weights, (2, 3), sums, True)

    held, away = [None] * 4, [None] * 4
    last = None
    for j in range(4):
        held[j], away[j] = expert_out(hidden if last is None else after(hidden, last), wd0, wd1, j)
        last = away[j]
    last = None
    for step in (3, 2, 1, 0):
        came = [trade(a, order[step]) for a, (_, _, order) in zip(away, CHAINS)]
        if not step:
            break
        half = held[0].shape[0] // 2
        for j in range(4):
            got = came[j] if last is None else after(came[j], last)
            away[j] = last = add(held[j][half:], got[half:])
            held[j] = add(held[j][:half], got[:half])

    folded = small(fold_kernel, folded_shape, *held, *came, name="fold")
    back = swap_experts(folded)
    out = jax.ShapeDtypeStruct(tokens.shape, bf16)
    return small(mix_kernel, out, tokens, combine, back, name="mix")


def solution(mesh):
    fine = Mesh(mesh.devices.reshape(4, 2, 4, 4, 2), AXES)
    rows = P(AXES, None)
    return jax.shard_map(
        per_device,
        mesh=fine,
        in_specs=(
            rows,
            P(),
            rows,
            rows,
            P(("zl", "y"), None, ("dp", "x", "c")),
            P(("zl", "y"), None, ("dp", "x", "c")),
            P(("zl", "y"), ("dp", "x", "c"), None),
        ),
        out_specs=rows,
        check_vma=False,
    )
```

```python
import functools

import jax
import jax.numpy as jnp
from jax import lax
from jax.experimental import pallas as pl
from jax.experimental.pallas import tpu as pltpu
from jax.sharding import Mesh
from jax.sharding import PartitionSpec as P

AXES = ("dp", "zl", "y", "x", "c")
STEPS = 6


DIMS = {"xa": ("x", 1), "xb": ("x", 3), "za": ("dp", 1), "zb": ("dp", 3), "c": ("c", 1)}
CHAINS = (
    (0, 2048, ("za", "zb", "xb", "xa")),
    (3072, 2048, ("zb", "za", "xa", "xb")),
    (2048, 1024, ("xa", "xb", "zb", "za")),
    (5120, 1024, ("xb", "xa", "za", "zb")),
)
OUT_CHAINS = tuple(
    (start, size, order)
    for (start, size), (_, _, order) in zip(
        ((0, 2048), (3072, 2048), (2048, 1024), (5120, 1024)), CHAINS
    )
)
CANON = ("xa", "xb", "za", "zb")
UNIT = 32
HALF = 8 * UNIT


def canon_block(order, index):
    return sum(((index >> k) & 1) << CANON.index(d) for k, d in enumerate(order))


def trade(value, dim):
    axis, mask = DIMS[dim]
    n = lax.axis_size(axis)
    return lax.ppermute(value, axis, [(i, i ^ mask) for i in range(n)])


def add(a, b):
    return (a.astype(jnp.float32) + b.astype(jnp.float32)).astype(a.dtype)


def after(value, *others):
    return lax.optimization_barrier((value, *others))[0]


def hidden_kernel(chains, first, last, *refs):
    n = len(chains)
    ins = refs[: 2 * n]
    wg0, wu0, wg1, wu1 = refs[2 * n : 2 * n + 4]
    refs = refs[2 * n + 4 :]
    before = None if first else refs[0]
    refs = refs if first else refs[1:]
    total, part = refs[0], refs[1]
    acc = refs[2] if last else total
    step = pl.program_id(0)
    units = wg0.shape[1]
    f32 = jnp.float32
    at = 0
    for k, c in enumerate(chains):
        _, width, order = CHAINS[c]
        steps = width // PART

        @pl.when((step >= at) & (step < at + steps))
        def _(k=k, order=order):
            for index in range(16):
                to = canon_block(order, index) * UNIT
                row = (index % 8) * UNIT
                part[to : to + UNIT, :] = ins[2 * k + index // 8][row : row + UNIT, :]

        at += steps

    @pl.when(step == 0)
    def _():
        acc[...] = jnp.zeros_like(acc) if first else before[...]

    for i, w in enumerate((wg0, wu0, wg1, wu1)):
        acc[i] += jnp.dot(part[...], w[...], preferred_element_type=f32)

    if last:

        @pl.when(step == at - 1)
        def _():
            for i in range(2):
                gate = acc[2 * i]
                value = gate / (1.0 + jnp.exp(-gate)) * acc[2 * i + 1]
                total[:, i * units : (i + 1) * units] = value.astype(total.dtype)


def out_kernel(order, hidden, wd0, wd1, keep, away):
    units = wd0.shape[0]
    f32 = jnp.float32
    total = jnp.dot(hidden[:, :units], wd0[...], preferred_element_type=f32) + jnp.dot(
        hidden[:, units:], wd1[...], preferred_element_type=f32
    )
    total = total.astype(jnp.bfloat16)
    for index in range(16):
        row = canon_block(order, index) * UNIT
        to = (index % 8) * UNIT
        (keep, away)[index // 8][to : to + UNIT, :] = total[row : row + UNIT]


PART = 1024
OUT_PART = 1024


def pick(table, i):
    value = table[0]
    for k, entry in enumerate(table[1:], 1):
        value = jnp.where(i >= k, entry, value)
    return value


def hidden_units(pieces, weights, chains, before, last):
    width, units = weights[0].shape
    count = 2 * HALF
    first = before is None
    in_specs, parts = [], []
    for c in chains:
        start, size, _ = CHAINS[c]
        low, steps = len(parts), size // PART
        to = lambda i, low=low, steps=steps: (0, jnp.clip(i - low, 0, steps - 1))
        in_specs += [pl.BlockSpec((HALF, PART), to)] * 2
        parts += [start // PART + k for k in range(steps)]
    whole = lambda *shape: pl.BlockSpec(shape, lambda i: (0,) * len(shape))
    in_specs += [pl.BlockSpec((PART, units), lambda i: (pick(parts, i), 0))] * 4
    sums = (4, count, units)
    if not first:
        in_specs.append(whole(*sums))
    scratch = [pltpu.VMEM((count, PART), jnp.bfloat16)]
    if last:
        out, out_spec = jax.ShapeDtypeStruct((count, 2 * units), jnp.bfloat16), whole(count, 2 * units)
        scratch.append(pltpu.VMEM(sums, jnp.float32))
    else:
        out, out_spec = jax.ShapeDtypeStruct(sums, jnp.float32), whole(*sums)
    depth = len(parts) * PART
    return pl.pallas_call(
        functools.partial(hidden_kernel, chains, first, last),
        grid=(len(parts),),
        out_shape=out,
        in_specs=in_specs,
        out_specs=out_spec,
        scratch_shapes=scratch,
        compiler_params=pltpu.CompilerParams(vmem_limit_bytes=32 << 20),
        cost_estimate=pl.CostEstimate(
            flops=8 * count * depth * units if last else 0,
            bytes_accessed=8 * depth * units + 2 * count * depth if last else 0,
            transcendentals=2 * count * units if last else 0,
        ),
        name="hidden",
    )(*pieces, *weights, *(() if first else (before,)))


def expert_out(hidden, wd0, wd1, chain):
    start, size, order = OUT_CHAINS[chain]
    units = wd0.shape[0]
    low, count = start // OUT_PART, 2 * HALF
    shape = jax.ShapeDtypeStruct((HALF, size), jnp.bfloat16)
    return pl.pallas_call(
        functools.partial(out_kernel, order),
        grid=(size // OUT_PART,),
        out_shape=[shape] * 2,
        in_specs=[pl.BlockSpec((count, 2 * units), lambda i: (0, 0))]
        + [pl.BlockSpec((units, OUT_PART), lambda i: (0, low + i))] * 2,
        out_specs=[pl.BlockSpec((HALF, OUT_PART), lambda i: (0, i))] * 2,
        compiler_params=pltpu.CompilerParams(vmem_limit_bytes=24 << 20),
        cost_estimate=pl.CostEstimate(
            flops=4 * count * size * units,
            bytes_accessed=4 * size * units + 2 * count * size,
            transcendentals=0,
        ),
        name="out",
    )(hidden, wd0, wd1)


def onehot(rows, columns, hit):
    row = lax.broadcasted_iota(jnp.int32, (rows, columns), 0)
    column = lax.broadcasted_iota(jnp.int32, (rows, columns), 1)
    return hit(row, column).astype(jnp.bfloat16)


def place_kernel(*refs):
    folded, combine = refs[4:6]
    routes, weights, tokens, gain = refs[6:10]
    copies = [pltpu.make_async_copy(refs[i], refs[6 + i], refs[10].at[i]) for i in range(4)]
    for copy in copies:
        copy.start()
    for copy in copies:
        copy.wait()
    f32 = jnp.float32
    count, width = tokens.shape
    half = width // 2
    wide = tokens[...].astype(f32)
    scale = lax.rsqrt(jnp.mean(wide * wide, axis=1, keepdims=True) + 1e-05)
    normed = (wide * scale * gain[...]).astype(jnp.bfloat16)
    rows = folded.shape[0]
    row = lax.broadcasted_iota(jnp.int32, (rows, 2 * count), 0)
    column = lax.broadcasted_iota(jnp.int32, (rows, 2 * count), 1)
    slot = lax.broadcasted_iota(jnp.int32, (2 * count, rows), 1)
    token = lax.broadcasted_iota(jnp.int32, (2 * count, rows), 0)
    picked = jnp.zeros((rows, 2 * count), f32)
    mixing = jnp.zeros((2 * count, rows), f32)
    flat = [routes[k, t] for t in range(count) for k in range(2)]
    for i, expert in enumerate(flat):
        rank = jnp.int32(0)
        for other in flat[:i]:
            rank += (other == expert).astype(jnp.int32)
        at = expert * 8 + rank
        weight = weights[i % 2, i // 2]
        for side in range(2):
            where = at + 4 * side
            of = i // 2 + count * side
            picked = jnp.where((row == where) & (column == of), 1.0, picked)
            mixing = jnp.where((slot == where) & (token == of), weight, mixing)
    picked = picked.astype(jnp.bfloat16)
    combine[...] = mixing
    both = jnp.concatenate([normed[:, :half], normed[:, half:]], axis=0)
    folded[...] = jnp.dot(picked, both, preferred_element_type=f32).astype(folded.dtype)


def unfold_kernel(folded, *outs):
    half = folded.shape[1]
    for side in range(2):
        take = onehot(UNIT, 2 * UNIT, lambda r, c: c == (r // 4) * 8 + r % 4 + 4 * side)
        rows = jnp.dot(take, folded[...], preferred_element_type=jnp.float32)
        for out, (start, size, _) in zip(outs, CHAINS):
            if start // half == side:
                out[...] = rows[:, start - side * half : start - side * half + size].astype(out.dtype)


def fold_kernel(*refs):
    n = len(CHAINS)
    held, came, folded = refs[:n], refs[n : 2 * n], refs[2 * n]
    half = folded.shape[1]
    f32 = jnp.float32
    for c, (start, size, _) in enumerate(OUT_CHAINS):
        total = (held[c][...].astype(f32) + came[c][...].astype(f32)).astype(folded.dtype)
        side = start // half
        give = onehot(2 * UNIT, UNIT, lambda r, c: r == (c // 4) * 8 + c % 4 + 4 * side)
        rows = jnp.dot(give, total, preferred_element_type=f32).astype(folded.dtype)
        columns = slice(start - side * half, start - side * half + size)
        if side == 0:
            folded[:, columns] = rows
        else:
            folded[:, columns] = folded[:, columns] + rows


def mix_kernel(tokens, combine, back, out):
    half = back.shape[1]
    count = tokens.shape[0]
    f32 = jnp.float32
    moe = jnp.dot(
        combine[...],
        back[...].astype(f32),
        precision=lax.Precision.HIGHEST,
        preferred_element_type=f32,
    )
    for side in range(2):
        columns = slice(side * half, side * half + half)
        total = tokens[:, columns].astype(f32) + moe[side * count : side * count + count]
        out[:, columns] = total.astype(out.dtype)


def small(kernel, out_shape, *args, space=pltpu.VMEM, scratch=(), limit=16, name):
    vmem = pl.BlockSpec(memory_space=pltpu.VMEM)
    return pl.pallas_call(
        kernel,
        out_shape=out_shape,
        in_specs=[pl.BlockSpec(memory_space=space)] * len(args),
        out_specs=jax.tree.map(lambda _: vmem, out_shape),
        scratch_shapes=scratch,
        compiler_params=pltpu.CompilerParams(vmem_limit_bytes=limit << 20),
        name=name,
    )(*args)


def swap_experts(folded):
    blocks = folded.reshape(8, 8, folded.shape[1])
    blocks = lax.all_to_all(blocks, ("zl", "y"), split_axis=0, concat_axis=0, tiled=True)
    return blocks.reshape(folded.shape)


def per_device(tokens, norm_gain, routes, route_weights, w_gate, w_up, w_down):
    bf16 = jnp.bfloat16
    count, width = tokens.shape
    wg0, wu0, wd0 = w_gate[0], w_up[0], w_down[0]
    wg1, wu1, wd1 = (trade(w, "c") for w in (wg0, wu0, wd0))

    folded_shape = jax.ShapeDtypeStruct((64, width // 2), bf16)
    folded, combine = small(
        place_kernel,
        [folded_shape, jax.ShapeDtypeStruct((2 * count, 64), jnp.float32)],
        routes.T,
        route_weights.T,
        tokens,
        norm_gain.reshape(1, width),
        space=pltpu.HBM,
        scratch=[
            pltpu.SMEM((2, count), jnp.int32),
            pltpu.SMEM((2, count), jnp.float32),
            pltpu.VMEM((count, width), bf16),
            pltpu.VMEM((1, width), jnp.float32),
            pltpu.SemaphoreType.DMA((4,)),
        ],
        limit=60,
        name="place",
    )
    folded = swap_experts(folded)
    folded, wg1, wu1, wd1 = lax.optimization_barrier((folded, wg1, wu1, wd1))
    heads = [jax.ShapeDtypeStruct((UNIT, size), bf16) for _, size, _ in CHAINS]
    held = list(small(unfold_kernel, heads, folded, name="unfold"))

    last = None
    for step in range(4):
        came = [trade(h, order[step]) for h, (_, _, order) in zip(held, CHAINS)]
        if step == 3:
            break
        for j in (2, 3, 0, 1):
            if last is not None:
                came[j] = after(came[j], last)
            held[j] = last = jnp.concatenate([held[j], came[j]], axis=0)
    weights = (wg0, wu0, wg1, wu1)
    came[0] = after(came[0], last)
    came[1] = after(came[1], came[0])
    sums = hidden_units((held[0], came[0], held[1], came[1]), weights, (0, 1), None, False)
    came[2] = after(came[2], sums)
    came[3] = after(came[3], came[2])
    hidden = hidden_units((held[2], came[2], held[3], came[3]), weights, (2, 3), sums, True)

    held, away = [None] * 4, [None] * 4
    last = None
    for j in range(4):
        held[j], away[j] = expert_out(hidden if last is None else after(hidden, last), wd0, wd1, j)
        last = away[j]
    last = None
    for step in (3, 2, 1, 0):
        came = [trade(a, order[step]) for a, (_, _, order) in zip(away, CHAINS)]
        if not step:
            break
        half = held[0].shape[0] // 2
        for j in range(4):
            got = came[j] if last is None else after(came[j], last)
            away[j] = last = add(held[j][half:], got[half:])
            held[j] = add(held[j][:half], got[:half])

    folded = small(fold_kernel, folded_shape, *held, *came, name="fold")
    back = swap_experts(folded)
    out = jax.ShapeDtypeStruct(tokens.shape, bf16)
    return small(mix_kernel, out, tokens, combine, back, name="mix")


def solution(mesh):
    fine = Mesh(mesh.devices.reshape(4, 2, 4, 4, 2), AXES)
    rows = P(AXES, None)
    return jax.shard_map(
        per_device,
        mesh=fine,
        in_specs=(
            rows,
            P(),
            rows,
            rows,
            P(("zl", "y"), None, ("dp", "x", "c")),
            P(("zl", "y"), None, ("dp", "x", "c")),
            P(("zl", "y"), ("dp", "x", "c"), None),
        ),
        out_specs=rows,
        check_vma=False,
    )
```

```python
import functools

import jax
import jax.numpy as jnp
from jax import lax
from jax.experimental import pallas as pl
from jax.experimental.pallas import tpu as pltpu
from jax.sharding import Mesh
from jax.sharding import PartitionSpec as P

AXES = ("dp", "zl", "y", "x", "c")
STEPS = 6


DIMS = {"xa": ("x", 1), "xb": ("x", 3), "za": ("dp", 1), "zb": ("dp", 3), "c": ("c", 1)}
CHAINS = (
    (0, 2048, ("za", "zb", "xb", "xa")),
    (3072, 2048, ("zb", "za", "xa", "xb")),
    (2048, 1024, ("xa", "xb", "zb", "za")),
    (5120, 1024, ("xa", "xb", "za", "zb")),
)
JOINED = ((0,), (1,), (2, 3))
CANON = ("xa", "xb", "za", "zb")
UNIT = 32
HALF = 8 * UNIT


def canon_block(order, index):
    return sum(((index >> k) & 1) << CANON.index(d) for k, d in enumerate(order))


def trade(value, dim):
    axis, mask = DIMS[dim]
    n = lax.axis_size(axis)
    return lax.ppermute(value, axis, [(i, i ^ mask) for i in range(n)])


def add(a, b):
    return (a.astype(jnp.float32) + b.astype(jnp.float32)).astype(a.dtype)


def after(value, *others):
    return lax.optimization_barrier((value, *others))[0]


def hidden_kernel(chains, first, last, *refs):
    n = len(chains)
    ins = refs[: 2 * n]
    wg0, wu0, wg1, wu1 = refs[2 * n : 2 * n + 4]
    refs = refs[2 * n + 4 :]
    before = None if first else refs[0]
    refs = refs if first else refs[1:]
    total, part = refs[0], refs[1]
    acc = refs[2] if last else total
    step = pl.program_id(0)
    units = wg0.shape[1]
    f32 = jnp.float32
    at = 0
    for k, c in enumerate(chains):
        _, width, order = CHAINS[c]
        steps = width // PART

        @pl.when((step >= at) & (step < at + steps))
        def _(k=k, order=order):
            for index in range(16):
                to = canon_block(order, index) * UNIT
                row = (index % 8) * UNIT
                part[to : to + UNIT, :] = ins[2 * k + index // 8][row : row + UNIT, :]

        at += steps

    @pl.when(step == 0)
    def _():
        acc[...] = jnp.zeros_like(acc) if first else before[...]

    for i, w in enumerate((wg0, wu0, wg1, wu1)):
        acc[i] += jnp.dot(part[...], w[...], preferred_element_type=f32)

    if last:

        @pl.when(step == at - 1)
        def _():
            for i in range(2):
                gate = acc[2 * i]
                value = gate / (1.0 + jnp.exp(-gate)) * acc[2 * i + 1]
                total[:, i * units : (i + 1) * units] = value.astype(total.dtype)


def out_kernel(order, hidden, wd0, wd1, keep, away):
    units = wd0.shape[0]
    f32 = jnp.float32
    total = jnp.dot(hidden[:, :units], wd0[...], preferred_element_type=f32) + jnp.dot(
        hidden[:, units:], wd1[...], preferred_element_type=f32
    )
    total = total.astype(jnp.bfloat16)
    for index in range(16):
        row = canon_block(order, index) * UNIT
        to = (index % 8) * UNIT
        (keep, away)[index // 8][to : to + UNIT, :] = total[row : row + UNIT]


PART = 1024


def pick(table, i):
    value = table[0]
    for k, entry in enumerate(table[1:], 1):
        value = jnp.where(i >= k, entry, value)
    return value


def hidden_units(pieces, weights, chains, before, last):
    width, units = weights[0].shape
    count = 2 * HALF
    first = before is None
    in_specs, parts = [], []
    for c in chains:
        start, size, _ = CHAINS[c]
        low, steps = len(parts), size // PART
        to = lambda i, low=low, steps=steps: (0, jnp.clip(i - low, 0, steps - 1))
        in_specs += [pl.BlockSpec((HALF, PART), to)] * 2
        parts += [start // PART + k for k in range(steps)]
    whole = lambda *shape: pl.BlockSpec(shape, lambda i: (0,) * len(shape))
    in_specs += [pl.BlockSpec((PART, units), lambda i: (pick(parts, i), 0))] * 4
    sums = (4, count, units)
    if not first:
        in_specs.append(whole(*sums))
    scratch = [pltpu.VMEM((count, PART), jnp.bfloat16)]
    if last:
        out, out_spec = jax.ShapeDtypeStruct((count, 2 * units), jnp.bfloat16), whole(count, 2 * units)
        scratch.append(pltpu.VMEM(sums, jnp.float32))
    else:
        out, out_spec = jax.ShapeDtypeStruct(sums, jnp.float32), whole(*sums)
    depth = len(parts) * PART
    return pl.pallas_call(
        functools.partial(hidden_kernel, chains, first, last),
        grid=(len(parts),),
        out_shape=out,
        in_specs=in_specs,
        out_specs=out_spec,
        scratch_shapes=scratch,
        compiler_params=pltpu.CompilerParams(vmem_limit_bytes=32 << 20),
        cost_estimate=pl.CostEstimate(
            flops=8 * count * depth * units if last else 0,
            bytes_accessed=8 * depth * units + 2 * count * depth if last else 0,
            transcendentals=2 * count * units if last else 0,
        ),
        name="hidden",
    )(*pieces, *weights, *(() if first else (before,)))


def expert_out(hidden, wd0, wd1, chain):
    start, size, order = CHAINS[chain]
    units = wd0.shape[0]
    low, count = start // PART, 2 * HALF
    shape = jax.ShapeDtypeStruct((HALF, size), jnp.bfloat16)
    return pl.pallas_call(
        functools.partial(out_kernel, order),
        grid=(size // PART,),
        out_shape=[shape] * 2,
        in_specs=[pl.BlockSpec((count, 2 * units), lambda i: (0, 0))]
        + [pl.BlockSpec((units, PART), lambda i: (0, low + i))] * 2,
        out_specs=[pl.BlockSpec((HALF, PART), lambda i: (0, i))] * 2,
        compiler_params=pltpu.CompilerParams(vmem_limit_bytes=24 << 20),
        cost_estimate=pl.CostEstimate(
            flops=4 * count * size * units,
            bytes_accessed=4 * size * units + 2 * count * size,
            transcendentals=0,
        ),
        name="out",
    )(hidden, wd0, wd1)


def onehot(rows, columns, hit):
    row = lax.broadcasted_iota(jnp.int32, (rows, columns), 0)
    column = lax.broadcasted_iota(jnp.int32, (rows, columns), 1)
    return hit(row, column).astype(jnp.bfloat16)


def place_kernel(*refs):
    folded, combine = refs[4:6]
    routes, weights, tokens, gain = refs[6:10]
    copies = [pltpu.make_async_copy(refs[i], refs[6 + i], refs[10].at[i]) for i in range(4)]
    for copy in copies:
        copy.start()
    for copy in copies:
        copy.wait()
    f32 = jnp.float32
    count, width = tokens.shape
    half = width // 2
    wide = tokens[...].astype(f32)
    scale = lax.rsqrt(jnp.mean(wide * wide, axis=1, keepdims=True) + 1e-05)
    normed = (wide * scale * gain[...]).astype(jnp.bfloat16)
    rows = folded.shape[0]
    row = lax.broadcasted_iota(jnp.int32, (rows, 2 * count), 0)
    column = lax.broadcasted_iota(jnp.int32, (rows, 2 * count), 1)
    slot = lax.broadcasted_iota(jnp.int32, (2 * count, rows), 1)
    token = lax.broadcasted_iota(jnp.int32, (2 * count, rows), 0)
    picked = jnp.zeros((rows, 2 * count), f32)
    mixing = jnp.zeros((2 * count, rows), f32)
    flat = [routes[k, t] for t in range(count) for k in range(2)]
    for i, expert in enumerate(flat):
        rank = jnp.int32(0)
        for other in flat[:i]:
            rank += (other == expert).astype(jnp.int32)
        at = expert * 8 + rank
        weight = weights[i % 2, i // 2]
        for side in range(2):
            where = at + 4 * side
            of = i // 2 + count * side
            picked = jnp.where((row == where) & (column == of), 1.0, picked)
            mixing = jnp.where((slot == where) & (token == of), weight, mixing)
    picked = picked.astype(jnp.bfloat16)
    combine[...] = mixing
    both = jnp.concatenate([normed[:, :half], normed[:, half:]], axis=0)
    folded[...] = jnp.dot(picked, both, preferred_element_type=f32).astype(folded.dtype)


def unfold_kernel(folded, *outs):
    half = folded.shape[1]
    sides = []
    for side in range(2):
        take = onehot(UNIT, 2 * UNIT, lambda r, c: c == (r // 4) * 8 + r % 4 + 4 * side)
        rows = jnp.dot(take, folded[...], preferred_element_type=jnp.float32)
        sides.append(rows.astype(folded.dtype))
    for out, joined in zip(outs, JOINED):
        at = 0
        for c in joined:
            start, size, _ = CHAINS[c]
            low = start % half
            out[:, at : at + size] = sides[start // half][:, low : low + size]
            at += size


def fold_kernel(*refs):
    n = len(CHAINS)
    held, came, folded = refs[:n], refs[n : 2 * n], refs[2 * n]
    half = folded.shape[1]
    f32 = jnp.float32
    for c, (start, size, _) in enumerate(CHAINS):
        total = (held[c][...].astype(f32) + came[c][...].astype(f32)).astype(folded.dtype)
        side = start // half
        give = onehot(2 * UNIT, UNIT, lambda r, c: r == (c // 4) * 8 + c % 4 + 4 * side)
        rows = jnp.dot(give, total, preferred_element_type=f32).astype(folded.dtype)
        columns = slice(start - side * half, start - side * half + size)
        if side == 0:
            folded[:, columns] = rows
        else:
            folded[:, columns] = folded[:, columns] + rows


def mix_kernel(tokens, combine, back, out):
    half = back.shape[1]
    count = tokens.shape[0]
    f32 = jnp.float32
    moe = jnp.dot(
        combine[...],
        back[...].astype(f32),
        precision=lax.Precision.HIGHEST,
        preferred_element_type=f32,
    )
    for side in range(2):
        columns = slice(side * half, side * half + half)
        total = tokens[:, columns].astype(f32) + moe[side * count : side * count + count]
        out[:, columns] = total.astype(out.dtype)


def small(kernel, out_shape, *args, space=pltpu.VMEM, scratch=(), limit=16, name):
    vmem = pl.BlockSpec(memory_space=pltpu.VMEM)
    return pl.pallas_call(
        kernel,
        out_shape=out_shape,
        in_specs=[pl.BlockSpec(memory_space=space)] * len(args),
        out_specs=jax.tree.map(lambda _: vmem, out_shape),
        scratch_shapes=scratch,
        compiler_params=pltpu.CompilerParams(vmem_limit_bytes=limit << 20),
        name=name,
    )(*args)


def swap_experts(folded):
    blocks = folded.reshape(8, 8, folded.shape[1])
    blocks = lax.all_to_all(blocks, ("zl", "y"), split_axis=0, concat_axis=0, tiled=True)
    return blocks.reshape(folded.shape)


def per_device(tokens, norm_gain, routes, route_weights, w_gate, w_up, w_down):
    bf16 = jnp.bfloat16
    count, width = tokens.shape
    wg0, wu0, wd0 = w_gate[0], w_up[0], w_down[0]

    folded_shape = jax.ShapeDtypeStruct((64, width // 2), bf16)
    folded, combine = small(
        place_kernel,
        [folded_shape, jax.ShapeDtypeStruct((2 * count, 64), jnp.float32)],
        routes.T,
        route_weights.T,
        tokens,
        norm_gain.reshape(1, width),
        space=pltpu.HBM,
        scratch=[
            pltpu.SMEM((2, count), jnp.int32),
            pltpu.SMEM((2, count), jnp.float32),
            pltpu.VMEM((count, width), bf16),
            pltpu.VMEM((1, width), jnp.float32),
            pltpu.SemaphoreType.DMA((4,)),
        ],
        limit=60,
        name="place",
    )
    wg1, wu1, wd1 = (trade(after(w, folded), "c") for w in (wg0, wu0, wd0))
    folded = swap_experts(folded)
    folded, wg1, wu1 = lax.optimization_barrier((folded, wg1, wu1))
    heads = [
        jax.ShapeDtypeStruct((UNIT, sum(CHAINS[c][1] for c in joined)), bf16) for joined in JOINED
    ]
    held = list(small(unfold_kernel, heads, folded, name="unfold"))

    last = None
    for step in range(2):
        came = [trade(h, CHAINS[joined[0]][2][step]) for h, joined in zip(held, JOINED)]
        for k in (2, 0, 1):
            if last is not None:
                came[k] = after(came[k], last)
            if (step, k) == (0, 1):
                came[k], wd1 = lax.optimization_barrier((came[k], wd1))
            if (step, k) == (1, 2):
                size = CHAINS[2][1]
                both = [
                    jnp.concatenate([held[k][:, at], came[k][:, at]], axis=0)
                    for at in (slice(0, size), slice(size, 2 * size))
                ]
                last = both[1]
            else:
                held[k] = last = jnp.concatenate([held[k], came[k]], axis=0)
    held = held[:2] + both
    came = [trade(h, order[2]) for h, (_, _, order) in zip(held, CHAINS)]
    for j in (2, 3, 0, 1):
        came[j] = after(came[j], last)
        held[j] = last = jnp.concatenate([held[j], came[j]], axis=0)
    came = [trade(h, order[3]) for h, (_, _, order) in zip(held, CHAINS)]
    weights = (wg0, wu0, wg1, wu1)
    came[0] = after(came[0], last)
    came[1] = after(came[1], came[0])
    sums = hidden_units((held[0], came[0], held[1], came[1]), weights, (0, 1), None, False)
    came[2] = after(came[2], sums)
    came[3] = after(came[3], came[2])
    hidden = hidden_units((held[2], came[2], held[3], came[3]), weights, (2, 3), sums, True)

    held, away = [None] * 4, [None] * 4
    last = None
    for j in range(4):
        held[j], away[j] = expert_out(hidden if last is None else after(hidden, last), wd0, wd1, j)
        last = away[j]
    last = None
    for step in (3, 2):
        came = [trade(a, order[step]) for a, (_, _, order) in zip(away, CHAINS)]
        half = held[0].shape[0] // 2
        for j in range(4):
            got = came[j] if last is None else after(came[j], last)
            away[j] = last = add(held[j][half:], got[half:])
            held[j] = add(held[j][:half], got[:half])
    join = lambda values: values[:2] + [jnp.concatenate(values[2:], axis=1)]
    held, away = join(held), join(away)
    last = None
    came = [trade(a, CHAINS[joined[0]][2][1]) for a, joined in zip(away, JOINED)]
    half = held[0].shape[0] // 2
    for k in range(3):
        got = came[k] if last is None else after(came[k], last)
        away[k] = last = add(held[k][half:], got[half:])
        held[k] = add(held[k][:half], got[:half])
    size = CHAINS[2][1]
    part = lambda values: values[:2] + [values[2][:, :size], values[2][:, size:]]
    held, away = part(held), part(away)
    came = [trade(a, order[0]) for a, (_, _, order) in zip(away, CHAINS)]

    folded = small(fold_kernel, folded_shape, *held, *came, name="fold")
    back = swap_experts(folded)
    out = jax.ShapeDtypeStruct(tokens.shape, bf16)
    return small(mix_kernel, out, tokens, combine, back, name="mix")


def solution(mesh):
    fine = Mesh(mesh.devices.reshape(4, 2, 4, 4, 2), AXES)
    rows = P(AXES, None)
    return jax.shard_map(
        per_device,
        mesh=fine,
        in_specs=(
            rows,
            P(),
            rows,
            rows,
            P(("zl", "y"), None, ("dp", "x", "c")),
            P(("zl", "y"), None, ("dp", "x", "c")),
            P(("zl", "y"), ("dp", "x", "c"), None),
        ),
        out_specs=rows,
        check_vma=False,
    )
```

```python
import functools

import jax
import jax.numpy as jnp
from jax import lax
from jax.experimental import pallas as pl
from jax.experimental.pallas import tpu as pltpu
from jax.sharding import Mesh
from jax.sharding import PartitionSpec as P

AXES = ("dp", "zl", "y", "x", "c")
STEPS = 6


DIMS = {"xa": ("x", 1), "xb": ("x", 3), "za": ("dp", 1), "zb": ("dp", 3), "c": ("c", 1)}
CHAINS = (
    (0, 2048, ("za", "zb", "xb", "xa")),
    (3072, 2048, ("zb", "za", "xa", "xb")),
    (2048, 1024, ("xa", "xb", "zb", "za")),
    (5120, 1024, ("xa", "xb", "za", "zb")),
)
JOINED = ((0,), (1,), (2, 3))
CANON = ("xa", "xb", "za", "zb")
UNIT = 32
HALF = 8 * UNIT


def canon_block(order, index):
    return sum(((index >> k) & 1) << CANON.index(d) for k, d in enumerate(order))


def trade(value, dim):
    axis, mask = DIMS[dim]
    n = lax.axis_size(axis)
    return lax.ppermute(value, axis, [(i, i ^ mask) for i in range(n)])


def add(a, b):
    return (a.astype(jnp.float32) + b.astype(jnp.float32)).astype(a.dtype)


def after(value, *others):
    return lax.optimization_barrier((value, *others))[0]


def hidden_kernel(chains, first, last, *refs):
    n = len(chains)
    ins = refs[: 2 * n]
    wg0, wu0, wg1, wu1 = refs[2 * n : 2 * n + 4]
    refs = refs[2 * n + 4 :]
    before = None if first else refs[0]
    refs = refs if first else refs[1:]
    total, part = refs[0], refs[1]
    acc = refs[2] if last else total
    step = pl.program_id(0)
    units = wg0.shape[1]
    f32 = jnp.float32
    at = 0
    for k, c in enumerate(chains):
        _, width, order = CHAINS[c]
        steps = width // PART

        @pl.when((step >= at) & (step < at + steps))
        def _(k=k, order=order):
            for index in range(16):
                to = canon_block(order, index) * UNIT
                row = (index % 8) * UNIT
                part[to : to + UNIT, :] = ins[2 * k + index // 8][row : row + UNIT, :]

        at += steps

    @pl.when(step == 0)
    def _():
        acc[...] = jnp.zeros_like(acc) if first else before[...]

    for i, w in enumerate((wg0, wu0, wg1, wu1)):
        acc[i] += jnp.dot(part[...], w[...], preferred_element_type=f32)

    if last:

        @pl.when(step == at - 1)
        def _():
            for i in range(2):
                gate = acc[2 * i]
                value = gate / (1.0 + jnp.exp(-gate)) * acc[2 * i + 1]
                total[:, i * units : (i + 1) * units] = value.astype(total.dtype)


def out_kernel(order, sent, hidden, wd0, wd1, out):
    units = wd0.shape[0]
    f32 = jnp.float32
    blocks = [canon_block(order, index + 8 * sent) * UNIT for index in range(8)]
    rows = jnp.concatenate([hidden[row : row + UNIT, :] for row in blocks], axis=0)
    total = jnp.dot(rows[:, :units], wd0[...], preferred_element_type=f32) + jnp.dot(
        rows[:, units:], wd1[...], preferred_element_type=f32
    )
    out[...] = total.astype(out.dtype)


PART = 1024


def pick(table, i):
    value = table[0]
    for k, entry in enumerate(table[1:], 1):
        value = jnp.where(i >= k, entry, value)
    return value


def hidden_units(pieces, weights, chains, before, last):
    width, units = weights[0].shape
    count = 2 * HALF
    first = before is None
    in_specs, parts = [], []
    for c in chains:
        start, size, _ = CHAINS[c]
        low, steps = len(parts), size // PART
        to = lambda i, low=low, steps=steps: (0, jnp.clip(i - low, 0, steps - 1))
        in_specs += [pl.BlockSpec((HALF, PART), to)] * 2
        parts += [start // PART + k for k in range(steps)]
    whole = lambda *shape: pl.BlockSpec(shape, lambda i: (0,) * len(shape))
    in_specs += [pl.BlockSpec((PART, units), lambda i: (pick(parts, i), 0))] * 4
    sums = (4, count, units)
    if not first:
        in_specs.append(whole(*sums))
    scratch = [pltpu.VMEM((count, PART), jnp.bfloat16)]
    if last:
        out, out_spec = jax.ShapeDtypeStruct((count, 2 * units), jnp.bfloat16), whole(count, 2 * units)
        scratch.append(pltpu.VMEM(sums, jnp.float32))
    else:
        out, out_spec = jax.ShapeDtypeStruct(sums, jnp.float32), whole(*sums)
    depth = len(parts) * PART
    return pl.pallas_call(
        functools.partial(hidden_kernel, chains, first, last),
        grid=(len(parts),),
        out_shape=out,
        in_specs=in_specs,
        out_specs=out_spec,
        scratch_shapes=scratch,
        compiler_params=pltpu.CompilerParams(vmem_limit_bytes=32 << 20),
        cost_estimate=pl.CostEstimate(
            flops=8 * count * depth * units if last else 0,
            bytes_accessed=8 * depth * units + 2 * count * depth if last else 0,
            transcendentals=2 * count * units if last else 0,
        ),
        name="hidden",
    )(*pieces, *weights, *(() if first else (before,)))


def expert_out(hidden, wd0, wd1, chain, sent):
    start, size, order = CHAINS[chain]
    units = wd0.shape[0]
    low, count = start // PART, 2 * HALF
    return pl.pallas_call(
        functools.partial(out_kernel, order, int(sent)),
        grid=(size // PART,),
        out_shape=jax.ShapeDtypeStruct((HALF, size), jnp.bfloat16),
        in_specs=[pl.BlockSpec((count, 2 * units), lambda i: (0, 0))]
        + [pl.BlockSpec((units, PART), lambda i: (0, low + i))] * 2,
        out_specs=pl.BlockSpec((HALF, PART), lambda i: (0, i)),
        compiler_params=pltpu.CompilerParams(vmem_limit_bytes=24 << 20),
        cost_estimate=pl.CostEstimate(
            flops=2 * count * size * units,
            bytes_accessed=4 * size * units + count * size,
            transcendentals=0,
        ),
        name="out",
    )(hidden, wd0, wd1)


def onehot(rows, columns, hit):
    row = lax.broadcasted_iota(jnp.int32, (rows, columns), 0)
    column = lax.broadcasted_iota(jnp.int32, (rows, columns), 1)
    return hit(row, column).astype(jnp.bfloat16)


def place_kernel(*refs):
    folded, combine = refs[4:6]
    routes, weights, tokens, gain = refs[6:10]
    copies = [pltpu.make_async_copy(refs[i], refs[6 + i], refs[10].at[i]) for i in range(4)]
    for copy in copies:
        copy.start()
    for copy in copies:
        copy.wait()
    f32 = jnp.float32
    count, width = tokens.shape
    half = width // 2
    wide = tokens[...].astype(f32)
    scale = lax.rsqrt(jnp.mean(wide * wide, axis=1, keepdims=True) + 1e-05)
    normed = (wide * scale * gain[...]).astype(jnp.bfloat16)
    rows = folded.shape[0]
    row = lax.broadcasted_iota(jnp.int32, (rows, 2 * count), 0)
    column = lax.broadcasted_iota(jnp.int32, (rows, 2 * count), 1)
    slot = lax.broadcasted_iota(jnp.int32, (2 * count, rows), 1)
    token = lax.broadcasted_iota(jnp.int32, (2 * count, rows), 0)
    picked = jnp.zeros((rows, 2 * count), f32)
    mixing = jnp.zeros((2 * count, rows), f32)
    flat = [routes[k, t] for t in range(count) for k in range(2)]
    for i, expert in enumerate(flat):
        rank = jnp.int32(0)
        for other in flat[:i]:
            rank += (other == expert).astype(jnp.int32)
        at = expert * 8 + rank
        weight = weights[i % 2, i // 2]
        for side in range(2):
            where = at + 4 * side
            of = i // 2 + count * side
            picked = jnp.where((row == where) & (column == of), 1.0, picked)
            mixing = jnp.where((slot == where) & (token == of), weight, mixing)
    picked = picked.astype(jnp.bfloat16)
    combine[...] = mixing
    both = jnp.concatenate([normed[:, :half], normed[:, half:]], axis=0)
    folded[...] = jnp.dot(picked, both, preferred_element_type=f32).astype(folded.dtype)


def unfold_kernel(folded, *outs):
    half = folded.shape[1]
    sides = []
    for side in range(2):
        take = onehot(UNIT, 2 * UNIT, lambda r, c: c == (r // 4) * 8 + r % 4 + 4 * side)
        rows = jnp.dot(take, folded[...], preferred_element_type=jnp.float32)
        sides.append(rows.astype(folded.dtype))
    for out, joined in zip(outs, JOINED):
        at = 0
        for c in joined:
            start, size, _ = CHAINS[c]
            low = start % half
            out[:, at : at + size] = sides[start // half][:, low : low + size]
            at += size


def fold_kernel(*refs):
    n = len(CHAINS)
    held, came, folded = refs[:n], refs[n : 2 * n], refs[2 * n]
    half = folded.shape[1]
    f32 = jnp.float32
    for c, (start, size, _) in enumerate(CHAINS):
        total = (held[c][...].astype(f32) + came[c][...].astype(f32)).astype(folded.dtype)
        side = start // half
        give = onehot(2 * UNIT, UNIT, lambda r, c: r == (c // 4) * 8 + c % 4 + 4 * side)
        rows = jnp.dot(give, total, preferred_element_type=f32).astype(folded.dtype)
        columns = slice(start - side * half, start - side * half + size)
        if side == 0:
            folded[:, columns] = rows
        else:
            folded[:, columns] = folded[:, columns] + rows


def mix_kernel(tokens, combine, back, out):
    half = back.shape[1]
    count = tokens.shape[0]
    f32 = jnp.float32
    moe = jnp.dot(
        combine[...],
        back[...].astype(f32),
        precision=lax.Precision.HIGHEST,
        preferred_element_type=f32,
    )
    for side in range(2):
        columns = slice(side * half, side * half + half)
        total = tokens[:, columns].astype(f32) + moe[side * count : side * count + count]
        out[:, columns] = total.astype(out.dtype)


def small(kernel, out_shape, *args, space=pltpu.VMEM, scratch=(), limit=16, name):
    vmem = pl.BlockSpec(memory_space=pltpu.VMEM)
    return pl.pallas_call(
        kernel,
        out_shape=out_shape,
        in_specs=[pl.BlockSpec(memory_space=space)] * len(args),
        out_specs=jax.tree.map(lambda _: vmem, out_shape),
        scratch_shapes=scratch,
        compiler_params=pltpu.CompilerParams(vmem_limit_bytes=limit << 20),
        name=name,
    )(*args)


def swap_experts(folded):
    blocks = folded.reshape(8, 8, folded.shape[1])
    blocks = lax.all_to_all(blocks, ("zl", "y"), split_axis=0, concat_axis=0, tiled=True)
    return blocks.reshape(folded.shape)


def per_device(tokens, norm_gain, routes, route_weights, w_gate, w_up, w_down):
    bf16 = jnp.bfloat16
    count, width = tokens.shape
    wg0, wu0, wd0 = w_gate[0], w_up[0], w_down[0]

    folded_shape = jax.ShapeDtypeStruct((64, width // 2), bf16)
    folded, combine = small(
        place_kernel,
        [folded_shape, jax.ShapeDtypeStruct((2 * count, 64), jnp.float32)],
        routes.T,
        route_weights.T,
        tokens,
        norm_gain.reshape(1, width),
        space=pltpu.HBM,
        scratch=[
            pltpu.SMEM((2, count), jnp.int32),
            pltpu.SMEM((2, count), jnp.float32),
            pltpu.VMEM((count, width), bf16),
            pltpu.VMEM((1, width), jnp.float32),
            pltpu.SemaphoreType.DMA((4,)),
        ],
        limit=60,
        name="place",
    )
    wg1, wu1, wd1 = (trade(after(w, folded), "c") for w in (wg0, wu0, wd0))
    folded = swap_experts(folded)
    folded, wg1, wu1 = lax.optimization_barrier((folded, wg1, wu1))
    heads = [
        jax.ShapeDtypeStruct((UNIT, sum(CHAINS[c][1] for c in joined)), bf16) for joined in JOINED
    ]
    held = list(small(unfold_kernel, heads, folded, name="unfold"))

    last = None
    for step in range(2):
        came = [trade(h, CHAINS[joined[0]][2][step]) for h, joined in zip(held, JOINED)]
        for k in (2, 0, 1):
            if last is not None:
                came[k] = after(came[k], *(last if isinstance(last, list) else (last,)))
            if (step, k) == (0, 1):
                came[k], wd1 = lax.optimization_barrier((came[k], wd1))
            if (step, k) == (1, 2):
                size = CHAINS[2][1]
                both = [
                    jnp.concatenate([held[k][:, at], came[k][:, at]], axis=0)
                    for at in (slice(0, size), slice(size, 2 * size))
                ]
                last = both
            else:
                held[k] = last = jnp.concatenate([held[k], came[k]], axis=0)
    held = held[:2] + both
    came = [trade(h, order[2]) for h, (_, _, order) in zip(held, CHAINS)]
    for j in (2, 3, 0, 1):
        came[j] = after(came[j], last)
        held[j] = last = jnp.concatenate([held[j], came[j]], axis=0)
    came = [trade(h, order[3]) for h, (_, _, order) in zip(held, CHAINS)]
    weights = (wg0, wu0, wg1, wu1)
    came[0] = after(came[0], last)
    came[1] = after(came[1], came[0])
    sums = hidden_units((held[0], came[0], held[1], came[1]), weights, (0, 1), None, False)
    came[2] = after(came[2], sums)
    came[3] = after(came[3], came[2])
    hidden = hidden_units((held[2], came[2], held[3], came[3]), weights, (2, 3), sums, True)

    held, away = [], []
    for j in range(4):
        given = after(hidden, away[-1]) if away else hidden
        away.append(expert_out(given, wd0, wd1, j, True))
    for j in range(4):
        given = after(hidden, away[-1], *held[-1:])
        held.append(expert_out(given, wd0, wd1, j, False))
    last = None
    for step in (3, 2):
        came = [trade(a, order[step]) for a, (_, _, order) in zip(away, CHAINS)]
        half = held[0].shape[0] // 2
        for j in range(4):
            got = came[j] if last is None else after(came[j], last)
            away[j] = last = add(held[j][half:], got[half:])
            held[j] = add(held[j][:half], got[:half])
    join = lambda values: values[:2] + [jnp.concatenate(values[2:], axis=1)]
    held, away = join(held), join(away)
    last = None
    came = [trade(a, CHAINS[joined[0]][2][1]) for a, joined in zip(away, JOINED)]
    half = held[0].shape[0] // 2
    for k in range(3):
        got = came[k] if last is None else after(came[k], last)
        away[k] = last = add(held[k][half:], got[half:])
        held[k] = add(held[k][:half], got[:half])
    size = CHAINS[2][1]
    part = lambda values: values[:2] + [values[2][:, :size], values[2][:, size:]]
    held, away = part(held), part(away)
    came = [trade(a, order[0]) for a, (_, _, order) in zip(away, CHAINS)]

    folded = small(fold_kernel, folded_shape, *held, *came, name="fold")
    back = swap_experts(folded)
    out = jax.ShapeDtypeStruct(tokens.shape, bf16)
    return small(mix_kernel, out, tokens, combine, back, name="mix")


def solution(mesh):
    fine = Mesh(mesh.devices.reshape(4, 2, 4, 4, 2), AXES)
    rows = P(AXES, None)
    return jax.shard_map(
        per_device,
        mesh=fine,
        in_specs=(
            rows,
            P(),
            rows,
            rows,
            P(("zl", "y"), None, ("dp", "x", "c")),
            P(("zl", "y"), None, ("dp", "x", "c")),
            P(("zl", "y"), ("dp", "x", "c"), None),
        ),
        out_specs=rows,
        check_vma=False,
    )
```

```python
import functools

import jax
import jax.numpy as jnp
from jax import lax
from jax.experimental import pallas as pl
from jax.experimental.pallas import tpu as pltpu
from jax.sharding import Mesh
from jax.sharding import PartitionSpec as P

AXES = ("dp", "zl", "y", "x", "c")
STEPS = 6


DIMS = {"xa": ("x", 1), "xb": ("x", 3), "za": ("dp", 1), "zb": ("dp", 3), "c": ("c", 1)}
CHAINS = (
    (0, 2048, ("za", "zb", "xb", "xa")),
    (3072, 2048, ("zb", "za", "xa", "xb")),
    (2048, 1024, ("xa", "xb", "zb", "za")),
    (5120, 1024, ("xa", "xb", "za", "zb")),
)
JOINED = ((0,), (1,), (2, 3))
CANON = ("xa", "xb", "za", "zb")
UNIT = 32
HALF = 8 * UNIT


def canon_block(order, index):
    return sum(((index >> k) & 1) << CANON.index(d) for k, d in enumerate(order))


def trade(value, dim):
    axis, mask = DIMS[dim]
    n = lax.axis_size(axis)
    return lax.ppermute(value, axis, [(i, i ^ mask) for i in range(n)])


def add(a, b):
    return (a.astype(jnp.float32) + b.astype(jnp.float32)).astype(a.dtype)


def after(value, *others):
    return lax.optimization_barrier((value, *others))[0]


def hidden_kernel(pieces, first, last, *refs):
    n = len(pieces)
    ins = refs[:n]
    wg0, wu0, wg1, wu1 = refs[n : n + 4]
    refs = refs[n + 4 :]
    before = None if first else refs[0]
    refs = refs if first else refs[1:]
    total = refs[0]
    acc = refs[1] if last else total
    step = pl.program_id(0)
    units = wg0.shape[1]
    f32 = jnp.float32

    @pl.when(step == 0)
    def _():
        acc[...] = jnp.zeros_like(acc) if first else before[...]

    at = 0
    for k, (c, came) in enumerate(pieces):
        _, width, order = CHAINS[c]
        steps = width // PART

        @pl.when((step >= at) & (step < at + steps))
        def _(k=k, order=order, came=came):
            for i, w in enumerate((wg0, wu0, wg1, wu1)):
                product = jnp.dot(ins[k][...], w[...], preferred_element_type=f32)
                for index in range(8):
                    to = canon_block(order, index + 8 * came) * UNIT
                    acc[i, to : to + UNIT, :] += product[index * UNIT : (index + 1) * UNIT]

        at += steps

    if last:

        @pl.when(step == at - 1)
        def _():
            for i in range(2):
                gate = acc[2 * i]
                value = gate / (1.0 + jnp.exp(-gate)) * acc[2 * i + 1]
                total[:, i * units : (i + 1) * units] = value.astype(total.dtype)


def out_kernel(order, sent, hidden, wd0, wd1, out):
    units = wd0.shape[0]
    f32 = jnp.float32
    blocks = [canon_block(order, index + 8 * sent) * UNIT for index in range(8)]
    rows = jnp.concatenate([hidden[row : row + UNIT, :] for row in blocks], axis=0)
    total = jnp.dot(rows[:, :units], wd0[...], preferred_element_type=f32) + jnp.dot(
        rows[:, units:], wd1[...], preferred_element_type=f32
    )
    out[...] = total.astype(out.dtype)


PART = 1024


def pick(table, i):
    value = table[0]
    for k, entry in enumerate(table[1:], 1):
        value = jnp.where(i >= k, entry, value)
    return value


def hidden_units(pieces, weights, before, last):
    width, units = weights[0].shape
    count = 2 * HALF
    first = before is None
    in_specs, parts = [], []
    for c, _ in pieces:
        start, size, _ = CHAINS[c]
        low, steps = len(parts), size // PART
        to = lambda i, low=low, steps=steps: (0, jnp.clip(i - low, 0, steps - 1))
        in_specs.append(pl.BlockSpec((HALF, PART), to))
        parts += [start // PART + k for k in range(steps)]
    whole = lambda *shape: pl.BlockSpec(shape, lambda i: (0,) * len(shape))
    in_specs += [pl.BlockSpec((PART, units), lambda i: (pick(parts, i), 0))] * 4
    sums = (4, count, units)
    if not first:
        in_specs.append(whole(*sums))
    if last:
        out, out_spec = jax.ShapeDtypeStruct((count, 2 * units), jnp.bfloat16), whole(count, 2 * units)
        scratch = [pltpu.VMEM(sums, jnp.float32)]
    else:
        out, out_spec, scratch = jax.ShapeDtypeStruct(sums, jnp.float32), whole(*sums), []
    depth = len(parts) * PART
    return pl.pallas_call(
        functools.partial(hidden_kernel, tuple(pieces), first, last),
        grid=(len(parts),),
        out_shape=out,
        in_specs=in_specs,
        out_specs=out_spec,
        scratch_shapes=scratch,
        compiler_params=pltpu.CompilerParams(vmem_limit_bytes=32 << 20),
        cost_estimate=pl.CostEstimate(
            flops=8 * HALF * depth * units if last else 0,
            bytes_accessed=8 * depth * units + 2 * HALF * depth if last else 0,
            transcendentals=2 * count * units if last else 0,
        ),
        name="hidden",
    )(*pieces.values(), *weights, *(() if first else (before,)))


def expert_out(hidden, wd0, wd1, chain, sent):
    start, size, order = CHAINS[chain]
    units = wd0.shape[0]
    low, count = start // PART, 2 * HALF
    return pl.pallas_call(
        functools.partial(out_kernel, order, int(sent)),
        grid=(size // PART,),
        out_shape=jax.ShapeDtypeStruct((HALF, size), jnp.bfloat16),
        in_specs=[pl.BlockSpec((count, 2 * units), lambda i: (0, 0))]
        + [pl.BlockSpec((units, PART), lambda i: (0, low + i))] * 2,
        out_specs=pl.BlockSpec((HALF, PART), lambda i: (0, i)),
        compiler_params=pltpu.CompilerParams(vmem_limit_bytes=24 << 20),
        cost_estimate=pl.CostEstimate(
            flops=2 * count * size * units,
            bytes_accessed=4 * size * units + count * size,
            transcendentals=0,
        ),
        name="out",
    )(hidden, wd0, wd1)


def onehot(rows, columns, hit):
    row = lax.broadcasted_iota(jnp.int32, (rows, columns), 0)
    column = lax.broadcasted_iota(jnp.int32, (rows, columns), 1)
    return hit(row, column).astype(jnp.bfloat16)


def place_kernel(*refs):
    folded, combine = refs[4:6]
    routes, weights, tokens, gain = refs[6:10]
    copies = [pltpu.make_async_copy(refs[i], refs[6 + i], refs[10].at[i]) for i in range(4)]
    for copy in copies:
        copy.start()
    for copy in copies:
        copy.wait()
    f32 = jnp.float32
    count, width = tokens.shape
    half = width // 2
    wide = tokens[...].astype(f32)
    scale = lax.rsqrt(jnp.mean(wide * wide, axis=1, keepdims=True) + 1e-05)
    normed = (wide * scale * gain[...]).astype(jnp.bfloat16)
    rows = folded.shape[0]
    row = lax.broadcasted_iota(jnp.int32, (rows, 2 * count), 0)
    column = lax.broadcasted_iota(jnp.int32, (rows, 2 * count), 1)
    slot = lax.broadcasted_iota(jnp.int32, (2 * count, rows), 1)
    token = lax.broadcasted_iota(jnp.int32, (2 * count, rows), 0)
    picked = jnp.zeros((rows, 2 * count), f32)
    mixing = jnp.zeros((2 * count, rows), f32)
    flat = [routes[k, t] for t in range(count) for k in range(2)]
    for i, expert in enumerate(flat):
        rank = jnp.int32(0)
        for other in flat[:i]:
            rank += (other == expert).astype(jnp.int32)
        at = expert * 8 + rank
        weight = weights[i % 2, i // 2]
        for side in range(2):
            where = at + 4 * side
            of = i // 2 + count * side
            picked = jnp.where((row == where) & (column == of), 1.0, picked)
            mixing = jnp.where((slot == where) & (token == of), weight, mixing)
    picked = picked.astype(jnp.bfloat16)
    combine[...] = mixing
    both = jnp.concatenate([normed[:, :half], normed[:, half:]], axis=0)
    folded[...] = jnp.dot(picked, both, preferred_element_type=f32).astype(folded.dtype)


def unfold_kernel(folded, *outs):
    half = folded.shape[1]
    sides = []
    for side in range(2):
        take = onehot(UNIT, 2 * UNIT, lambda r, c: c == (r // 4) * 8 + r % 4 + 4 * side)
        rows = jnp.dot(take, folded[...], preferred_element_type=jnp.float32)
        sides.append(rows.astype(folded.dtype))
    for out, joined in zip(outs, JOINED):
        at = 0
        for c in joined:
            start, size, _ = CHAINS[c]
            low = start % half
            out[:, at : at + size] = sides[start // half][:, low : low + size]
            at += size


def fold_kernel(*refs):
    n = len(CHAINS)
    held, came, folded = refs[:n], refs[n : 2 * n], refs[2 * n]
    half = folded.shape[1]
    f32 = jnp.float32
    for c, (start, size, _) in enumerate(CHAINS):
        total = (held[c][...].astype(f32) + came[c][...].astype(f32)).astype(folded.dtype)
        side = start // half
        give = onehot(2 * UNIT, UNIT, lambda r, c: r == (c // 4) * 8 + c % 4 + 4 * side)
        rows = jnp.dot(give, total, preferred_element_type=f32).astype(folded.dtype)
        columns = slice(start - side * half, start - side * half + size)
        if side == 0:
            folded[:, columns] = rows
        else:
            folded[:, columns] = folded[:, columns] + rows


def mix_kernel(tokens, combine, back, out):
    half = back.shape[1]
    count = tokens.shape[0]
    f32 = jnp.float32
    moe = jnp.dot(
        combine[...],
        back[...].astype(f32),
        precision=lax.Precision.HIGHEST,
        preferred_element_type=f32,
    )
    for side in range(2):
        columns = slice(side * half, side * half + half)
        total = tokens[:, columns].astype(f32) + moe[side * count : side * count + count]
        out[:, columns] = total.astype(out.dtype)


def small(kernel, out_shape, *args, space=pltpu.VMEM, scratch=(), limit=16, name):
    vmem = pl.BlockSpec(memory_space=pltpu.VMEM)
    return pl.pallas_call(
        kernel,
        out_shape=out_shape,
        in_specs=[pl.BlockSpec(memory_space=space)] * len(args),
        out_specs=jax.tree.map(lambda _: vmem, out_shape),
        scratch_shapes=scratch,
        compiler_params=pltpu.CompilerParams(vmem_limit_bytes=limit << 20),
        name=name,
    )(*args)


def swap_experts(folded):
    blocks = folded.reshape(8, 8, folded.shape[1])
    blocks = lax.all_to_all(blocks, ("zl", "y"), split_axis=0, concat_axis=0, tiled=True)
    return blocks.reshape(folded.shape)


def per_device(tokens, norm_gain, routes, route_weights, w_gate, w_up, w_down):
    bf16 = jnp.bfloat16
    count, width = tokens.shape
    wg0, wu0, wd0 = w_gate[0], w_up[0], w_down[0]

    folded_shape = jax.ShapeDtypeStruct((64, width // 2), bf16)
    folded, combine = small(
        place_kernel,
        [folded_shape, jax.ShapeDtypeStruct((2 * count, 64), jnp.float32)],
        routes.T,
        route_weights.T,
        tokens,
        norm_gain.reshape(1, width),
        space=pltpu.HBM,
        scratch=[
            pltpu.SMEM((2, count), jnp.int32),
            pltpu.SMEM((2, count), jnp.float32),
            pltpu.VMEM((count, width), bf16),
            pltpu.VMEM((1, width), jnp.float32),
            pltpu.SemaphoreType.DMA((4,)),
        ],
        limit=60,
        name="place",
    )
    wg1, wu1, wd1 = (trade(after(w, folded), "c") for w in (wg0, wu0, wd0))
    folded = swap_experts(folded)
    folded, wg1, wu1 = lax.optimization_barrier((folded, wg1, wu1))
    heads = [
        jax.ShapeDtypeStruct((UNIT, sum(CHAINS[c][1] for c in joined)), bf16) for joined in JOINED
    ]
    held = list(small(unfold_kernel, heads, folded, name="unfold"))

    last = None
    for step in range(2):
        came = [trade(h, CHAINS[joined[0]][2][step]) for h, joined in zip(held, JOINED)]
        for k in (2, 0, 1):
            if last is not None:
                came[k] = after(came[k], *(last if isinstance(last, list) else (last,)))
            if (step, k) == (0, 1):
                came[k], wd1 = lax.optimization_barrier((came[k], wd1))
            if (step, k) == (1, 2):
                size = CHAINS[2][1]
                both = [
                    jnp.concatenate([held[k][:, at], came[k][:, at]], axis=0)
                    for at in (slice(0, size), slice(size, 2 * size))
                ]
                last = both
            else:
                held[k] = last = jnp.concatenate([held[k], came[k]], axis=0)
    held = held[:2] + both
    came = [trade(h, order[2]) for h, (_, _, order) in zip(held, CHAINS)]
    for j in (2, 3, 0, 1):
        came[j] = after(came[j], last)
        held[j] = last = jnp.concatenate([held[j], came[j]], axis=0)
    came = [trade(h, order[3]) for h, (_, _, order) in zip(held, CHAINS)]
    weights = (wg0, wu0, wg1, wu1)
    sums = hidden_units({(j, False): held[j] for j in range(4)}, weights, None, False)
    came[0] = after(came[0], last, sums)
    came[1] = after(came[1], came[0])
    sums = hidden_units({(j, True): came[j] for j in (0, 1)}, weights, sums, False)
    came[2] = after(came[2], sums)
    came[3] = after(came[3], came[2])
    hidden = hidden_units({(j, True): came[j] for j in (2, 3)}, weights, sums, True)

    held, away = [], []
    for j in range(4):
        given = after(hidden, away[-1]) if away else hidden
        away.append(expert_out(given, wd0, wd1, j, True))
    for j in range(4):
        given = after(hidden, away[-1], *held[-1:])
        held.append(expert_out(given, wd0, wd1, j, False))
    last = None
    for step in (3, 2):
        came = [trade(a, order[step]) for a, (_, _, order) in zip(away, CHAINS)]
        half = held[0].shape[0] // 2
        for j in range(4):
            got = came[j] if last is None else after(came[j], last)
            away[j] = last = add(held[j][half:], got[half:])
            held[j] = add(held[j][:half], got[:half])
    join = lambda values: values[:2] + [jnp.concatenate(values[2:], axis=1)]
    held, away = join(held), join(away)
    last = None
    came = [trade(a, CHAINS[joined[0]][2][1]) for a, joined in zip(away, JOINED)]
    half = held[0].shape[0] // 2
    for k in range(3):
        got = came[k] if last is None else after(came[k], last)
        away[k] = last = add(held[k][half:], got[half:])
        held[k] = add(held[k][:half], got[:half])
    size = CHAINS[2][1]
    part = lambda values: values[:2] + [values[2][:, :size], values[2][:, size:]]
    held, away = part(held), part(away)
    came = [trade(a, order[0]) for a, (_, _, order) in zip(away, CHAINS)]

    folded = small(fold_kernel, folded_shape, *held, *came, name="fold")
    back = swap_experts(folded)
    out = jax.ShapeDtypeStruct(tokens.shape, bf16)
    return small(mix_kernel, out, tokens, combine, back, name="mix")


def solution(mesh):
    fine = Mesh(mesh.devices.reshape(4, 2, 4, 4, 2), AXES)
    rows = P(AXES, None)
    return jax.shard_map(
        per_device,
        mesh=fine,
        in_specs=(
            rows,
            P(),
            rows,
            rows,
            P(("zl", "y"), None, ("dp", "x", "c")),
            P(("zl", "y"), None, ("dp", "x", "c")),
            P(("zl", "y"), ("dp", "x", "c"), None),
        ),
        out_specs=rows,
        check_vma=False,
    )
```

```python
import functools

import jax
import jax.numpy as jnp
from jax import lax
from jax.experimental import pallas as pl
from jax.experimental.pallas import tpu as pltpu
from jax.sharding import Mesh
from jax.sharding import PartitionSpec as P

AXES = ("dp", "zl", "y", "x", "c")
STEPS = 6


DIMS = {"xa": ("x", 1), "xb": ("x", 3), "za": ("dp", 1), "zb": ("dp", 3), "c": ("c", 1)}
CHAINS = (
    (0, 1792, ("za", "zb", "xb", "xa")),
    (3072, 1792, ("zb", "za", "xa", "xb")),
    (1792, 1280, ("xa", "xb", "zb", "za")),
    (4864, 1280, ("xa", "xb", "za", "zb")),
)
OUT_CHAINS = tuple(
    (start, size, order)
    for (start, size), (_, _, order) in zip(
        ((0, 2048), (3072, 2048), (2048, 1024), (5120, 1024)), CHAINS
    )
)
DEPTHS = (896, 896, 1280, 1280)
JOINED = ((0,), (1,), (2, 3))
CANON = ("xa", "xb", "za", "zb")
UNIT = 32
HALF = 8 * UNIT


def canon_block(order, index):
    return sum(((index >> k) & 1) << CANON.index(d) for k, d in enumerate(order))


def trade(value, dim):
    axis, mask = DIMS[dim]
    n = lax.axis_size(axis)
    return lax.ppermute(value, axis, [(i, i ^ mask) for i in range(n)])


def add(a, b):
    return (a.astype(jnp.float32) + b.astype(jnp.float32)).astype(a.dtype)


def after(value, *others):
    return lax.optimization_barrier((value, *others))[0]


def depths_of(pieces):
    return sorted({DEPTHS[c] for c, _ in pieces})


def hidden_kernel(pieces, first, last, *refs):
    n = len(pieces)
    ins = refs[:n]
    depths = depths_of(pieces)
    weights = [refs[n + 4 * k : n + 4 * k + 4] for k in range(len(depths))]
    refs = refs[n + 4 * len(depths) :]
    before = None if first else refs[0]
    refs = refs if first else refs[1:]
    total = refs[0]
    acc = refs[1] if last else total
    step = pl.program_id(0)
    units = weights[0][0].shape[1]
    f32 = jnp.float32

    @pl.when(step == 0)
    def _():
        acc[...] = jnp.zeros_like(acc) if first else before[...]

    at = 0
    for k, (c, came) in enumerate(pieces):
        _, width, order = CHAINS[c]
        steps = width // DEPTHS[c]

        @pl.when((step >= at) & (step < at + steps))
        def _(k=k, order=order, came=came, ws=weights[depths.index(DEPTHS[c])]):
            for i, w in enumerate(ws):
                product = jnp.dot(ins[k][...], w[...], preferred_element_type=f32)
                for index in range(8):
                    to = canon_block(order, index + 8 * came) * UNIT
                    acc[i, to : to + UNIT, :] += product[index * UNIT : (index + 1) * UNIT]

        at += steps

    if last:

        @pl.when(step == at - 1)
        def _():
            for i in range(2):
                gate = acc[2 * i]
                value = gate / (1.0 + jnp.exp(-gate)) * acc[2 * i + 1]
                total[:, i * units : (i + 1) * units] = value.astype(total.dtype)


def out_kernel(order, sent, hidden, wd0, wd1, out):
    units = wd0.shape[0]
    f32 = jnp.float32
    blocks = [canon_block(order, index + 8 * sent) * UNIT for index in range(8)]
    rows = jnp.concatenate([hidden[row : row + UNIT, :] for row in blocks], axis=0)
    total = jnp.dot(rows[:, :units], wd0[...], preferred_element_type=f32) + jnp.dot(
        rows[:, units:], wd1[...], preferred_element_type=f32
    )
    out[...] = total.astype(out.dtype)


PART = 1024


def pick(table, i):
    value = table[0][1]
    for step, entry in table[1:]:
        value = jnp.where(i >= step, entry, value)
    return value


def hidden_units(pieces, weights, before, last):
    width, units = weights[0].shape
    count = 2 * HALF
    first = before is None
    in_specs, tables, steps = [], {}, 0
    for c, _ in pieces:
        start, size, _ = CHAINS[c]
        depth = DEPTHS[c]
        more = size // depth
        to = lambda i, low=steps, more=more: (0, jnp.clip(i - low, 0, more - 1))
        in_specs.append(pl.BlockSpec((HALF, depth), to))
        tables.setdefault(depth, []).extend(
            (steps + k, start + k * depth) for k in range(more)
        )
        steps += more
    whole = lambda *shape: pl.BlockSpec(shape, lambda i: (0,) * len(shape))
    for depth in depths_of(pieces):
        at = lambda i, table=tables[depth]: (pl.multiple_of(pick(table, i), 128), 0)
        in_specs += [pl.BlockSpec((pl.Element(depth), pl.Element(units)), at)] * 4
    sums = (4, count, units)
    if not first:
        in_specs.append(whole(*sums))
    if last:
        out, out_spec = jax.ShapeDtypeStruct((count, 2 * units), jnp.bfloat16), whole(count, 2 * units)
        scratch = [pltpu.VMEM(sums, jnp.float32)]
    else:
        out, out_spec, scratch = jax.ShapeDtypeStruct(sums, jnp.float32), whole(*sums), []
    depth = sum(CHAINS[c][1] for c, _ in pieces)
    return pl.pallas_call(
        functools.partial(hidden_kernel, tuple(pieces), first, last),
        grid=(steps,),
        out_shape=out,
        in_specs=in_specs,
        out_specs=out_spec,
        scratch_shapes=scratch,
        compiler_params=pltpu.CompilerParams(vmem_limit_bytes=32 << 20),
        cost_estimate=pl.CostEstimate(
            flops=8 * HALF * depth * units if last else 0,
            bytes_accessed=8 * depth * units + 2 * HALF * depth if last else 0,
            transcendentals=2 * count * units if last else 0,
        ),
        name="hidden",
    )(*pieces.values(), *weights * len(tables), *(() if first else (before,)))


def expert_out(hidden, wd0, wd1, chain, sent):
    start, size, order = OUT_CHAINS[chain]
    units = wd0.shape[0]
    low, count = start // PART, 2 * HALF
    return pl.pallas_call(
        functools.partial(out_kernel, order, int(sent)),
        grid=(size // PART,),
        out_shape=jax.ShapeDtypeStruct((HALF, size), jnp.bfloat16),
        in_specs=[pl.BlockSpec((count, 2 * units), lambda i: (0, 0))]
        + [pl.BlockSpec((units, PART), lambda i: (0, low + i))] * 2,
        out_specs=pl.BlockSpec((HALF, PART), lambda i: (0, i)),
        compiler_params=pltpu.CompilerParams(vmem_limit_bytes=24 << 20),
        cost_estimate=pl.CostEstimate(
            flops=2 * count * size * units,
            bytes_accessed=4 * size * units + count * size,
            transcendentals=0,
        ),
        name="out",
    )(hidden, wd0, wd1)


def onehot(rows, columns, hit):
    row = lax.broadcasted_iota(jnp.int32, (rows, columns), 0)
    column = lax.broadcasted_iota(jnp.int32, (rows, columns), 1)
    return hit(row, column).astype(jnp.bfloat16)


def place_kernel(*refs):
    folded, combine = refs[4:6]
    routes, weights, tokens, gain = refs[6:10]
    copies = [pltpu.make_async_copy(refs[i], refs[6 + i], refs[10].at[i]) for i in range(4)]
    for copy in copies:
        copy.start()
    for copy in copies:
        copy.wait()
    f32 = jnp.float32
    count, width = tokens.shape
    half = width // 2
    wide = tokens[...].astype(f32)
    scale = lax.rsqrt(jnp.mean(wide * wide, axis=1, keepdims=True) + 1e-05)
    normed = (wide * scale * gain[...]).astype(jnp.bfloat16)
    rows = folded.shape[0]
    row = lax.broadcasted_iota(jnp.int32, (rows, 2 * count), 0)
    column = lax.broadcasted_iota(jnp.int32, (rows, 2 * count), 1)
    slot = lax.broadcasted_iota(jnp.int32, (2 * count, rows), 1)
    token = lax.broadcasted_iota(jnp.int32, (2 * count, rows), 0)
    picked = jnp.zeros((rows, 2 * count), f32)
    mixing = jnp.zeros((2 * count, rows), f32)
    flat = [routes[k, t] for t in range(count) for k in range(2)]
    for i, expert in enumerate(flat):
        rank = jnp.int32(0)
        for other in flat[:i]:
            rank += (other == expert).astype(jnp.int32)
        at = expert * 8 + rank
        weight = weights[i % 2, i // 2]
        for side in range(2):
            where = at + 4 * side
            of = i // 2 + count * side
            picked = jnp.where((row == where) & (column == of), 1.0, picked)
            mixing = jnp.where((slot == where) & (token == of), weight, mixing)
    picked = picked.astype(jnp.bfloat16)
    combine[...] = mixing
    both = jnp.concatenate([normed[:, :half], normed[:, half:]], axis=0)
    folded[...] = jnp.dot(picked, both, preferred_element_type=f32).astype(folded.dtype)


def unfold_kernel(folded, *outs):
    half = folded.shape[1]
    sides = []
    for side in range(2):
        take = onehot(UNIT, 2 * UNIT, lambda r, c: c == (r // 4) * 8 + r % 4 + 4 * side)
        rows = jnp.dot(take, folded[...], preferred_element_type=jnp.float32)
        sides.append(rows.astype(folded.dtype))
    for out, joined in zip(outs, JOINED):
        at = 0
        for c in joined:
            start, size, _ = CHAINS[c]
            low = start % half
            out[:, at : at + size] = sides[start // half][:, low : low + size]
            at += size


def fold_kernel(*refs):
    n = len(CHAINS)
    held, came, folded = refs[:n], refs[n : 2 * n], refs[2 * n]
    half = folded.shape[1]
    f32 = jnp.float32
    for c, (start, size, _) in enumerate(OUT_CHAINS):
        total = (held[c][...].astype(f32) + came[c][...].astype(f32)).astype(folded.dtype)
        side = start // half
        give = onehot(2 * UNIT, UNIT, lambda r, c: r == (c // 4) * 8 + c % 4 + 4 * side)
        rows = jnp.dot(give, total, preferred_element_type=f32).astype(folded.dtype)
        columns = slice(start - side * half, start - side * half + size)
        if side == 0:
            folded[:, columns] = rows
        else:
            folded[:, columns] = folded[:, columns] + rows


def mix_kernel(tokens, combine, back, out):
    half = back.shape[1]
    count = tokens.shape[0]
    f32 = jnp.float32
    moe = jnp.dot(
        combine[...],
        back[...].astype(f32),
        precision=lax.Precision.HIGHEST,
        preferred_element_type=f32,
    )
    for side in range(2):
        columns = slice(side * half, side * half + half)
        total = tokens[:, columns].astype(f32) + moe[side * count : side * count + count]
        out[:, columns] = total.astype(out.dtype)


def small(kernel, out_shape, *args, space=pltpu.VMEM, scratch=(), limit=16, name):
    vmem = pl.BlockSpec(memory_space=pltpu.VMEM)
    return pl.pallas_call(
        kernel,
        out_shape=out_shape,
        in_specs=[pl.BlockSpec(memory_space=space)] * len(args),
        out_specs=jax.tree.map(lambda _: vmem, out_shape),
        scratch_shapes=scratch,
        compiler_params=pltpu.CompilerParams(vmem_limit_bytes=limit << 20),
        name=name,
    )(*args)


def swap_experts(folded):
    blocks = folded.reshape(8, 8, folded.shape[1])
    blocks = lax.all_to_all(blocks, ("zl", "y"), split_axis=0, concat_axis=0, tiled=True)
    return blocks.reshape(folded.shape)


def per_device(tokens, norm_gain, routes, route_weights, w_gate, w_up, w_down):
    bf16 = jnp.bfloat16
    count, width = tokens.shape
    wg0, wu0, wd0 = w_gate[0], w_up[0], w_down[0]

    folded_shape = jax.ShapeDtypeStruct((64, width // 2), bf16)
    folded, combine = small(
        place_kernel,
        [folded_shape, jax.ShapeDtypeStruct((2 * count, 64), jnp.float32)],
        routes.T,
        route_weights.T,
        tokens,
        norm_gain.reshape(1, width),
        space=pltpu.HBM,
        scratch=[
            pltpu.SMEM((2, count), jnp.int32),
            pltpu.SMEM((2, count), jnp.float32),
            pltpu.VMEM((count, width), bf16),
            pltpu.VMEM((1, width), jnp.float32),
            pltpu.SemaphoreType.DMA((4,)),
        ],
        limit=60,
        name="place",
    )
    wg1, wu1, wd1 = (trade(after(w, folded), "c") for w in (wg0, wu0, wd0))
    folded = swap_experts(folded)
    folded, wg1, wu1 = lax.optimization_barrier((folded, wg1, wu1))
    heads = [
        jax.ShapeDtypeStruct((UNIT, sum(CHAINS[c][1] for c in joined)), bf16) for joined in JOINED
    ]
    held = list(small(unfold_kernel, heads, folded, name="unfold"))

    last = None
    for step in range(2):
        came = [trade(h, CHAINS[joined[0]][2][step]) for h, joined in zip(held, JOINED)]
        for k in (2, 0, 1):
            if last is not None:
                came[k] = after(came[k], *(last if isinstance(last, list) else (last,)))
            if (step, k) == (0, 1):
                came[k], wd1 = lax.optimization_barrier((came[k], wd1))
            if (step, k) == (1, 2):
                size = CHAINS[2][1]
                both = [
                    jnp.concatenate([held[k][:, at], came[k][:, at]], axis=0)
                    for at in (slice(0, size), slice(size, 2 * size))
                ]
                last = both
            else:
                held[k] = last = jnp.concatenate([held[k], came[k]], axis=0)
    held = held[:2] + both
    came = [trade(h, order[2]) for h, (_, _, order) in zip(held, CHAINS)]
    for j in (2, 3, 0, 1):
        came[j] = after(came[j], last)
        held[j] = last = jnp.concatenate([held[j], came[j]], axis=0)
    came = [trade(h, order[3]) for h, (_, _, order) in zip(held, CHAINS)]
    weights = (wg0, wu0, wg1, wu1)
    sums = hidden_units({(j, False): held[j] for j in range(4)}, weights, None, False)
    came[0] = after(came[0], last, sums)
    came[1] = after(came[1], came[0])
    sums = hidden_units({(j, True): came[j] for j in (0, 1)}, weights, sums, False)
    came[2] = after(came[2], sums)
    came[3] = after(came[3], came[2])
    hidden = hidden_units({(j, True): came[j] for j in (2, 3)}, weights, sums, True)

    held, away = [], []
    for j in range(4):
        given = after(hidden, away[-1]) if away else hidden
        away.append(expert_out(given, wd0, wd1, j, True))
    for j in range(4):
        given = after(hidden, away[-1], *held[-1:])
        held.append(expert_out(given, wd0, wd1, j, False))
    last = None
    for step in (3, 2):
        came = [trade(a, order[step]) for a, (_, _, order) in zip(away, CHAINS)]
        half = held[0].shape[0] // 2
        for j in range(4):
            got = came[j] if last is None else after(came[j], last)
            away[j] = last = add(held[j][half:], got[half:])
            held[j] = add(held[j][:half], got[:half])
    join = lambda values: values[:2] + [jnp.concatenate(values[2:], axis=1)]
    held, away = join(held), join(away)
    last = None
    came = [trade(a, CHAINS[joined[0]][2][1]) for a, joined in zip(away, JOINED)]
    half = held[0].shape[0] // 2
    for k in range(3):
        got = came[k] if last is None else after(came[k], last)
        away[k] = last = add(held[k][half:], got[half:])
        held[k] = add(held[k][:half], got[:half])
    size = OUT_CHAINS[2][1]
    part = lambda values: values[:2] + [values[2][:, :size], values[2][:, size:]]
    held, away = part(held), part(away)
    came = [trade(a, order[0]) for a, (_, _, order) in zip(away, CHAINS)]

    folded = small(fold_kernel, folded_shape, *held, *came, name="fold")
    back = swap_experts(folded)
    out = jax.ShapeDtypeStruct(tokens.shape, bf16)
    return small(mix_kernel, out, tokens, combine, back, name="mix")


def solution(mesh):
    fine = Mesh(mesh.devices.reshape(4, 2, 4, 4, 2), AXES)
    rows = P(AXES, None)
    return jax.shard_map(
        per_device,
        mesh=fine,
        in_specs=(
            rows,
            P(),
            rows,
            rows,
            P(("zl", "y"), None, ("dp", "x", "c")),
            P(("zl", "y"), None, ("dp", "x", "c")),
            P(("zl", "y"), ("dp", "x", "c"), None),
        ),
        out_specs=rows,
        check_vma=False,
    )
```

```python
import functools

import jax
import jax.numpy as jnp
from jax import lax
from jax.experimental import pallas as pl
from jax.experimental.pallas import tpu as pltpu
from jax.sharding import Mesh
from jax.sharding import PartitionSpec as P

AXES = ("dp", "zl", "y", "x", "c")
STEPS = 6


DIMS = {"xa": ("x", 1), "xb": ("x", 3), "za": ("dp", 1), "zb": ("dp", 3), "c": ("c", 1)}
CHAINS = (
    (0, 2048, ("za", "zb", "xb", "xa")),
    (3072, 2048, ("zb", "za", "xa", "xb")),
    (2048, 1024, ("xa", "xb", "zb", "za")),
    (5120, 1024, ("xa", "xb", "za", "zb")),
)
JOINED = ((0,), (1,), (2, 3))
CANON = ("xa", "xb", "za", "zb")
UNIT = 32
HALF = 8 * UNIT


def canon_block(order, index):
    return sum(((index >> k) & 1) << CANON.index(d) for k, d in enumerate(order))


def trade(value, dim):
    axis, mask = DIMS[dim]
    n = lax.axis_size(axis)
    return lax.ppermute(value, axis, [(i, i ^ mask) for i in range(n)])


def add(a, b):
    return (a.astype(jnp.float32) + b.astype(jnp.float32)).astype(a.dtype)


def after(value, *others):
    return lax.optimization_barrier((value, *others))[0]


def hidden_kernel(pieces, first, last, more, *refs):
    n = len(pieces)
    ins = refs[:n]
    wg0, wu0, wg1, wu1 = refs[n : n + 4]
    refs = refs[n + 4 :]
    before = None if first else refs[0]
    refs = refs if first else refs[1:]
    extra, refs = refs[:more], refs[more:]
    total = refs[0]
    acc = refs[1] if last else total
    step = pl.program_id(0)
    units = wg0.shape[1]
    f32 = jnp.float32

    @pl.when(step == 0)
    def _():
        acc[...] = jnp.zeros_like(acc) if first else before[...]
        for k, product in enumerate(extra):
            for index in range(8):
                to = canon_block(CHAINS[2 + k // 4][2], index + 8) * UNIT
                acc[k % 4, to : to + UNIT, :] += product[index * UNIT : (index + 1) * UNIT, :]

    at = 0
    for k, (c, came) in enumerate(pieces):
        _, width, order = CHAINS[c]
        steps = width // PART

        @pl.when((step >= at) & (step < at + steps))
        def _(k=k, order=order, came=came):
            for i, w in enumerate((wg0, wu0, wg1, wu1)):
                product = jnp.dot(ins[k][...], w[...], preferred_element_type=f32)
                for index in range(8):
                    to = canon_block(order, index + 8 * came) * UNIT
                    acc[i, to : to + UNIT, :] += product[index * UNIT : (index + 1) * UNIT]

        at += steps

    if last:

        @pl.when(step == at - 1)
        def _():
            for i in range(2):
                gate = acc[2 * i]
                value = gate / (1.0 + jnp.exp(-gate)) * acc[2 * i + 1]
                total[:, i * units : (i + 1) * units] = value.astype(total.dtype)


def out_kernel(order, sent, hidden, wd0, wd1, out):
    units = wd0.shape[0]
    f32 = jnp.float32
    blocks = [canon_block(order, index + 8 * sent) * UNIT for index in range(8)]
    rows = jnp.concatenate([hidden[row : row + UNIT, :] for row in blocks], axis=0)
    total = jnp.dot(rows[:, :units], wd0[...], preferred_element_type=f32) + jnp.dot(
        rows[:, units:], wd1[...], preferred_element_type=f32
    )
    out[...] = total.astype(out.dtype)


PART = 1024


def pick(table, i):
    value = table[0]
    for k, entry in enumerate(table[1:], 1):
        value = jnp.where(i >= k, entry, value)
    return value


def hidden_units(pieces, weights, before, last, extra=()):
    width, units = weights[0].shape
    count = 2 * HALF
    first = before is None
    in_specs, parts = [], []
    for c, _ in pieces:
        start, size, _ = CHAINS[c]
        low, steps = len(parts), size // PART
        to = lambda i, low=low, steps=steps: (0, jnp.clip(i - low, 0, steps - 1))
        in_specs.append(pl.BlockSpec((HALF, PART), to))
        parts += [start // PART + k for k in range(steps)]
    whole = lambda *shape: pl.BlockSpec(shape, lambda i: (0,) * len(shape))
    in_specs += [pl.BlockSpec((PART, units), lambda i: (pick(parts, i), 0))] * 4
    sums = (4, count, units)
    if not first:
        in_specs.append(whole(*sums))
    in_specs += [whole(HALF, units)] * len(extra)
    if last:
        out, out_spec = jax.ShapeDtypeStruct((count, 2 * units), jnp.bfloat16), whole(count, 2 * units)
        scratch = [pltpu.VMEM(sums, jnp.float32)]
    else:
        out, out_spec, scratch = jax.ShapeDtypeStruct(sums, jnp.float32), whole(*sums), []
    depth = len(parts) * PART
    return pl.pallas_call(
        functools.partial(hidden_kernel, tuple(pieces), first, last, len(extra)),
        grid=(len(parts),),
        out_shape=out,
        in_specs=in_specs,
        out_specs=out_spec,
        scratch_shapes=scratch,
        compiler_params=pltpu.CompilerParams(vmem_limit_bytes=32 << 20),
        cost_estimate=pl.CostEstimate(
            flops=8 * HALF * depth * units if last else 0,
            bytes_accessed=8 * depth * units + 2 * HALF * depth if last else 0,
            transcendentals=2 * count * units if last else 0,
        ),
        name="hidden",
    )(*pieces.values(), *weights, *(() if first else (before,)), *extra)


def expert_out(hidden, wd0, wd1, chain, sent):
    start, size, order = CHAINS[chain]
    units = wd0.shape[0]
    low, count = start // PART, 2 * HALF
    return pl.pallas_call(
        functools.partial(out_kernel, order, int(sent)),
        grid=(size // PART,),
        out_shape=jax.ShapeDtypeStruct((HALF, size), jnp.bfloat16),
        in_specs=[pl.BlockSpec((count, 2 * units), lambda i: (0, 0))]
        + [pl.BlockSpec((units, PART), lambda i: (0, low + i))] * 2,
        out_specs=pl.BlockSpec((HALF, PART), lambda i: (0, i)),
        compiler_params=pltpu.CompilerParams(vmem_limit_bytes=24 << 20),
        cost_estimate=pl.CostEstimate(
            flops=2 * count * size * units,
            bytes_accessed=4 * size * units + count * size,
            transcendentals=0,
        ),
        name="out",
    )(hidden, wd0, wd1)


def onehot(rows, columns, hit):
    row = lax.broadcasted_iota(jnp.int32, (rows, columns), 0)
    column = lax.broadcasted_iota(jnp.int32, (rows, columns), 1)
    return hit(row, column).astype(jnp.bfloat16)


def place_kernel(*refs):
    folded, combine = refs[4:6]
    routes, weights, tokens, gain = refs[6:10]
    copies = [pltpu.make_async_copy(refs[i], refs[6 + i], refs[10].at[i]) for i in range(4)]
    for copy in copies:
        copy.start()
    for copy in copies:
        copy.wait()
    f32 = jnp.float32
    count, width = tokens.shape
    half = width // 2
    wide = tokens[...].astype(f32)
    scale = lax.rsqrt(jnp.mean(wide * wide, axis=1, keepdims=True) + 1e-05)
    normed = (wide * scale * gain[...]).astype(jnp.bfloat16)
    rows = folded.shape[0]
    row = lax.broadcasted_iota(jnp.int32, (rows, 2 * count), 0)
    column = lax.broadcasted_iota(jnp.int32, (rows, 2 * count), 1)
    slot = lax.broadcasted_iota(jnp.int32, (2 * count, rows), 1)
    token = lax.broadcasted_iota(jnp.int32, (2 * count, rows), 0)
    picked = jnp.zeros((rows, 2 * count), f32)
    mixing = jnp.zeros((2 * count, rows), f32)
    flat = [routes[k, t] for t in range(count) for k in range(2)]
    for i, expert in enumerate(flat):
        rank = jnp.int32(0)
        for other in flat[:i]:
            rank += (other == expert).astype(jnp.int32)
        at = expert * 8 + rank
        weight = weights[i % 2, i // 2]
        for side in range(2):
            where = at + 4 * side
            of = i // 2 + count * side
            picked = jnp.where((row == where) & (column == of), 1.0, picked)
            mixing = jnp.where((slot == where) & (token == of), weight, mixing)
    picked = picked.astype(jnp.bfloat16)
    combine[...] = mixing
    both = jnp.concatenate([normed[:, :half], normed[:, half:]], axis=0)
    folded[...] = jnp.dot(picked, both, preferred_element_type=f32).astype(folded.dtype)


def unfold_kernel(folded, *outs):
    half = folded.shape[1]
    sides = []
    for side in range(2):
        take = onehot(UNIT, 2 * UNIT, lambda r, c: c == (r // 4) * 8 + r % 4 + 4 * side)
        rows = jnp.dot(take, folded[...], preferred_element_type=jnp.float32)
        sides.append(rows.astype(folded.dtype))
    for out, joined in zip(outs, JOINED):
        at = 0
        for c in joined:
            start, size, _ = CHAINS[c]
            low = start % half
            out[:, at : at + size] = sides[start // half][:, low : low + size]
            at += size


def fold_kernel(*refs):
    n = len(CHAINS)
    held, came, folded = refs[:n], refs[n : 2 * n], refs[2 * n]
    half = folded.shape[1]
    f32 = jnp.float32
    for c, (start, size, _) in enumerate(CHAINS):
        total = (held[c][...].astype(f32) + came[c][...].astype(f32)).astype(folded.dtype)
        side = start // half
        give = onehot(2 * UNIT, UNIT, lambda r, c: r == (c // 4) * 8 + c % 4 + 4 * side)
        rows = jnp.dot(give, total, preferred_element_type=f32).astype(folded.dtype)
        columns = slice(start - side * half, start - side * half + size)
        if side == 0:
            folded[:, columns] = rows
        else:
            folded[:, columns] = folded[:, columns] + rows


def mix_kernel(tokens, combine, back, out):
    half = back.shape[1]
    count = tokens.shape[0]
    f32 = jnp.float32
    moe = jnp.dot(
        combine[...],
        back[...].astype(f32),
        precision=lax.Precision.HIGHEST,
        preferred_element_type=f32,
    )
    for side in range(2):
        columns = slice(side * half, side * half + half)
        total = tokens[:, columns].astype(f32) + moe[side * count : side * count + count]
        out[:, columns] = total.astype(out.dtype)


def small(kernel, out_shape, *args, space=pltpu.VMEM, scratch=(), limit=16, name):
    vmem = pl.BlockSpec(memory_space=pltpu.VMEM)
    return pl.pallas_call(
        kernel,
        out_shape=out_shape,
        in_specs=[pl.BlockSpec(memory_space=space)] * len(args),
        out_specs=jax.tree.map(lambda _: vmem, out_shape),
        scratch_shapes=scratch,
        compiler_params=pltpu.CompilerParams(vmem_limit_bytes=limit << 20),
        name=name,
    )(*args)


def swap_experts(folded):
    blocks = folded.reshape(8, 8, folded.shape[1])
    blocks = lax.all_to_all(blocks, ("zl", "y"), split_axis=0, concat_axis=0, tiled=True)
    return blocks.reshape(folded.shape)


def per_device(tokens, norm_gain, routes, route_weights, w_gate, w_up, w_down):
    bf16 = jnp.bfloat16
    count, width = tokens.shape
    wg0, wu0, wd0 = w_gate[0], w_up[0], w_down[0]

    folded_shape = jax.ShapeDtypeStruct((64, width // 2), bf16)
    folded, combine = small(
        place_kernel,
        [folded_shape, jax.ShapeDtypeStruct((2 * count, 64), jnp.float32)],
        routes.T,
        route_weights.T,
        tokens,
        norm_gain.reshape(1, width),
        space=pltpu.HBM,
        scratch=[
            pltpu.SMEM((2, count), jnp.int32),
            pltpu.SMEM((2, count), jnp.float32),
            pltpu.VMEM((count, width), bf16),
            pltpu.VMEM((1, width), jnp.float32),
            pltpu.SemaphoreType.DMA((4,)),
        ],
        limit=60,
        name="place",
    )
    wg1, wu1, wd1 = (trade(after(w, folded), "c") for w in (wg0, wu0, wd0))
    folded = swap_experts(folded)
    folded, wg1, wu1 = lax.optimization_barrier((folded, wg1, wu1))
    heads = [
        jax.ShapeDtypeStruct((UNIT, sum(CHAINS[c][1] for c in joined)), bf16) for joined in JOINED
    ]
    held = list(small(unfold_kernel, heads, folded, name="unfold"))

    last = None
    for step in range(2):
        came = [trade(h, CHAINS[joined[0]][2][step]) for h, joined in zip(held, JOINED)]
        for k in (2, 0, 1):
            if last is not None:
                came[k] = after(came[k], *(last if isinstance(last, list) else (last,)))
            if (step, k) == (0, 1):
                came[k], wd1 = lax.optimization_barrier((came[k], wd1))
            if (step, k) == (1, 2):
                size = CHAINS[2][1]
                both = [
                    jnp.concatenate([held[k][:, at], came[k][:, at]], axis=0)
                    for at in (slice(0, size), slice(size, 2 * size))
                ]
                last = both
            else:
                held[k] = last = jnp.concatenate([held[k], came[k]], axis=0)
    held = held[:2] + both
    came = [trade(h, order[2]) for h, (_, _, order) in zip(held, CHAINS)]
    for j in (2, 3, 0, 1):
        came[j] = after(came[j], last)
        held[j] = last = jnp.concatenate([held[j], came[j]], axis=0)
    came = [trade(h, order[3]) for h, (_, _, order) in zip(held, CHAINS)]
    weights = (wg0, wu0, wg1, wu1)
    sums = hidden_units({(j, False): held[j] for j in range(4)}, weights, None, False)
    came[2] = after(came[2], last, sums)
    came[3] = after(came[3], came[2])
    extra = []
    for j in (2, 3):
        start, size, _ = CHAINS[j]
        for w in weights:
            product = jnp.dot(came[j], w[start : start + size], preferred_element_type=jnp.float32)
            extra.append(product)
    came[0] = after(came[0], *extra)
    came[1] = after(came[1], came[0])
    hidden = hidden_units({(j, True): came[j] for j in (0, 1)}, weights, sums, True, extra)

    held, away = [], []
    for j in range(4):
        given = after(hidden, away[-1]) if away else hidden
        away.append(expert_out(given, wd0, wd1, j, True))
    for j in range(4):
        given = after(hidden, away[-1], *held[-1:])
        held.append(expert_out(given, wd0, wd1, j, False))
    last = None
    for step in (3, 2):
        came = [trade(a, order[step]) for a, (_, _, order) in zip(away, CHAINS)]
        half = held[0].shape[0] // 2
        for j in range(4):
            got = came[j] if last is None else after(came[j], last)
            away[j] = last = add(held[j][half:], got[half:])
            held[j] = add(held[j][:half], got[:half])
    join = lambda values: values[:2] + [jnp.concatenate(values[2:], axis=1)]
    held, away = join(held), join(away)
    last = None
    came = [trade(a, CHAINS[joined[0]][2][1]) for a, joined in zip(away, JOINED)]
    half = held[0].shape[0] // 2
    for k in range(3):
        got = came[k] if last is None else after(came[k], last)
        away[k] = last = add(held[k][half:], got[half:])
        held[k] = add(held[k][:half], got[:half])
    size = CHAINS[2][1]
    part = lambda values: values[:2] + [values[2][:, :size], values[2][:, size:]]
    held, away = part(held), part(away)
    came = [trade(a, order[0]) for a, (_, _, order) in zip(away, CHAINS)]

    folded = small(fold_kernel, folded_shape, *held, *came, name="fold")
    back = swap_experts(folded)
    out = jax.ShapeDtypeStruct(tokens.shape, bf16)
    return small(mix_kernel, out, tokens, combine, back, name="mix")


def solution(mesh):
    fine = Mesh(mesh.devices.reshape(4, 2, 4, 4, 2), AXES)
    rows = P(AXES, None)
    return jax.shard_map(
        per_device,
        mesh=fine,
        in_specs=(
            rows,
            P(),
            rows,
            rows,
            P(("zl", "y"), None, ("dp", "x", "c")),
            P(("zl", "y"), None, ("dp", "x", "c")),
            P(("zl", "y"), ("dp", "x", "c"), None),
        ),
        out_specs=rows,
        check_vma=False,
    )
```

```python
import functools

import jax
import jax.numpy as jnp
from jax import lax
from jax.experimental import pallas as pl
from jax.experimental.pallas import tpu as pltpu
from jax.sharding import Mesh
from jax.sharding import PartitionSpec as P

AXES = ("dp", "zl", "y", "x", "c")
STEPS = 6


DIMS = {"xa": ("x", 1), "xb": ("x", 3), "za": ("dp", 1), "zb": ("dp", 3), "c": ("c", 1)}
CHAINS = (
    (0, 2048, ("za", "zb", "xb", "xa")),
    (3072, 2048, ("zb", "za", "xa", "xb")),
    (2048, 1024, ("xa", "xb", "zb", "za")),
    (5120, 1024, ("xa", "xb", "za", "zb")),
)
JOINED = ((0,), (1,), (2, 3))
CANON = ("xa", "xb", "za", "zb")
UNIT = 32
HALF = 8 * UNIT


def canon_block(order, index):
    return sum(((index >> k) & 1) << CANON.index(d) for k, d in enumerate(order))


def trade(value, dim):
    axis, mask = DIMS[dim]
    n = lax.axis_size(axis)
    return lax.ppermute(value, axis, [(i, i ^ mask) for i in range(n)])


def add(values):
    return sum(v.astype(jnp.float32) for v in values)


def after(value, *others):
    return lax.optimization_barrier((value, *others))[0]


def hidden_kernel(pieces, first, last, *refs):
    n = len(pieces)
    ins = refs[:n]
    wg0, wu0, wg1, wu1 = refs[n : n + 4]
    refs = refs[n + 4 :]
    before = None if first else refs[0]
    refs = refs if first else refs[1:]
    total = refs[0]
    acc = refs[1] if last else total
    step = pl.program_id(0)
    units = wg0.shape[1]
    f32 = jnp.float32

    @pl.when(step == 0)
    def _():
        acc[...] = jnp.zeros_like(acc) if first else before[...]

    at = 0
    for k, (c, came) in enumerate(pieces):
        _, width, order = CHAINS[c]
        steps = width // PART

        @pl.when((step >= at) & (step < at + steps))
        def _(k=k, order=order, came=came):
            for i, w in enumerate((wg0, wu0, wg1, wu1)):
                product = jnp.dot(ins[k][...], w[...], preferred_element_type=f32)
                for index in range(8):
                    to = canon_block(order, index + 8 * came) * UNIT
                    acc[i, to : to + UNIT, :] += product[index * UNIT : (index + 1) * UNIT]

        at += steps

    if last:

        @pl.when(step == at - 1)
        def _():
            for i in range(2):
                gate = acc[2 * i]
                value = gate / (1.0 + jnp.exp(-gate)) * acc[2 * i + 1]
                total[:, i * units : (i + 1) * units] = value.astype(total.dtype)


def out_kernel(order, sent, hidden, wd0, wd1, out):
    units = wd0.shape[0]
    f32 = jnp.float32
    blocks = [canon_block(order, index + 8 * sent) * UNIT for index in range(8)]
    rows = jnp.concatenate([hidden[row : row + UNIT, :] for row in blocks], axis=0)
    total = jnp.dot(rows[:, :units], wd0[...], preferred_element_type=f32) + jnp.dot(
        rows[:, units:], wd1[...], preferred_element_type=f32
    )
    out[...] = total.astype(out.dtype)


PART = 1024


def pick(table, i):
    value = table[0]
    for k, entry in enumerate(table[1:], 1):
        value = jnp.where(i >= k, entry, value)
    return value


def hidden_units(pieces, weights, before, last):
    width, units = weights[0].shape
    count = 2 * HALF
    first = before is None
    in_specs, parts = [], []
    for c, _ in pieces:
        start, size, _ = CHAINS[c]
        low, steps = len(parts), size // PART
        to = lambda i, low=low, steps=steps: (0, jnp.clip(i - low, 0, steps - 1))
        in_specs.append(pl.BlockSpec((HALF, PART), to))
        parts += [start // PART + k for k in range(steps)]
    whole = lambda *shape: pl.BlockSpec(shape, lambda i: (0,) * len(shape))
    in_specs += [pl.BlockSpec((PART, units), lambda i: (pick(parts, i), 0))] * 4
    sums = (4, count, units)
    if not first:
        in_specs.append(whole(*sums))
    if last:
        out, out_spec = jax.ShapeDtypeStruct((count, 2 * units), jnp.bfloat16), whole(count, 2 * units)
        scratch = [pltpu.VMEM(sums, jnp.float32)]
    else:
        out, out_spec, scratch = jax.ShapeDtypeStruct(sums, jnp.float32), whole(*sums), []
    depth = len(parts) * PART
    return pl.pallas_call(
        functools.partial(hidden_kernel, tuple(pieces), first, last),
        grid=(len(parts),),
        out_shape=out,
        in_specs=in_specs,
        out_specs=out_spec,
        scratch_shapes=scratch,
        compiler_params=pltpu.CompilerParams(vmem_limit_bytes=32 << 20),
        cost_estimate=pl.CostEstimate(
            flops=8 * HALF * depth * units if last else 0,
            bytes_accessed=8 * depth * units + 2 * HALF * depth if last else 0,
            transcendentals=2 * count * units if last else 0,
        ),
        name="hidden",
    )(*pieces.values(), *weights, *(() if first else (before,)))


def expert_out(hidden, wd0, wd1, chain, sent):
    start, size, order = CHAINS[chain]
    units = wd0.shape[0]
    low, count = start // PART, 2 * HALF
    return pl.pallas_call(
        functools.partial(out_kernel, order, int(sent)),
        grid=(size // PART,),
        out_shape=jax.ShapeDtypeStruct((HALF, size), jnp.bfloat16),
        in_specs=[pl.BlockSpec((count, 2 * units), lambda i: (0, 0))]
        + [pl.BlockSpec((units, PART), lambda i: (0, low + i))] * 2,
        out_specs=pl.BlockSpec((HALF, PART), lambda i: (0, i)),
        compiler_params=pltpu.CompilerParams(vmem_limit_bytes=24 << 20),
        cost_estimate=pl.CostEstimate(
            flops=2 * count * size * units,
            bytes_accessed=4 * size * units + count * size,
            transcendentals=0,
        ),
        name="out",
    )(hidden, wd0, wd1)


def onehot(rows, columns, hit):
    row = lax.broadcasted_iota(jnp.int32, (rows, columns), 0)
    column = lax.broadcasted_iota(jnp.int32, (rows, columns), 1)
    return hit(row, column).astype(jnp.bfloat16)


def place_kernel(*refs):
    folded, combine = refs[4:6]
    routes, weights, tokens, gain = refs[6:10]
    copies = [pltpu.make_async_copy(refs[i], refs[6 + i], refs[10].at[i]) for i in range(4)]
    for copy in copies:
        copy.start()
    for copy in copies:
        copy.wait()
    f32 = jnp.float32
    count, width = tokens.shape
    half = width // 2
    wide = tokens[...].astype(f32)
    scale = lax.rsqrt(jnp.mean(wide * wide, axis=1, keepdims=True) + 1e-05)
    normed = (wide * scale * gain[...]).astype(jnp.bfloat16)
    rows = folded.shape[0]
    row = lax.broadcasted_iota(jnp.int32, (rows, 2 * count), 0)
    column = lax.broadcasted_iota(jnp.int32, (rows, 2 * count), 1)
    slot = lax.broadcasted_iota(jnp.int32, (2 * count, rows), 1)
    token = lax.broadcasted_iota(jnp.int32, (2 * count, rows), 0)
    picked = jnp.zeros((rows, 2 * count), f32)
    mixing = jnp.zeros((2 * count, rows), f32)
    flat = [routes[k, t] for t in range(count) for k in range(2)]
    for i, expert in enumerate(flat):
        rank = jnp.int32(0)
        for other in flat[:i]:
            rank += (other == expert).astype(jnp.int32)
        at = expert * 8 + rank
        weight = weights[i % 2, i // 2]
        for side in range(2):
            where = at + 4 * side
            of = i // 2 + count * side
            picked = jnp.where((row == where) & (column == of), 1.0, picked)
            mixing = jnp.where((slot == where) & (token == of), weight, mixing)
    picked = picked.astype(jnp.bfloat16)
    combine[...] = mixing
    both = jnp.concatenate([normed[:, :half], normed[:, half:]], axis=0)
    folded[...] = jnp.dot(picked, both, preferred_element_type=f32).astype(folded.dtype)


def unfold_kernel(folded, *outs):
    half = folded.shape[1]
    sides = []
    for side in range(2):
        take = onehot(UNIT, 2 * UNIT, lambda r, c: c == (r // 4) * 8 + r % 4 + 4 * side)
        rows = jnp.dot(take, folded[...], preferred_element_type=jnp.float32)
        sides.append(rows.astype(folded.dtype))
    for out, joined in zip(outs, JOINED):
        at = 0
        for c in joined:
            start, size, _ = CHAINS[c]
            low = start % half
            out[:, at : at + size] = sides[start // half][:, low : low + size]
            at += size


def fold_kernel(*refs):
    n = len(CHAINS)
    held, came, folded = refs[:n], refs[n : 2 * n], refs[2 * n]
    half = folded.shape[1]
    f32 = jnp.float32
    for c, (start, size, _) in enumerate(CHAINS):
        total = (held[c][...].astype(f32) + came[c][...].astype(f32)).astype(folded.dtype)
        side = start // half
        give = onehot(2 * UNIT, UNIT, lambda r, c: r == (c // 4) * 8 + c % 4 + 4 * side)
        rows = jnp.dot(give, total, preferred_element_type=f32).astype(folded.dtype)
        columns = slice(start - side * half, start - side * half + size)
        if side == 0:
            folded[:, columns] = rows
        else:
            folded[:, columns] = folded[:, columns] + rows


def mix_kernel(tokens, combine, back, out):
    half = back.shape[1]
    count = tokens.shape[0]
    f32 = jnp.float32
    moe = jnp.dot(
        combine[...],
        back[...].astype(f32),
        precision=lax.Precision.HIGHEST,
        preferred_element_type=f32,
    )
    for side in range(2):
        columns = slice(side * half, side * half + half)
        total = tokens[:, columns].astype(f32) + moe[side * count : side * count + count]
        out[:, columns] = total.astype(out.dtype)


def small(kernel, out_shape, *args, space=pltpu.VMEM, scratch=(), limit=16, name):
    vmem = pl.BlockSpec(memory_space=pltpu.VMEM)
    return pl.pallas_call(
        kernel,
        out_shape=out_shape,
        in_specs=[pl.BlockSpec(memory_space=space)] * len(args),
        out_specs=jax.tree.map(lambda _: vmem, out_shape),
        scratch_shapes=scratch,
        compiler_params=pltpu.CompilerParams(vmem_limit_bytes=limit << 20),
        name=name,
    )(*args)


def swap_experts(folded):
    blocks = folded.reshape(8, 8, folded.shape[1])
    blocks = lax.all_to_all(blocks, ("zl", "y"), split_axis=0, concat_axis=0, tiled=True)
    return blocks.reshape(folded.shape)


def per_device(tokens, norm_gain, routes, route_weights, w_gate, w_up, w_down):
    bf16 = jnp.bfloat16
    count, width = tokens.shape
    wg0, wu0, wd0 = w_gate[0], w_up[0], w_down[0]

    folded_shape = jax.ShapeDtypeStruct((64, width // 2), bf16)
    folded, combine = small(
        place_kernel,
        [folded_shape, jax.ShapeDtypeStruct((2 * count, 64), jnp.float32)],
        routes.T,
        route_weights.T,
        tokens,
        norm_gain.reshape(1, width),
        space=pltpu.HBM,
        scratch=[
            pltpu.SMEM((2, count), jnp.int32),
            pltpu.SMEM((2, count), jnp.float32),
            pltpu.VMEM((count, width), bf16),
            pltpu.VMEM((1, width), jnp.float32),
            pltpu.SemaphoreType.DMA((4,)),
        ],
        limit=60,
        name="place",
    )
    wg1, wu1, wd1 = (trade(after(w, folded), "c") for w in (wg0, wu0, wd0))
    folded = swap_experts(folded)
    folded, wg1, wu1 = lax.optimization_barrier((folded, wg1, wu1))
    heads = [
        jax.ShapeDtypeStruct((UNIT, sum(CHAINS[c][1] for c in joined)), bf16) for joined in JOINED
    ]
    held = list(small(unfold_kernel, heads, folded, name="unfold"))

    last = None
    for step in range(2):
        came = [trade(h, CHAINS[joined[0]][2][step]) for h, joined in zip(held, JOINED)]
        for k in (2, 0, 1):
            if last is not None:
                came[k] = after(came[k], *(last if isinstance(last, list) else (last,)))
            if (step, k) == (0, 1):
                came[k], wd1 = lax.optimization_barrier((came[k], wd1))
            if (step, k) == (1, 2):
                size = CHAINS[2][1]
                both = [
                    jnp.concatenate([held[k][:, at], came[k][:, at]], axis=0)
                    for at in (slice(0, size), slice(size, 2 * size))
                ]
                last = both
            else:
                held[k] = last = jnp.concatenate([held[k], came[k]], axis=0)
    held = held[:2] + both
    came = [trade(h, order[2]) for h, (_, _, order) in zip(held, CHAINS)]
    for j in (2, 3, 0, 1):
        came[j] = after(came[j], last)
        held[j] = last = jnp.concatenate([held[j], came[j]], axis=0)
    came = [trade(h, order[3]) for h, (_, _, order) in zip(held, CHAINS)]
    weights = (wg0, wu0, wg1, wu1)
    sums = hidden_units({(j, False): held[j] for j in range(4)}, weights, None, False)
    came[0] = after(came[0], last, sums)
    came[1] = after(came[1], came[0])
    sums = hidden_units({(j, True): came[j] for j in (0, 1)}, weights, sums, False)
    came[2] = after(came[2], sums)
    came[3] = after(came[3], came[2])
    hidden = hidden_units({(j, True): came[j] for j in (2, 3)}, weights, sums, True)

    held, away = [], []
    for j in range(4):
        given = after(hidden, away[-1]) if away else hidden
        away.append(expert_out(given, wd0, wd1, j, True))
    for j in range(4):
        given = after(hidden, away[-1], *held[-1:])
        held.append(expert_out(given, wd0, wd1, j, False))
    parts = [[h] for h in held]
    last = None
    for step in (3, 2):
        came = [trade(a, order[step]) for a, (_, _, order) in zip(away, CHAINS)]
        half = away[0].shape[0] // 2
        for j in range(4):
            parts[j].append(came[j] if last is None else after(came[j], last))
            away[j] = last = add([p[half:] for p in parts[j]]).astype(bf16)
            parts[j] = [p[:half] for p in parts[j]]
    size = CHAINS[2][1]
    joined = away[:2] + [jnp.concatenate(away[2:], axis=1)]
    came = [trade(a, CHAINS[j][2][1]) for j, a in enumerate(joined)]
    half = away[0].shape[0] // 2
    last = None
    for k in range(3):
        got = came[k] if last is None else after(came[k], last)
        for j, piece in ((k, got),) if k < 2 else ((2, got[:, :size]), (3, got[:, size:])):
            parts[j].append(piece)
            away[j] = last = add([p[half:] for p in parts[j]]).astype(bf16)
            parts[j] = [p[:half] for p in parts[j]]
    came = [trade(a, order[0]) for a, (_, _, order) in zip(away, CHAINS)]
    held = [add(p) for p in parts]

    folded = small(fold_kernel, folded_shape, *held, *came, name="fold")
    back = swap_experts(folded)
    out = jax.ShapeDtypeStruct(tokens.shape, bf16)
    return small(mix_kernel, out, tokens, combine, back, name="mix")


def solution(mesh):
    fine = Mesh(mesh.devices.reshape(4, 2, 4, 4, 2), AXES)
    rows = P(AXES, None)
    return jax.shard_map(
        per_device,
        mesh=fine,
        in_specs=(
            rows,
            P(),
            rows,
            rows,
            P(("zl", "y"), None, ("dp", "x", "c")),
            P(("zl", "y"), None, ("dp", "x", "c")),
            P(("zl", "y"), ("dp", "x", "c"), None),
        ),
        out_specs=rows,
        check_vma=False,
    )
```

```python
import functools

import jax
import jax.numpy as jnp
from jax import lax
from jax.experimental import pallas as pl
from jax.experimental.pallas import tpu as pltpu
from jax.sharding import Mesh
from jax.sharding import PartitionSpec as P

AXES = ("dp", "zl", "y", "x", "c")
STEPS = 6


DIMS = {"xa": ("x", 1), "xb": ("x", 3), "za": ("dp", 1), "zb": ("dp", 3), "c": ("c", 1)}
CHAINS = (
    (0, 2048, ("za", "zb", "xb", "xa")),
    (3072, 2048, ("zb", "za", "xa", "xb")),
    (2048, 1024, ("xa", "xb", "zb", "za")),
    (5120, 1024, ("xa", "xb", "za", "zb")),
)
JOINED = ((0,), (1,), (2, 3))
CANON = ("xa", "xb", "za", "zb")
UNIT = 32
HALF = 8 * UNIT


def canon_block(order, index):
    return sum(((index >> k) & 1) << CANON.index(d) for k, d in enumerate(order))


def trade(value, dim):
    axis, mask = DIMS[dim]
    n = lax.axis_size(axis)
    return lax.ppermute(value, axis, [(i, i ^ mask) for i in range(n)])


def add(values):
    return sum(v.astype(jnp.float32) for v in values)


def after(value, *others):
    return lax.optimization_barrier((value, *others))[0]


def hidden_kernel(pieces, first, last, more, *refs):
    n = len(pieces)
    ins = refs[:n]
    wg0, wu0, wg1, wu1 = refs[n : n + 4]
    refs = refs[n + 4 :]
    before = None if first else refs[0]
    refs = refs if first else refs[1:]
    extra, refs = refs[:more], refs[more:]
    total = refs[0]
    acc = refs[1] if last else total
    step = pl.program_id(0)
    units = wg0.shape[1]
    f32 = jnp.float32

    @pl.when(step == 0)
    def _():
        acc[...] = jnp.zeros_like(acc) if first else before[...]
        for k, product in enumerate(extra):
            for index in range(8):
                to = canon_block(CHAINS[2 + k // 4][2], index + 8) * UNIT
                acc[k % 4, to : to + UNIT, :] += product[index * UNIT : (index + 1) * UNIT, :]

    at = 0
    for k, (c, came) in enumerate(pieces):
        _, width, order = CHAINS[c]
        steps = width // PART

        @pl.when((step >= at) & (step < at + steps))
        def _(k=k, order=order, came=came):
            for i, w in enumerate((wg0, wu0, wg1, wu1)):
                product = jnp.dot(ins[k][...], w[...], preferred_element_type=f32)
                for index in range(8):
                    to = canon_block(order, index + 8 * came) * UNIT
                    acc[i, to : to + UNIT, :] += product[index * UNIT : (index + 1) * UNIT]

        at += steps

    if last:

        @pl.when(step == at - 1)
        def _():
            for i in range(2):
                gate = acc[2 * i]
                value = gate / (1.0 + jnp.exp(-gate)) * acc[2 * i + 1]
                total[:, i * units : (i + 1) * units] = value.astype(total.dtype)


def out_kernel(order, sent, hidden, wd0, wd1, out):
    units = wd0.shape[0]
    f32 = jnp.float32
    blocks = [canon_block(order, index + 8 * sent) * UNIT for index in range(8)]
    rows = jnp.concatenate([hidden[row : row + UNIT, :] for row in blocks], axis=0)
    total = jnp.dot(rows[:, :units], wd0[...], preferred_element_type=f32) + jnp.dot(
        rows[:, units:], wd1[...], preferred_element_type=f32
    )
    out[...] = total.astype(out.dtype)


PART = 1024


def pick(table, i):
    value = table[0]
    for k, entry in enumerate(table[1:], 1):
        value = jnp.where(i >= k, entry, value)
    return value


def hidden_units(pieces, weights, before, last, extra=()):
    width, units = weights[0].shape
    count = 2 * HALF
    first = before is None
    in_specs, parts = [], []
    for c, _ in pieces:
        start, size, _ = CHAINS[c]
        low, steps = len(parts), size // PART
        to = lambda i, low=low, steps=steps: (0, jnp.clip(i - low, 0, steps - 1))
        in_specs.append(pl.BlockSpec((HALF, PART), to))
        parts += [start // PART + k for k in range(steps)]
    whole = lambda *shape: pl.BlockSpec(shape, lambda i: (0,) * len(shape))
    in_specs += [pl.BlockSpec((PART, units), lambda i: (pick(parts, i), 0))] * 4
    sums = (4, count, units)
    if not first:
        in_specs.append(whole(*sums))
    in_specs += [whole(HALF, units)] * len(extra)
    if last:
        out, out_spec = jax.ShapeDtypeStruct((count, 2 * units), jnp.bfloat16), whole(count, 2 * units)
        scratch = [pltpu.VMEM(sums, jnp.float32)]
    else:
        out, out_spec, scratch = jax.ShapeDtypeStruct(sums, jnp.float32), whole(*sums), []
    depth = len(parts) * PART
    return pl.pallas_call(
        functools.partial(hidden_kernel, tuple(pieces), first, last, len(extra)),
        grid=(len(parts),),
        out_shape=out,
        in_specs=in_specs,
        out_specs=out_spec,
        scratch_shapes=scratch,
        compiler_params=pltpu.CompilerParams(vmem_limit_bytes=32 << 20),
        cost_estimate=pl.CostEstimate(
            flops=8 * HALF * depth * units if last else 0,
            bytes_accessed=8 * depth * units + 2 * HALF * depth if last else 0,
            transcendentals=2 * count * units if last else 0,
        ),
        name="hidden",
    )(*pieces.values(), *weights, *(() if first else (before,)), *extra)


def expert_out(hidden, wd0, wd1, chain, sent):
    start, size, order = CHAINS[chain]
    units = wd0.shape[0]
    low, count = start // PART, 2 * HALF
    return pl.pallas_call(
        functools.partial(out_kernel, order, int(sent)),
        grid=(size // PART,),
        out_shape=jax.ShapeDtypeStruct((HALF, size), jnp.bfloat16),
        in_specs=[pl.BlockSpec((count, 2 * units), lambda i: (0, 0))]
        + [pl.BlockSpec((units, PART), lambda i: (0, low + i))] * 2,
        out_specs=pl.BlockSpec((HALF, PART), lambda i: (0, i)),
        compiler_params=pltpu.CompilerParams(vmem_limit_bytes=24 << 20),
        cost_estimate=pl.CostEstimate(
            flops=2 * count * size * units,
            bytes_accessed=4 * size * units + count * size,
            transcendentals=0,
        ),
        name="out",
    )(hidden, wd0, wd1)


def onehot(rows, columns, hit):
    row = lax.broadcasted_iota(jnp.int32, (rows, columns), 0)
    column = lax.broadcasted_iota(jnp.int32, (rows, columns), 1)
    return hit(row, column).astype(jnp.bfloat16)


def place_kernel(*refs):
    folded, combine = refs[4:6]
    routes, weights, tokens, gain = refs[6:10]
    copies = [pltpu.make_async_copy(refs[i], refs[6 + i], refs[10].at[i]) for i in range(4)]
    for copy in copies:
        copy.start()
    for copy in copies:
        copy.wait()
    f32 = jnp.float32
    count, width = tokens.shape
    half = width // 2
    wide = tokens[...].astype(f32)
    scale = lax.rsqrt(jnp.mean(wide * wide, axis=1, keepdims=True) + 1e-05)
    normed = (wide * scale * gain[...]).astype(jnp.bfloat16)
    rows = folded.shape[0]
    row = lax.broadcasted_iota(jnp.int32, (rows, 2 * count), 0)
    column = lax.broadcasted_iota(jnp.int32, (rows, 2 * count), 1)
    slot = lax.broadcasted_iota(jnp.int32, (2 * count, rows), 1)
    token = lax.broadcasted_iota(jnp.int32, (2 * count, rows), 0)
    picked = jnp.zeros((rows, 2 * count), f32)
    mixing = jnp.zeros((2 * count, rows), f32)
    flat = [routes[k, t] for t in range(count) for k in range(2)]
    for i, expert in enumerate(flat):
        rank = jnp.int32(0)
        for other in flat[:i]:
            rank += (other == expert).astype(jnp.int32)
        at = expert * 8 + rank
        weight = weights[i % 2, i // 2]
        for side in range(2):
            where = at + 4 * side
            of = i // 2 + count * side
            picked = jnp.where((row == where) & (column == of), 1.0, picked)
            mixing = jnp.where((slot == where) & (token == of), weight, mixing)
    picked = picked.astype(jnp.bfloat16)
    combine[...] = mixing
    both = jnp.concatenate([normed[:, :half], normed[:, half:]], axis=0)
    folded[...] = jnp.dot(picked, both, preferred_element_type=f32).astype(folded.dtype)


def unfold_kernel(folded, *outs):
    half = folded.shape[1]
    sides = []
    for side in range(2):
        take = onehot(UNIT, 2 * UNIT, lambda r, c: c == (r // 4) * 8 + r % 4 + 4 * side)
        rows = jnp.dot(take, folded[...], preferred_element_type=jnp.float32)
        sides.append(rows.astype(folded.dtype))
    for out, joined in zip(outs, JOINED):
        at = 0
        for c in joined:
            start, size, _ = CHAINS[c]
            low = start % half
            out[:, at : at + size] = sides[start // half][:, low : low + size]
            at += size


def fold_kernel(*refs):
    n = len(CHAINS)
    held, came, folded = refs[:n], refs[n : 2 * n], refs[2 * n]
    half = folded.shape[1]
    f32 = jnp.float32
    for c, (start, size, _) in enumerate(CHAINS):
        total = (held[c][...].astype(f32) + came[c][...].astype(f32)).astype(folded.dtype)
        side = start // half
        give = onehot(2 * UNIT, UNIT, lambda r, c: r == (c // 4) * 8 + c % 4 + 4 * side)
        rows = jnp.dot(give, total, preferred_element_type=f32).astype(folded.dtype)
        columns = slice(start - side * half, start - side * half + size)
        if side == 0:
            folded[:, columns] = rows
        else:
            folded[:, columns] = folded[:, columns] + rows


def mix_kernel(tokens, combine, back, out):
    half = back.shape[1]
    count = tokens.shape[0]
    f32 = jnp.float32
    moe = jnp.dot(
        combine[...],
        back[...].astype(f32),
        precision=lax.Precision.HIGHEST,
        preferred_element_type=f32,
    )
    for side in range(2):
        columns = slice(side * half, side * half + half)
        total = tokens[:, columns].astype(f32) + moe[side * count : side * count + count]
        out[:, columns] = total.astype(out.dtype)


def small(kernel, out_shape, *args, space=pltpu.VMEM, scratch=(), limit=16, name):
    vmem = pl.BlockSpec(memory_space=pltpu.VMEM)
    return pl.pallas_call(
        kernel,
        out_shape=out_shape,
        in_specs=[pl.BlockSpec(memory_space=space)] * len(args),
        out_specs=jax.tree.map(lambda _: vmem, out_shape),
        scratch_shapes=scratch,
        compiler_params=pltpu.CompilerParams(vmem_limit_bytes=limit << 20),
        name=name,
    )(*args)


def swap_experts(folded):
    blocks = folded.reshape(8, 8, folded.shape[1])
    blocks = lax.all_to_all(blocks, ("zl", "y"), split_axis=0, concat_axis=0, tiled=True)
    return blocks.reshape(folded.shape)


def per_device(tokens, norm_gain, routes, route_weights, w_gate, w_up, w_down):
    bf16 = jnp.bfloat16
    count, width = tokens.shape
    wg0, wu0, wd0 = w_gate[0], w_up[0], w_down[0]

    folded_shape = jax.ShapeDtypeStruct((64, width // 2), bf16)
    folded, combine = small(
        place_kernel,
        [folded_shape, jax.ShapeDtypeStruct((2 * count, 64), jnp.float32)],
        routes.T,
        route_weights.T,
        tokens,
        norm_gain.reshape(1, width),
        space=pltpu.HBM,
        scratch=[
            pltpu.SMEM((2, count), jnp.int32),
            pltpu.SMEM((2, count), jnp.float32),
            pltpu.VMEM((count, width), bf16),
            pltpu.VMEM((1, width), jnp.float32),
            pltpu.SemaphoreType.DMA((4,)),
        ],
        limit=60,
        name="place",
    )
    wg1, wu1, wd1 = (trade(after(w, folded), "c") for w in (wg0, wu0, wd0))
    folded = swap_experts(folded)
    folded, wg1, wu1 = lax.optimization_barrier((folded, wg1, wu1))
    heads = [
        jax.ShapeDtypeStruct((UNIT, sum(CHAINS[c][1] for c in joined)), bf16) for joined in JOINED
    ]
    held = list(small(unfold_kernel, heads, folded, name="unfold"))

    last = None
    for step in range(2):
        came = [trade(h, CHAINS[joined[0]][2][step]) for h, joined in zip(held, JOINED)]
        for k in (2, 0, 1):
            if last is not None:
                came[k] = after(came[k], *(last if isinstance(last, list) else (last,)))
            if (step, k) == (0, 1):
                came[k], wd1 = lax.optimization_barrier((came[k], wd1))
            if (step, k) == (1, 2):
                size = CHAINS[2][1]
                both = [
                    jnp.concatenate([held[k][:, at], came[k][:, at]], axis=0)
                    for at in (slice(0, size), slice(size, 2 * size))
                ]
                last = both
            else:
                held[k] = last = jnp.concatenate([held[k], came[k]], axis=0)
    held = held[:2] + both
    came = [trade(h, order[2]) for h, (_, _, order) in zip(held, CHAINS)]
    for j in (2, 3, 0, 1):
        came[j] = after(came[j], last)
        held[j] = last = jnp.concatenate([held[j], came[j]], axis=0)
    came = [trade(h, order[3]) for h, (_, _, order) in zip(held, CHAINS)]
    weights = (wg0, wu0, wg1, wu1)
    sums = hidden_units({(j, False): held[j] for j in range(4)}, weights, None, False)
    came[2] = after(came[2], last, sums)
    came[3] = after(came[3], came[2])
    extra = []
    for j in (2, 3):
        start, size, _ = CHAINS[j]
        for w in weights:
            product = jnp.dot(came[j], w[start : start + size], preferred_element_type=jnp.float32)
            extra.append(product)
    came[0] = after(came[0], *extra)
    came[1] = after(came[1], came[0])
    hidden = hidden_units({(j, True): came[j] for j in (0, 1)}, weights, sums, True, extra)

    held, away = [], []
    for j in range(4):
        given = after(hidden, away[-1]) if away else hidden
        away.append(expert_out(given, wd0, wd1, j, True))
    for j in range(4):
        given = after(hidden, away[-1], *held[-1:])
        held.append(expert_out(given, wd0, wd1, j, False))
    parts = [[h] for h in held]
    last = None
    for step in (3, 2):
        came = [trade(a, order[step]) for a, (_, _, order) in zip(away, CHAINS)]
        half = away[0].shape[0] // 2
        for j in range(4):
            parts[j].append(came[j] if last is None else after(came[j], last))
            away[j] = last = add([p[half:] for p in parts[j]]).astype(bf16)
            parts[j] = [p[:half] for p in parts[j]]
    size = CHAINS[2][1]
    joined = away[:2] + [jnp.concatenate(away[2:], axis=1)]
    came = [trade(a, CHAINS[j][2][1]) for j, a in enumerate(joined)]
    half = away[0].shape[0] // 2
    last = None
    for k in range(3):
        got = came[k] if last is None else after(came[k], last)
        for j, piece in ((k, got),) if k < 2 else ((2, got[:, :size]), (3, got[:, size:])):
            parts[j].append(piece)
            away[j] = last = add([p[half:] for p in parts[j]]).astype(bf16)
            parts[j] = [p[:half] for p in parts[j]]
    came = [trade(a, order[0]) for a, (_, _, order) in zip(away, CHAINS)]
    held = [add(p) for p in parts]

    folded = small(fold_kernel, folded_shape, *held, *came, name="fold")
    back = swap_experts(folded)
    out = jax.ShapeDtypeStruct(tokens.shape, bf16)
    return small(mix_kernel, out, tokens, combine, back, name="mix")


def solution(mesh):
    fine = Mesh(mesh.devices.reshape(4, 2, 4, 4, 2), AXES)
    rows = P(AXES, None)
    return jax.shard_map(
        per_device,
        mesh=fine,
        in_specs=(
            rows,
            P(),
            rows,
            rows,
            P(("zl", "y"), None, ("dp", "x", "c")),
            P(("zl", "y"), None, ("dp", "x", "c")),
            P(("zl", "y"), ("dp", "x", "c"), None),
        ),
        out_specs=rows,
        check_vma=False,
    )
```
